32 devices in a mesh: dp: 4 (over z), row: 4 (over y, core), col: 2 (over x).
Axes of the slice: x: 2, y: 2, z: 4, core: 2. Of those that a mesh axis runs over, the one named last changes fastest.
Arguments:
- layer_input: bfloat16 [8192, 2048], P(('dp', 'col'), 'row'), may hold values from -6 to 6
- lengths: int32 [16, 4], replicated, may hold values from 1 to 256, 512 in all within a row
- deal_table: int32 [4, 4], replicated, may hold values from 0 to 3, each once within a row
- ln1_gain: float32 [2048], P('row'), may hold values from 0.5 to 1.5
- ln1_bias: float32 [2048], P('row'), may hold values from -1.5 to 1.5
- qkv_weight: bfloat16 [2048, 6144], P('row', 'col'), may hold values from -1 to 1
- qkv_bias: float32 [6144], P('col'), may hold values from -1.5 to 1.5
- dense_weight: bfloat16 [2048, 2048], P('col', 'row'), may hold values from -1 to 1
- dense_bias: float32 [2048], P('row'), may hold values from -1.5 to 1.5
- ln2_gain: float32 [2048], P('row'), may hold values from 0.5 to 1.5
- ln2_bias: float32 [2048], P('row'), may hold values from -1.5 to 1.5
- fc1_weight: bfloat16 [2048, 8192], P('row', 'col'), may hold values from -1 to 1
- fc1_bias: float32 [8192], P('col'), may hold values from -1.5 to 1.5
- fc2_weight: bfloat16 [8192, 2048], P('col', 'row'), may hold values from -0.0625 to 0.0625
- fc2_bias: float32 [2048], P('row'), may hold values from -1.5 to 1.5
- cotangent: bfloat16 [8192, 2048], P(('dp', 'col'), 'row'), may hold values from -6 to 6
Outputs:
- output: bfloat16 [8192, 2048], P(('dp', 'col'), 'row')
- input_grad: float32 [8192, 2048], P(('dp', 'col'), 'row')
- ln1_gain_grad: float32 [2048], P('row')
- ln1_bias_grad: float32 [2048], P('row')
- qkv_weight_grad: float32 [2048, 6144], P('row', 'col')
- qkv_bias_grad: float32 [6144], P('col')
- dense_weight_grad: float32 [2048, 2048], P('col', 'row')
- dense_bias_grad: float32 [2048], P('row')
- ln2_gain_grad: float32 [2048], P('row')
- ln2_bias_grad: float32 [2048], P('row')
- fc1_weight_grad: float32 [2048, 8192], P('row', 'col')
- fc1_bias_grad: float32 [8192], P('col')
- fc2_weight_grad: float32 [8192, 2048], P('col', 'row')
- fc2_bias_grad: float32 [2048], P('row')
The draws below stay inside these ranges and needn't reach their ends.
Inputs may be any that keep to these rules, and one draw needn't show every extreme that they name: Row i holds, in token order, the lengths of the 4 sequences packed in given slab i; each row sums to 512. `deal_table`: each row is a permutation of the 4 groups.
All inputs are finite; a program needn't handle non-finite values.
Results may differ from the reference program's by a relative error of at most 0.0091.
Values may be sent and summed in bfloat16 or wider, within the bound.
A program may use at most 384 MiB of HBM per device.

```python
import math
from functools import partial
import jax
import jax.numpy as jnp
import numpy as np
from jax import lax

D = 2048
H = 16
HD = 128
ROT = 32
FF = 8192
SLAB = 512
SEQS = 4
SLABS = 16
TOKENS = 8192
N_DP = 4
N_ROW = 4


def rows_with_common(key, row_total, col_total):
    random_key, common_key = jax.random.split(key)
    random_part = jax.random.truncated_normal(random_key, -6.0, 6.0, (row_total, col_total), jnp.float32)
    common_row = jax.random.truncated_normal(common_key, -6.0, 6.0, (1, col_total), jnp.float32)
    scale = row_total ** (-0.5)
    return (random_part * scale + common_row * (0.5 * scale)).astype(jnp.bfloat16)


def draw_qkv_weight(key, part):
    key = jax.random.fold_in(key, 11)
    return rows_with_common(key, D, 3 * D)


def draw_fc1_weight(key, part):
    key = jax.random.fold_in(key, 23)
    return rows_with_common(key, D, FF)


def levels(stream_key, extent, shards, least, largest):
    def one(axis_at, parts):
        steps = jax.random.uniform(jax.random.fold_in(jax.random.fold_in(stream_key, 6), axis_at), (parts,), jnp.float32, least / len(shards), largest / len(shards))
        return jnp.repeat(jnp.exp(steps), extent[axis_at] // parts).reshape((-1,) + (1,) * (len(extent) - axis_at - 1))

    factor_of = one(*shards[0])
    for cut in shards[1:]:
        factor_of = factor_of * one(*cut)
    return factor_of


def split_up(count, total, reach, skew):
    weights = [(1 << 20) // math.isqrt(standing ** skew) + 1 for standing in range(2, count + 1)]
    spare, holding = total - reach - (count - 1), [1] * (count - 1)
    while spare > 0:
        free = [i for i in range(count - 1) if holding[i] < reach]
        pool, remaining = sum([weights[i] for i in free]), spare
        for i in free:
            extra = min(reach - holding[i], max(1, remaining * weights[i] // pool), spare)
            holding[i] = holding[i] + extra
            spare = spare - extra
    return np.array([reach] + holding)


def uneven_parts(key, amount, total, limit, slope):
    if amount == 2:
        one = jax.random.randint(key, (), max(1, total - limit), min(limit, total - 1) + 1)
        return jnp.stack([one, total - one])
    tallies = jnp.asarray(split_up(amount, total, limit, slope), jnp.int32)
    couples = (amount - 1) // 2
    source_of, taker = tallies[1:1 + 2 * couples:2], tallies[2:2 + 2 * couples:2]
    slack = jnp.minimum(source_of - 1, limit - taker)
    passed = jax.random.randint(jax.random.fold_in(key, 1), (couples,), 0, 1 << 20) % (slack + 1)
    tallies = tallies.at[1:1 + 2 * couples:2].set(source_of - passed).at[2:2 + 2 * couples:2].set(taker + passed)
    return tallies[jax.random.permutation(jax.random.fold_in(key, 2), amount)]


def bell_draw(rng, dims, width, bound, pieces=(), kind=jnp.bfloat16):
    array = width * jax.random.normal(rng, dims, jnp.float32)
    if pieces:
        array = array * levels(rng, dims, pieces, -0.22, 0.18)
    return jnp.clip(array, -bound, bound).astype(kind)


def setup_inputs(seed: int = 0) -> dict:
    seeds = jax.random.split(jax.random.key(seed), 17)
    layer_input = bell_draw(seeds[0], (TOKENS, D), 1.0, 6.0, ((0, 8), (1, 4)))
    lengths = jax.vmap(lambda own: uneven_parts(own, SEQS, SLAB, SLAB // 2, 1))(jax.random.split(seeds[1], SLABS)).reshape((SLABS, SEQS)).astype(jnp.int32)
    deal_table = jax.vmap(lambda own: jax.random.permutation(own, N_DP))(jax.random.split(seeds[2], N_ROW)).reshape((N_ROW, N_DP)).astype(jnp.int32)
    ln1_gain = jnp.clip(1.0 + 0.1 * jax.random.normal(seeds[3], (D,), jnp.float32), 0.5, 1.5)
    ln1_bias = bell_draw(seeds[4], (D,), 0.3, 1.5, ((0, 4),), jnp.float32)
    qkv_weight = draw_qkv_weight(jax.random.fold_in(seeds[16], 71), 0)
    qkv_bias = bell_draw(seeds[6], (3 * D,), 0.3, 1.5, ((0, 2),), jnp.float32)
    dense_weight = bell_draw(seeds[7], (D, D), (D // 64) ** -0.5, 1.0, ((0, 2), (1, 4)))
    dense_bias = bell_draw(seeds[8], (D,), 0.3, 1.5, ((0, 4),), jnp.float32)
    ln2_gain = jnp.clip(1.0 + 0.1 * jax.random.normal(seeds[9], (D,), jnp.float32), 0.5, 1.5)
    ln2_bias = bell_draw(seeds[10], (D,), 0.3, 1.5, ((0, 4),), jnp.float32)
    fc1_weight = draw_fc1_weight(jax.random.fold_in(seeds[16], 71), 0)
    fc1_bias = bell_draw(seeds[12], (FF,), 0.3, 1.5, ((0, 2),), jnp.float32)
    fc2_weight = bell_draw(seeds[13], (FF, D), FF ** -0.5, 0.0625, ((0, 2), (1, 4)))
    fc2_bias = bell_draw(seeds[14], (D,), 0.3, 1.5, ((0, 4),), jnp.float32)
    cotangent = bell_draw(seeds[15], (TOKENS, D), 1.0, 6.0, ((0, 8), (1, 4)))
    return {"layer_input": layer_input, "lengths": lengths, "deal_table": deal_table, "ln1_gain": ln1_gain, "ln1_bias": ln1_bias, "qkv_weight": qkv_weight, "qkv_bias": qkv_bias, "dense_weight": dense_weight, "dense_bias": dense_bias, "ln2_gain": ln2_gain, "ln2_bias": ln2_bias, "fc1_weight": fc1_weight, "fc1_bias": fc1_bias, "fc2_weight": fc2_weight, "fc2_bias": fc2_bias, "cotangent": cotangent}


@jax.custom_vjp
def low(v):
    return lax.optimization_barrier(v.astype(jnp.bfloat16)).astype(jnp.float32)

@jax.custom_vjp
def low_back(v):
    return v

def low_keep(v):
    return (low(v), None)

def low_pass(kept, grad):
    return (grad,)

def back_keep(v):
    return (v, None)

def back_low(kept, grad):
    return (low(grad),)
low.defvjp(low_keep, low_pass)
low_back.defvjp(back_keep, back_low)
norm_epsilon = 1e-05
masked_score = -1000000000.0
highest = lax.Precision.HIGHEST

def product(left_side, right_side):
    return jnp.dot(left_side, right_side, precision=highest, preferred_element_type=jnp.float32)

def rotary_tables(positions):
    frequency = 1.0 / 10000.0 ** (jnp.arange(0, ROT, 2, dtype=jnp.float32) / ROT)
    angles = positions.astype(jnp.float32)[:, None] * frequency[None, :]
    angles = jnp.concatenate([angles, angles], axis=1)
    return (jnp.cos(angles), jnp.sin(angles))

def rotate(values, cos_table, sin_table):
    half_rot = ROT // 2
    rotated = values[..., :ROT]
    turned = jnp.concatenate([-rotated[..., half_rot:], rotated[..., :half_rot]], axis=-1)
    rotated = rotated * cos_table[:, None, :] + turned * sin_table[:, None, :]
    return jnp.concatenate([rotated, values[..., ROT:]], axis=-1)

def segment_layout(seq_lengths, length):
    seq_ends = jnp.cumsum(seq_lengths).astype(jnp.int32)
    token_place = jnp.arange(length, dtype=jnp.int32)
    sequence_ids = lax.optimization_barrier(jnp.sum((token_place[:, None] >= seq_ends[None, :]).astype(jnp.int32), axis=1))
    starts = seq_ends - seq_lengths
    seq_hits = sequence_ids[:, None] == jnp.arange(seq_lengths.shape[0], dtype=jnp.int32)[None, :]
    seq_begin = lax.optimization_barrier(jnp.sum(jnp.where(seq_hits, starts[None, :], 0), axis=1))
    return (sequence_ids, token_place - seq_begin)

def slab_forward(params, slab_in, seq_lengths):
    ln1_gain, ln1_bias, qkv_weight, qkv_bias, dense_weight, dense_bias, ln2_gain, ln2_bias, fc1_weight, fc1_bias, fc2_weight, fc2_bias = params
    sequence_ids, positions = segment_layout(seq_lengths, SLAB)
    row_mean = lax.optimization_barrier(jnp.mean(slab_in, axis=-1, keepdims=True))
    variance = lax.optimization_barrier(jnp.mean(slab_in * slab_in, axis=-1, keepdims=True)) - row_mean * row_mean
    normed = (slab_in - row_mean) * lax.rsqrt(variance + norm_epsilon)
    ln1_out = low(normed * ln1_gain + ln1_bias)
    ln2_out = low(normed * ln2_gain + ln2_bias)
    qkv_out = low_back(product(ln1_out, qkv_weight) + qkv_bias).reshape(SLAB, H, 3, HD)
    cos_table, sin_table = rotary_tables(positions)
    queries = low(rotate(qkv_out[:, :, 0], cos_table, sin_table))
    keys_rot = low(rotate(qkv_out[:, :, 1], cos_table, sin_table))
    values = low(qkv_out[:, :, 2])
    scores = low_back(jnp.einsum('qhd,khd->hqk', queries, keys_rot, precision=highest) * (1.0 / math.sqrt(HD)))
    token_place = jnp.arange(SLAB, dtype=jnp.int32)
    allowed = (sequence_ids[:, None] == sequence_ids[None, :]) & (token_place[None, :] <= token_place[:, None])
    scores = jnp.where(allowed[None], scores, masked_score)
    row_top = lax.optimization_barrier(jnp.max(scores, axis=-1, keepdims=True))
    expanded = jnp.exp(scores - row_top)
    probs_full = low(expanded / lax.optimization_barrier(jnp.sum(expanded, axis=-1, keepdims=True)))
    mixture = jnp.einsum('hqk,khd->qhd', probs_full, values, precision=highest).reshape(SLAB, D)
    attn_out = low(low_back(mixture))
    hidden = low_back(product(ln2_out, fc1_weight) + fc1_bias)
    activated = low(jax.nn.gelu(hidden, approximate=False))
    return slab_in + product(attn_out, dense_weight) + dense_bias + product(activated, fc2_weight) + fc2_bias

def reference(layer_input, lengths, deal_table, ln1_gain, ln1_bias, qkv_weight, qkv_bias, dense_weight, dense_bias, ln2_gain, ln2_bias, fc1_weight, fc1_bias, fc2_weight, fc2_bias, cotangent):
    slab_index = jnp.arange(N_ROW, dtype=jnp.int32)[None, :]
    dealt_ids = (deal_table.T.astype(jnp.int32) * N_ROW + slab_index).reshape(-1)
    inverse = jnp.argsort(deal_table, axis=1).astype(jnp.int32)
    back_ids = (inverse.T * N_ROW + slab_index).reshape(-1)
    slab_data = layer_input.astype(jnp.float32).reshape(SLABS, SLAB, D)[dealt_ids]
    slab_lengths = lengths[dealt_ids]
    params = (ln1_gain, ln1_bias, qkv_weight.astype(jnp.float32), qkv_bias, dense_weight.astype(jnp.float32), dense_bias, ln2_gain, ln2_bias, fc1_weight.astype(jnp.float32), fc1_bias, fc2_weight.astype(jnp.float32), fc2_bias)

    def forward(slabs_in, weights):
        slab_step = jax.checkpoint(partial(slab_forward, weights))
        return lax.map(lambda pair_in: slab_step(pair_in[0], pair_in[1]), (slabs_in, slab_lengths))
    result, pullback = jax.vjp(forward, slab_data, params)
    grad_slabs, weight_grads = pullback(cotangent.astype(jnp.float32).reshape(SLABS, SLAB, D))
    input_grad = grad_slabs[back_ids].reshape(TOKENS, D)
    return (result.reshape(TOKENS, D).astype(jnp.bfloat16), input_grad, weight_grads[0], weight_grads[1], weight_grads[2], weight_grads[3], weight_grads[4], weight_grads[5], weight_grads[6], weight_grads[7], weight_grads[8], weight_grads[9], weight_grads[10], weight_grads[11])
```

```python
from functools import partial
import math

import jax
import jax.numpy as jnp
from jax import lax
from jax.experimental import pallas as pl
from jax.experimental.pallas import tpu as pltpu
from jax.sharding import PartitionSpec as P

D = 2048
HD = 128
ROT = 32
QBLK = 512
CHUNK = 256
BF16 = jnp.bfloat16
F32 = jnp.float32


norm_epsilon = 1e-05
masked_score = -1000000000.0


def rotary_tables(positions):
    frequency = 1.0 / 10000.0 ** (jnp.arange(0, ROT, 2, dtype=jnp.float32) / ROT)
    angles = positions.astype(jnp.float32)[:, None] * frequency[None, :]
    angles = jnp.concatenate([angles, angles], axis=1)
    return (jnp.cos(angles), jnp.sin(angles))


def rotate(values, cos_table, sin_table):
    half_rot = ROT // 2
    rotated = values[..., :ROT]
    turned = jnp.concatenate([-rotated[..., half_rot:], rotated[..., :half_rot]], axis=-1)
    rotated = rotated * cos_table[:, None, :] + turned * sin_table[:, None, :]
    return jnp.concatenate([rotated, values[..., ROT:]], axis=-1)


def segment_layout(seq_lengths, length):
    seq_ends = jnp.cumsum(seq_lengths)
    token_place = jnp.arange(length, dtype=jnp.int32)
    sequence_ids = jnp.sum((token_place[:, None] >= seq_ends[None, :]).astype(jnp.int32), axis=1)
    starts = seq_ends - seq_lengths
    seq_hits = sequence_ids[:, None] == jnp.arange(seq_lengths.shape[0], dtype=jnp.int32)[None, :]
    seq_begin = jnp.sum(jnp.where(seq_hits, starts[None, :], 0), axis=1)
    return (sequence_ids, token_place - seq_begin)


def contract_rows(left_side, right_side):
    return lax.dot_general(
        left_side, right_side, (((0,), (0,)), ((), ())), preferred_element_type=jnp.float32
    )


def contract_cols(left_side, right_side):
    return lax.dot_general(
        left_side, right_side, (((1,), (1,)), ((), ())), preferred_element_type=jnp.float32
    )


def pick_rows(pooled, chosen):
    row_hits = chosen[None, :] == jnp.arange(pooled.shape[0], dtype=jnp.int32)[:, None]
    return jnp.sum(jnp.where(row_hits[:, :, None], pooled.astype(jnp.float32), 0.0), axis=0)


def local(
    layer_input,
    lengths,
    deal_table,
    ln1_gain,
    ln1_bias,
    qkv_weight,
    qkv_bias,
    dense_weight,
    dense_bias,
    ln2_gain,
    ln2_bias,
    fc1_weight,
    fc1_bias,
    fc2_weight,
    fc2_bias,
    cotangent,
):
    dp_count = lax.axis_size("dp")
    row_count = lax.axis_size("row")
    col_count = lax.axis_size("col")
    group_id = lax.axis_index("dp")
    row_id = lax.axis_index("row")
    col_id = lax.axis_index("col")
    own_rows, own_feats = layer_input.shape
    group_rows = own_rows * col_count
    slab_rows = group_rows // row_count
    qkv_cols = qkv_weight.shape[1]
    attn_cols = dense_weight.shape[0]
    heads_here = qkv_cols // (3 * HD)
    score_scale = 1.0 / math.sqrt(HD)
    local_slab = (col_id * own_rows + jnp.arange(own_rows, dtype=jnp.int32)) // slab_rows
    slab_hits = local_slab[:, None] == jnp.arange(row_count, dtype=jnp.int32)[None, :]
    deal_here = lax.dynamic_index_in_dim(deal_table, group_id, 1, keepdims=False)
    source = jnp.sum(jnp.where(slab_hits, deal_here[None, :], 0), axis=1)
    pooled = lax.all_gather(layer_input, "dp", axis=0, tiled=True).reshape(
        dp_count, own_rows, own_feats
    )
    mine_rows = pick_rows(pooled, source).astype(jnp.bfloat16)
    input_all = lax.all_gather(mine_rows, "col", axis=0, tiled=True)
    input_wide = input_all.astype(jnp.float32)
    row_stats = lax.psum(
        (jnp.sum(input_wide, axis=1), jnp.sum(input_wide * input_wide, axis=1)), "row"
    )
    row_mean = row_stats[0] / D
    inv_std = lax.rsqrt(row_stats[1] / D - row_mean * row_mean + norm_epsilon)
    normed = (input_wide - row_mean[:, None]) * inv_std[:, None]
    own_start = col_id * own_rows
    normed_own = lax.dynamic_slice_in_dim(normed, own_start, own_rows, 0)
    inv_std_own = lax.dynamic_slice_in_dim(inv_std, own_start, own_rows, 0)
    ln1_all = (normed * ln1_gain + ln1_bias).astype(jnp.bfloat16)
    ln2_all = (normed * ln2_gain + ln2_bias).astype(jnp.bfloat16)
    part_one = ln1_all
    part_two = ln2_all
    first_sums = lax.psum_scatter(
        jnp.concatenate(
            [
                jnp.dot(part_one, qkv_weight, preferred_element_type=jnp.float32),
                jnp.dot(part_two, fc1_weight, preferred_element_type=jnp.float32),
            ],
            axis=1,
        ),
        "row",
        scatter_dimension=0,
        tiled=True,
    )
    qkv_out = first_sums[:, :qkv_cols] + qkv_bias
    hidden = first_sums[:, qkv_cols:] + fc1_bias
    slab_source = (
        lax.dynamic_index_in_dim(deal_here, row_id, 0, keepdims=False) * row_count + row_id
    )
    seq_lengths = lax.dynamic_index_in_dim(lengths, slab_source, 0, keepdims=False)
    sequence_ids, positions = segment_layout(seq_lengths, slab_rows)
    token_place = jnp.arange(slab_rows, dtype=jnp.int32)
    cos_table, sin_table = rotary_tables(positions)
    packed = qkv_out.reshape(slab_rows, heads_here, 3, HD)
    query_pre = packed[:, :, 0]
    key_pre = packed[:, :, 1]
    queries = rotate(query_pre, cos_table, sin_table).astype(jnp.bfloat16)
    keys_rot = rotate(key_pre, cos_table, sin_table).astype(jnp.bfloat16)
    values = packed[:, :, 2].astype(jnp.bfloat16)

    def block_scores(block_id):
        first_row = block_id * QBLK
        last_row = first_row + QBLK
        allowed = (sequence_ids[first_row:last_row, None] == sequence_ids[None, :last_row]) & (
            token_place[None, :last_row] <= token_place[first_row:last_row, None]
        )
        scores = (
            jnp.einsum("qhd,khd->hqk", queries, keys_rot, preferred_element_type=jnp.float32)
            * score_scale
        )
        return jnp.where(allowed[None], scores, masked_score)

    block_id = 0
    last_row = (block_id + 1) * QBLK
    scores = block_scores(block_id)
    row_top = jnp.max(scores, axis=-1, keepdims=True)
    exp_total = jnp.sum(jnp.exp(scores - row_top), axis=-1, keepdims=True)
    log_total = row_top + jnp.log(exp_total)
    probs_low = jnp.exp(scores - log_total).astype(jnp.bfloat16)
    mixtures = jnp.einsum("hqk,khd->qhd", probs_low, values, preferred_element_type=jnp.float32)
    log_totals = [log_total]
    attn_out = mixtures.reshape(slab_rows, attn_cols).astype(jnp.bfloat16)
    activated = jax.nn.gelu(hidden, approximate=False).astype(jnp.bfloat16)
    attn_all, act_all = (
        lax.all_gather(attn_out, "row", axis=0, tiled=True),
        lax.all_gather(activated, "row", axis=0, tiled=True),
    )
    part_one = attn_all
    part_two = act_all
    branch_sum = lax.psum_scatter(
        jnp.dot(part_one, dense_weight, preferred_element_type=jnp.float32)
        + jnp.dot(part_two, fc2_weight, preferred_element_type=jnp.float32),
        "col",
        scatter_dimension=0,
        tiled=True,
    )
    output = (mine_rows.astype(jnp.float32) + branch_sum + dense_bias + fc2_bias).astype(
        jnp.bfloat16
    )
    grad_all = lax.all_gather(cotangent, "col", axis=0, tiled=True)
    dense_grad = contract_rows(attn_all, grad_all)
    fc2_grad = contract_rows(act_all, grad_all)
    out_bias_grad = jnp.sum(grad_all, axis=0, dtype=jnp.float32)
    grad_block = grad_all
    grad_second = lax.psum_scatter(
        jnp.concatenate(
            [contract_cols(grad_block, dense_weight), contract_cols(grad_block, fc2_weight)], axis=1
        ),
        "row",
        scatter_dimension=0,
        tiled=True,
    )
    grad_mix = grad_second[:, :attn_cols].astype(jnp.bfloat16).reshape(slab_rows, heads_here, HD)
    gelu_back = jax.vjp(partial(jax.nn.gelu, approximate=False), hidden)[1]
    grad_hidden = gelu_back(grad_second[:, attn_cols:])[0]
    grad_key = jnp.zeros((slab_rows, heads_here, HD), jnp.float32)
    grad_value = jnp.zeros((slab_rows, heads_here, HD), jnp.float32)
    block_id = 0
    first_row = block_id * QBLK
    last_row = first_row + QBLK
    probs_full = jnp.exp(block_scores(block_id) - log_totals[block_id])
    probs_low = probs_full.astype(jnp.bfloat16)
    grad_block = grad_mix
    grad_value = grad_value.at[:last_row].add(
        jnp.einsum("hqk,qhd->khd", probs_low, grad_block, preferred_element_type=jnp.float32)
    )
    grad_probs = jnp.einsum("qhd,khd->hqk", grad_block, values, preferred_element_type=jnp.float32)
    centre = jnp.sum(probs_full * grad_probs, axis=-1, keepdims=True)
    grad_scores = (probs_full * (grad_probs - centre)).astype(jnp.bfloat16)
    grad_queries = (
        jnp.einsum("hqk,khd->qhd", grad_scores, keys_rot, preferred_element_type=jnp.float32)
        * score_scale
    )
    grad_key = grad_key.at[:last_row].add(
        jnp.einsum("hqk,qhd->khd", grad_scores, queries, preferred_element_type=jnp.float32)
        * score_scale
    )
    turn_back = jax.vjp(lambda values_in: rotate(values_in, cos_table, sin_table), query_pre)[1]
    grad_query_pre = turn_back(grad_queries)[0]
    grad_key_pre = turn_back(grad_key)[0]
    grad_qkv = jnp.stack([grad_query_pre, grad_key_pre, grad_value], axis=2).reshape(
        slab_rows, qkv_cols
    )
    grad_first = jnp.concatenate([grad_qkv, grad_hidden], axis=1).astype(jnp.bfloat16)
    grad_first_all = lax.all_gather(grad_first, "row", axis=0, tiled=True)
    grad_qkv_all = grad_first_all[:, :qkv_cols]
    grad_hidden_all = grad_first_all[:, qkv_cols:]
    qkv_weight_grad = contract_rows(ln1_all, grad_qkv_all)
    qkv_bias_grad = jnp.sum(grad_qkv_all, axis=0, dtype=jnp.float32)
    fc1_weight_grad = contract_rows(ln2_all, grad_hidden_all)
    fc1_bias_grad = jnp.sum(grad_hidden_all, axis=0, dtype=jnp.float32)
    grad_block = grad_first_all
    summed = lax.psum_scatter(
        jnp.concatenate(
            [
                contract_cols(grad_block[:, :qkv_cols], qkv_weight),
                contract_cols(grad_block[:, qkv_cols:], fc1_weight),
            ],
            axis=1,
        ),
        "col",
        scatter_dimension=0,
        tiled=True,
    )
    grad_ln_one = summed[:, :own_feats]
    grad_ln_two = summed[:, own_feats:]
    gain_terms = (
        jnp.sum(grad_ln_one * normed_own, axis=0),
        jnp.sum(grad_ln_one, axis=0),
        jnp.sum(grad_ln_two * normed_own, axis=0),
        jnp.sum(grad_ln_two, axis=0),
    )
    grad_normed = grad_ln_one * ln1_gain + grad_ln_two * ln2_gain
    row_sums = lax.psum(
        (jnp.sum(grad_normed, axis=1), jnp.sum(grad_normed * normed_own, axis=1)), "row"
    )
    grad_dealt = cotangent.astype(jnp.float32) + inv_std_own[:, None] * (
        grad_normed - row_sums[0][:, None] / D - normed_own * row_sums[1][:, None] / D
    )
    gain_sums = lax.psum(
        (gain_terms[0], gain_terms[1], gain_terms[2], gain_terms[3]), ("dp", "col")
    )
    weights_summed = lax.psum(
        (
            qkv_weight_grad,
            qkv_bias_grad,
            dense_grad,
            fc1_weight_grad,
            fc1_bias_grad,
            fc2_grad,
            out_bias_grad,
        ),
        "dp",
    )
    pool_back = lax.all_gather(grad_dealt, "dp", axis=0, tiled=True).reshape(
        dp_count, own_rows, own_feats
    )
    back_here = jnp.sum(
        jnp.where(deal_table == group_id, jnp.arange(dp_count, dtype=jnp.int32)[None, :], 0), axis=1
    )
    target = jnp.sum(jnp.where(slab_hits, back_here[None, :], 0), axis=1)
    input_grad = pick_rows(pool_back, target)
    return (
        output,
        input_grad,
        gain_sums[0],
        gain_sums[1],
        weights_summed[0],
        weights_summed[1],
        weights_summed[2],
        weights_summed[6],
        gain_sums[2],
        gain_sums[3],
        weights_summed[3],
        weights_summed[4],
        weights_summed[5],
        weights_summed[6],
    )


def row_swap(block, offset):
    return lax.ppermute(block, "row", [(i, i ^ offset) for i in range(4)])


def col_swap(block):
    return lax.ppermute(block, "col", [(0, 1), (1, 0)])


def line_route(item, sources):
    plane = lax.axis_index("dp")
    from_below = lax.ppermute(item, "dp", [(0, 1), (1, 2)])
    from_above = lax.ppermute(item, "dp", [(3, 2), (2, 1)])
    far = lax.ppermute(jnp.where(plane == 1, from_below, from_above), "dp", [(1, 2), (2, 1)])
    beside = jnp.where(plane == 1, from_above, from_below)
    edge_wants = jnp.where(plane == 1, sources[:, 0], sources[:, 3])[:, None, None]
    outward = jnp.where(edge_wants == plane, item, jnp.where(edge_wants == 3 - plane, beside, far))
    at_edge = lax.ppermute(outward, "dp", [(1, 0), (2, 3)])
    wants = lax.dynamic_index_in_dim(sources, plane, 1, keepdims=True)[:, :, None]
    near = jnp.where(wants == 3 - plane, beside, far)
    inner = jnp.where((wants == 0) & (plane == 1), from_below, near)
    inner = jnp.where((wants == 3) & (plane == 2), from_above, inner)
    moved = jnp.where((plane == 0) | (plane == 3), at_edge, inner)
    return jnp.where(wants == plane, item, moved)


def line_sum(block):
    plane = lax.axis_index("dp")
    arrived = lax.ppermute(block, "dp", [(0, 1), (3, 2)])
    half = (block.astype(F32) + arrived.astype(F32)).astype(BF16)
    other = lax.ppermute(half, "dp", [(1, 2), (2, 1)])
    full = (half.astype(F32) + other.astype(F32)).astype(BF16)
    edge = lax.ppermute(full, "dp", [(1, 0), (2, 3)])
    return jnp.where((plane == 0) | (plane == 3), edge, full)


def attention_body(qkv_ref, back_ref, cos_ref, low_ref, high_ref, begin_ref, attn_ref, grad_ref):
    scale = 1.0 / math.sqrt(HD)
    cos, low, high = cos_ref[...], low_ref[...], high_ref[...]

    def turn(values):
        return values * cos + pltpu.roll(values, HD - 16, 1) * low + pltpu.roll(values, 16, 1) * high

    def turn_back(values):
        return (
            values * cos
            + pltpu.roll(values * high, HD - 16, 1)
            + pltpu.roll(values * low, 16, 1)
        )

    def product(left, right, dims):
        return lax.dot_general(left, right, (dims, ((), ())), preferred_element_type=F32)

    query = turn(qkv_ref[:, :HD]).astype(BF16)
    key = turn(qkv_ref[:, HD : 2 * HD]).astype(BF16)
    value = qkv_ref[:, 2 * HD :].astype(BF16)
    back = back_ref[...]
    rows = query.shape[0]
    scores = product(query, key, ((1,), (1,))) * scale
    at = lax.broadcasted_iota(jnp.int32, (rows, rows), 0)
    of = lax.broadcasted_iota(jnp.int32, (rows, rows), 1)
    allowed = (of <= at) & (of >= begin_ref[:, :1])
    scores = jnp.where(allowed, scores, masked_score)
    weight = jnp.exp(scores - jnp.max(scores, axis=1, keepdims=True))
    probs = weight * (1.0 / jnp.sum(weight, axis=1, keepdims=True))
    probs_low = probs.astype(BF16)
    attn_ref[...] = product(probs_low, value, ((1,), (0,))).astype(BF16)
    grad_probs = product(back, value, ((1,), (1,)))
    centre = jnp.sum(probs * grad_probs, axis=1, keepdims=True)
    grad_scores = (probs * (grad_probs - centre)).astype(BF16)
    grad_query = product(grad_scores, key, ((1,), (0,))) * scale
    grad_key = product(grad_scores, query, ((0,), (0,))) * scale
    grad_ref[:, :HD] = turn_back(grad_query).astype(BF16)
    grad_ref[:, HD : 2 * HD] = turn_back(grad_key).astype(BF16)
    grad_ref[:, 2 * HD :] = product(probs_low, back, ((0,), (0,))).astype(BF16)


def attention_both(qkv, back, cos, low, high, begin):
    rows = qkv.shape[0]
    heads = qkv.shape[1] // (3 * HD)
    slab = 512
    per_slab = pl.BlockSpec((slab, HD), lambda s, h: (s, 0))
    return pl.pallas_call(
        attention_body,
        grid=(rows // slab, heads),
        in_specs=[
            pl.BlockSpec((slab, 3 * HD), lambda s, h: (s, h)),
            pl.BlockSpec((slab, HD), lambda s, h: (s, h)),
            per_slab,
            per_slab,
            per_slab,
            per_slab,
        ],
        out_specs=[
            pl.BlockSpec((slab, HD), lambda s, h: (s, h)),
            pl.BlockSpec((slab, 3 * HD), lambda s, h: (s, h)),
        ],
        out_shape=[
            jax.ShapeDtypeStruct((rows, heads * HD), BF16),
            jax.ShapeDtypeStruct((rows, heads * 3 * HD), BF16),
        ],
        compiler_params=pltpu.CompilerParams(vmem_limit_bytes=40 * 1024 * 1024),
        cost_estimate=pl.CostEstimate(
            flops=14 * rows * slab * HD * heads,
            bytes_accessed=rows * heads * HD * 24,
            transcendentals=rows * slab * heads,
        ),
    )(qkv, back, cos, low, high, begin)


def dealt_layer(
    layer_input,
    lengths,
    deal_table,
    ln1_gain,
    ln1_bias,
    qkv_weight,
    qkv_bias,
    dense_weight,
    dense_bias,
    ln2_gain,
    ln2_bias,
    fc1_weight,
    fc1_bias,
    fc2_weight,
    fc2_bias,
    cotangent,
):
    plane = lax.axis_index("dp")
    row = lax.axis_index("row")
    col = lax.axis_index("col")
    own_rows, own_feats = layer_input.shape
    rows = 2 * own_rows
    slab = own_rows // 2
    qkv_cols = qkv_weight.shape[1]
    qkv_here = qkv_cols // 4
    attn_here = dense_weight.shape[0] // 4
    hidden_cols = fc1_weight.shape[1]
    hidden_here = hidden_cols // 4

    slab_ids = 2 * col + jnp.arange(2, dtype=jnp.int32)
    deal_here = lax.dynamic_slice_in_dim(deal_table, 2 * col, 2, 0)
    undeal_here = jnp.argmax(
        deal_here[:, None, :] == jnp.arange(4, dtype=jnp.int32)[None, :, None], axis=2
    ).astype(jnp.int32)

    def plane_gather(own):
        across = row_swap(own, 2)
        halves = [[own, across], [col_swap(own), col_swap(across)]]
        return [
            [pair[0], row_swap(pair[0], 1), pair[1], row_swap(pair[1], 1)] for pair in halves
        ]

    def swap_rows(pieces):
        return [pieces(0)] + [row_swap(pieces(j), j) for j in (1, 2, 3)]

    x_parts = plane_gather(layer_input)
    norms = jnp.stack([ln1_gain, ln1_bias, ln2_gain, ln2_bias])
    norms = jnp.concatenate(swap_rows(lambda j: norms), axis=1)

    cot_own = line_route(cotangent.reshape(2, slab, own_feats), undeal_here).reshape(
        own_rows, own_feats
    )
    cot_parts = plane_gather(cot_own)

    def first_slice(weight, width, at, size):
        parts = swap_rows(
            lambda j: lax.dynamic_slice_in_dim(weight, (row ^ j) * width + at, size, 1)
        )
        return jnp.concatenate(parts, axis=0)

    def second_slice(weight, width, at, size):
        parts = swap_rows(
            lambda j: lax.dynamic_slice_in_dim(weight, (row ^ j) * width + at, size, 0)
        )
        return jnp.concatenate(parts, axis=1)

    chunks = range(0, hidden_here, CHUNK)
    fc1_parts = [first_slice(fc1_weight, hidden_here, at, CHUNK) for at in chunks]
    fc2_parts = [second_slice(fc2_weight, hidden_here, at, CHUNK) for at in chunks]
    qkv_here_weight = first_slice(qkv_weight, qkv_here, 0, qkv_here)
    dense_here = second_slice(dense_weight, attn_here, 0, attn_here)

    x_all = jnp.concatenate([jnp.concatenate(half, axis=1) for half in x_parts], axis=0)
    wide = x_all.astype(F32)
    mean = jnp.sum(wide, axis=1, keepdims=True) / D
    inv_std = lax.rsqrt(jnp.sum(wide * wide, axis=1, keepdims=True) / D - mean * mean + norm_epsilon)
    normed = (wide - mean) * inv_std
    ln1_all = (normed * norms[0] + norms[1]).astype(BF16)
    ln2_all = (normed * norms[2] + norms[3]).astype(BF16)
    cot_all = jnp.concatenate([jnp.concatenate(half, axis=1) for half in cot_parts], axis=0)

    qkv_bias_here = lax.dynamic_slice_in_dim(qkv_bias, row * qkv_here, qkv_here, 0)
    fc1_bias_here = lax.dynamic_slice_in_dim(fc1_bias, row * hidden_here, hidden_here, 0)

    qkv_grad = jnp.zeros((own_feats, qkv_cols), F32)
    fc1_grad = jnp.zeros((own_feats, hidden_cols), F32)
    dense_grad = jnp.zeros((dense_weight.shape[0], own_feats), F32)
    fc2_grad = jnp.zeros((fc2_weight.shape[0], own_feats), F32)

    def first_grad(total, grad, width, at):
        size = grad.shape[1]
        pieces = swap_rows(lambda j: grad[j * own_feats : (j + 1) * own_feats])
        summed = line_sum(jnp.concatenate(pieces, axis=0)).astype(F32)
        for j in range(4):
            total = lax.dynamic_update_slice(
                total,
                summed[j * own_feats : (j + 1) * own_feats],
                (0, (row ^ j) * width + at),
            )
        return total

    def second_grad(total, grad, width, at):
        size = grad.shape[0]
        pieces = swap_rows(lambda j: grad[:, j * own_feats : (j + 1) * own_feats])
        summed = line_sum(jnp.concatenate(pieces, axis=0)).astype(F32)
        for j in range(4):
            total = lax.dynamic_update_slice(
                total, summed[j * size : (j + 1) * size], ((row ^ j) * width + at, 0)
            )
        return total

    acts, hidden_grads, hidden_sums = [], [], []
    gain2 = jnp.zeros((D,), F32)
    for k, at in enumerate(chunks):
        hidden = (
            jnp.dot(ln2_all, fc1_parts[k], preferred_element_type=F32)
            + fc1_bias_here[at : at + CHUNK]
        )
        act, gelu_back = jax.vjp(partial(jax.nn.gelu, approximate=False), hidden)
        act = act.astype(BF16)
        grad_act = contract_cols(cot_all, fc2_parts[k])
        grad_hidden = gelu_back(grad_act)[0].astype(BF16)
        acts.append(act)
        hidden_grads.append(grad_hidden)
        hidden_sums.append(jnp.sum(grad_hidden, axis=0, dtype=F32))
        fc2_grad = second_grad(
            fc2_grad, contract_rows(act, cot_all).astype(BF16), hidden_here, at
        )
        grad = contract_rows(ln2_all, grad_hidden)
        gain2 += jnp.sum(grad * fc1_parts[k].astype(F32), axis=1)
        fc1_grad = first_grad(fc1_grad, grad.astype(BF16), hidden_here, at)

    qkv = jnp.dot(ln1_all, qkv_here_weight, preferred_element_type=F32) + qkv_bias_here
    grad_mix = contract_cols(cot_all, dense_here).astype(BF16)
    slab_order = jnp.concatenate([slab_ids, (slab_ids + 2) % 4])
    lengths_here = jnp.take(lengths, plane * 4 + slab_order, axis=0)
    positions = jnp.concatenate([segment_layout(lengths_here[s], slab)[1] for s in range(4)])
    begins = jnp.tile(jnp.arange(slab, dtype=jnp.int32), 4) - positions
    cos_table, sin_table = rotary_tables(positions)
    lane = jnp.arange(HD)
    cos_table = jnp.pad(cos_table, ((0, 0), (0, HD - ROT)), constant_values=1.0)
    sin_table = jnp.pad(sin_table, ((0, 0), (0, HD - ROT)))
    low_table = jnp.where(lane < ROT // 2, -sin_table, 0.0)
    high_table = jnp.where(lane < ROT // 2, 0.0, sin_table)
    attn, grad_qkv = attention_both(
        qkv,
        grad_mix,
        cos_table,
        low_table,
        high_table,
        jnp.broadcast_to(begins[:, None], (rows, HD)),
    )
    dense_grad = second_grad(dense_grad, contract_rows(attn, cot_all).astype(BF16), attn_here, 0)
    gain1 = jnp.zeros((D,), F32)
    for at in range(0, qkv_here, CHUNK):
        grad = contract_rows(ln1_all, grad_qkv[:, at : at + CHUNK])
        gain1 += jnp.sum(grad * qkv_here_weight[:, at : at + CHUNK].astype(F32), axis=1)
        qkv_grad = first_grad(qkv_grad, grad.astype(BF16), qkv_here, at)
    qkv_sum = jnp.sum(grad_qkv, axis=0, dtype=F32)
    hidden_sum = jnp.concatenate(hidden_sums)

    def plane_scatter(part):
        blocks = [part[:, j * own_feats : (j + 1) * own_feats] for j in range(4)]
        sent = [row_swap(blocks[j].astype(BF16), 1) for j in (1, 3)]
        chip = [blocks[2 * j] + sent[j].astype(F32) for j in range(2)]
        sent = [col_swap(chip[j][own_rows:].astype(BF16)) for j in range(2)]
        half = [chip[j][:own_rows] + sent[j].astype(F32) for j in range(2)]
        return half[0] + row_swap(half[1].astype(BF16), 2).astype(F32)

    branch = plane_scatter(
        jnp.dot(
            jnp.concatenate([attn] + acts, axis=1),
            jnp.concatenate([dense_here] + fc2_parts, axis=0),
            preferred_element_type=F32,
        )
    )
    output = (layer_input.astype(F32) + branch + dense_bias + fc2_bias).astype(BF16)
    output = line_route(output.reshape(2, slab, own_feats), deal_here).reshape(own_rows, own_feats)

    fc1_here = jnp.concatenate(fc1_parts, axis=1)
    grad_hidden = jnp.concatenate(hidden_grads, axis=1)
    grad_normed = plane_scatter(
        contract_cols(grad_qkv, qkv_here_weight) * norms[0]
        + contract_cols(grad_hidden, fc1_here) * norms[2]
    )
    normed_own = normed[:own_rows, :own_feats]
    row_sums = lax.psum(
        (jnp.sum(grad_normed, axis=1), jnp.sum(grad_normed * normed_own, axis=1)), "row"
    )
    input_grad = cot_own.astype(F32) + inv_std[:own_rows] * (
        grad_normed - row_sums[0][:, None] / D - normed_own * row_sums[1][:, None] / D
    )

    bias1 = jnp.dot(qkv_here_weight.astype(F32), qkv_sum, precision="highest")
    bias2 = jnp.dot(fc1_here.astype(F32), hidden_sum, precision="highest")
    gain1 = (gain1 - norms[1] * bias1) / norms[0]
    gain2 = (gain2 - norms[3] * bias2) / norms[2]
    norm_sums = jnp.stack([gain1, bias1, gain2, bias2]).reshape(4, 4, own_feats)
    norm_sums = jnp.stack(
        [lax.dynamic_index_in_dim(norm_sums, row ^ j, 1, keepdims=False) for j in range(4)], axis=1
    )
    bias_here = jnp.sum(cotangent, axis=0, dtype=F32)
    bias_sum = jnp.zeros((4, own_feats), F32).at[row].set(bias_here)
    qkv_sums = jnp.zeros((2, 4, qkv_here), F32).at[col, row].set(qkv_sum)
    hidden_sums = jnp.zeros((2, 4, hidden_here), F32).at[col, row].set(hidden_sum)
    small = lax.psum(
        jnp.concatenate(
            [norm_sums.reshape(-1), bias_sum.reshape(-1), qkv_sums.reshape(-1), hidden_sums.reshape(-1)]
        ),
        ("dp", "row", "col"),
    )
    sizes = [4 * D, D, 2 * qkv_cols]
    norm_sums, bias_sum, qkv_sums, hidden_sums = jnp.split(
        small, [sizes[0], sizes[0] + sizes[1], sum(sizes)]
    )
    norm_sums = lax.dynamic_index_in_dim(norm_sums.reshape(4, 4, own_feats), row, 1, keepdims=False)
    bias_sum = lax.dynamic_index_in_dim(bias_sum.reshape(4, own_feats), row, 0, keepdims=False)
    qkv_bias_grad = lax.dynamic_index_in_dim(qkv_sums.reshape(2, qkv_cols), col, 0, keepdims=False)
    fc1_bias_grad = lax.dynamic_index_in_dim(
        hidden_sums.reshape(2, hidden_cols), col, 0, keepdims=False
    )
    return (
        output,
        input_grad,
        norm_sums[0],
        norm_sums[1],
        qkv_grad,
        qkv_bias_grad,
        dense_grad,
        bias_sum,
        norm_sums[2],
        norm_sums[3],
        fc1_grad,
        fc1_bias_grad,
        fc2_grad,
        bias_sum,
    )


def solution(mesh):
    grid = tuple(mesh.shape[axis] for axis in ("dp", "row", "col"))
    placed = (
        P(("dp", "col"), "row"),
        P(),
        P(),
        P("row"),
        P("row"),
        P("row", "col"),
        P("col"),
        P("col", "row"),
        P("row"),
        P("row"),
        P("row"),
        P("row", "col"),
        P("col"),
        P("col", "row"),
        P("row"),
        P(("dp", "col"), "row"),
    )
    return jax.shard_map(
        dealt_layer if grid == (4, 4, 2) else local,
        mesh=mesh,
        in_specs=placed,
        out_specs=(
            P(("dp", "col"), "row"),
            P(("dp", "col"), "row"),
            P("row"),
            P("row"),
            P("row", "col"),
            P("col"),
            P("col", "row"),
            P("row"),
            P("row"),
            P("row"),
            P("row", "col"),
            P("col"),
            P("col", "row"),
            P("row"),
        ),
        check_vma=False,
    )
```

```python
from functools import partial
import math

import jax
import jax.numpy as jnp
from jax import lax
from jax.experimental import pallas as pl
from jax.experimental.pallas import tpu as pltpu
from jax.sharding import PartitionSpec as P

D = 2048
HD = 128
ROT = 32
QBLK = 512
CHUNK = 256
BF16 = jnp.bfloat16
F32 = jnp.float32


norm_epsilon = 1e-05
masked_score = -1000000000.0


def rotary_tables(positions):
    frequency = 1.0 / 10000.0 ** (jnp.arange(0, ROT, 2, dtype=jnp.float32) / ROT)
    angles = positions.astype(jnp.float32)[:, None] * frequency[None, :]
    angles = jnp.concatenate([angles, angles], axis=1)
    return (jnp.cos(angles), jnp.sin(angles))


def rotate(values, cos_table, sin_table):
    half_rot = ROT // 2
    rotated = values[..., :ROT]
    turned = jnp.concatenate([-rotated[..., half_rot:], rotated[..., :half_rot]], axis=-1)
    rotated = rotated * cos_table[:, None, :] + turned * sin_table[:, None, :]
    return jnp.concatenate([rotated, values[..., ROT:]], axis=-1)


def segment_layout(seq_lengths, length):
    seq_ends = jnp.cumsum(seq_lengths)
    token_place = jnp.arange(length, dtype=jnp.int32)
    sequence_ids = jnp.sum((token_place[:, None] >= seq_ends[None, :]).astype(jnp.int32), axis=1)
    starts = seq_ends - seq_lengths
    seq_hits = sequence_ids[:, None] == jnp.arange(seq_lengths.shape[0], dtype=jnp.int32)[None, :]
    seq_begin = jnp.sum(jnp.where(seq_hits, starts[None, :], 0), axis=1)
    return (sequence_ids, token_place - seq_begin)


def contract_rows(left_side, right_side):
    return lax.dot_general(
        left_side, right_side, (((0,), (0,)), ((), ())), preferred_element_type=jnp.float32
    )


def contract_cols(left_side, right_side):
    return lax.dot_general(
        left_side, right_side, (((1,), (1,)), ((), ())), preferred_element_type=jnp.float32
    )


def pick_rows(pooled, chosen):
    row_hits = chosen[None, :] == jnp.arange(pooled.shape[0], dtype=jnp.int32)[:, None]
    return jnp.sum(jnp.where(row_hits[:, :, None], pooled.astype(jnp.float32), 0.0), axis=0)


def local(
    layer_input,
    lengths,
    deal_table,
    ln1_gain,
    ln1_bias,
    qkv_weight,
    qkv_bias,
    dense_weight,
    dense_bias,
    ln2_gain,
    ln2_bias,
    fc1_weight,
    fc1_bias,
    fc2_weight,
    fc2_bias,
    cotangent,
):
    dp_count = lax.axis_size("dp")
    row_count = lax.axis_size("row")
    col_count = lax.axis_size("col")
    group_id = lax.axis_index("dp")
    row_id = lax.axis_index("row")
    col_id = lax.axis_index("col")
    own_rows, own_feats = layer_input.shape
    group_rows = own_rows * col_count
    slab_rows = group_rows // row_count
    qkv_cols = qkv_weight.shape[1]
    attn_cols = dense_weight.shape[0]
    heads_here = qkv_cols // (3 * HD)
    score_scale = 1.0 / math.sqrt(HD)
    local_slab = (col_id * own_rows + jnp.arange(own_rows, dtype=jnp.int32)) // slab_rows
    slab_hits = local_slab[:, None] == jnp.arange(row_count, dtype=jnp.int32)[None, :]
    deal_here = lax.dynamic_index_in_dim(deal_table, group_id, 1, keepdims=False)
    source = jnp.sum(jnp.where(slab_hits, deal_here[None, :], 0), axis=1)
    pooled = lax.all_gather(layer_input, "dp", axis=0, tiled=True).reshape(
        dp_count, own_rows, own_feats
    )
    mine_rows = pick_rows(pooled, source).astype(jnp.bfloat16)
    input_all = lax.all_gather(mine_rows, "col", axis=0, tiled=True)
    input_wide = input_all.astype(jnp.float32)
    row_stats = lax.psum(
        (jnp.sum(input_wide, axis=1), jnp.sum(input_wide * input_wide, axis=1)), "row"
    )
    row_mean = row_stats[0] / D
    inv_std = lax.rsqrt(row_stats[1] / D - row_mean * row_mean + norm_epsilon)
    normed = (input_wide - row_mean[:, None]) * inv_std[:, None]
    own_start = col_id * own_rows
    normed_own = lax.dynamic_slice_in_dim(normed, own_start, own_rows, 0)
    inv_std_own = lax.dynamic_slice_in_dim(inv_std, own_start, own_rows, 0)
    ln1_all = (normed * ln1_gain + ln1_bias).astype(jnp.bfloat16)
    ln2_all = (normed * ln2_gain + ln2_bias).astype(jnp.bfloat16)
    part_one = ln1_all
    part_two = ln2_all
    first_sums = lax.psum_scatter(
        jnp.concatenate(
            [
                jnp.dot(part_one, qkv_weight, preferred_element_type=jnp.float32),
                jnp.dot(part_two, fc1_weight, preferred_element_type=jnp.float32),
            ],
            axis=1,
        ),
        "row",
        scatter_dimension=0,
        tiled=True,
    )
    qkv_out = first_sums[:, :qkv_cols] + qkv_bias
    hidden = first_sums[:, qkv_cols:] + fc1_bias
    slab_source = (
        lax.dynamic_index_in_dim(deal_here, row_id, 0, keepdims=False) * row_count + row_id
    )
    seq_lengths = lax.dynamic_index_in_dim(lengths, slab_source, 0, keepdims=False)
    sequence_ids, positions = segment_layout(seq_lengths, slab_rows)
    token_place = jnp.arange(slab_rows, dtype=jnp.int32)
    cos_table, sin_table = rotary_tables(positions)
    packed = qkv_out.reshape(slab_rows, heads_here, 3, HD)
    query_pre = packed[:, :, 0]
    key_pre = packed[:, :, 1]
    queries = rotate(query_pre, cos_table, sin_table).astype(jnp.bfloat16)
    keys_rot = rotate(key_pre, cos_table, sin_table).astype(jnp.bfloat16)
    values = packed[:, :, 2].astype(jnp.bfloat16)

    def block_scores(block_id):
        first_row = block_id * QBLK
        last_row = first_row + QBLK
        allowed = (sequence_ids[first_row:last_row, None] == sequence_ids[None, :last_row]) & (
            token_place[None, :last_row] <= token_place[first_row:last_row, None]
        )
        scores = (
            jnp.einsum("qhd,khd->hqk", queries, keys_rot, preferred_element_type=jnp.float32)
            * score_scale
        )
        return jnp.where(allowed[None], scores, masked_score)

    block_id = 0
    last_row = (block_id + 1) * QBLK
    scores = block_scores(block_id)
    row_top = jnp.max(scores, axis=-1, keepdims=True)
    exp_total = jnp.sum(jnp.exp(scores - row_top), axis=-1, keepdims=True)
    log_total = row_top + jnp.log(exp_total)
    probs_low = jnp.exp(scores - log_total).astype(jnp.bfloat16)
    mixtures = jnp.einsum("hqk,khd->qhd", probs_low, values, preferred_element_type=jnp.float32)
    log_totals = [log_total]
    attn_out = mixtures.reshape(slab_rows, attn_cols).astype(jnp.bfloat16)
    activated = jax.nn.gelu(hidden, approximate=False).astype(jnp.bfloat16)
    attn_all, act_all = (
        lax.all_gather(attn_out, "row", axis=0, tiled=True),
        lax.all_gather(activated, "row", axis=0, tiled=True),
    )
    part_one = attn_all
    part_two = act_all
    branch_sum = lax.psum_scatter(
        jnp.dot(part_one, dense_weight, preferred_element_type=jnp.float32)
        + jnp.dot(part_two, fc2_weight, preferred_element_type=jnp.float32),
        "col",
        scatter_dimension=0,
        tiled=True,
    )
    output = (mine_rows.astype(jnp.float32) + branch_sum + dense_bias + fc2_bias).astype(
        jnp.bfloat16
    )
    grad_all = lax.all_gather(cotangent, "col", axis=0, tiled=True)
    dense_grad = contract_rows(attn_all, grad_all)
    fc2_grad = contract_rows(act_all, grad_all)
    out_bias_grad = jnp.sum(grad_all, axis=0, dtype=jnp.float32)
    grad_block = grad_all
    grad_second = lax.psum_scatter(
        jnp.concatenate(
            [contract_cols(grad_block, dense_weight), contract_cols(grad_block, fc2_weight)], axis=1
        ),
        "row",
        scatter_dimension=0,
        tiled=True,
    )
    grad_mix = grad_second[:, :attn_cols].astype(jnp.bfloat16).reshape(slab_rows, heads_here, HD)
    gelu_back = jax.vjp(partial(jax.nn.gelu, approximate=False), hidden)[1]
    grad_hidden = gelu_back(grad_second[:, attn_cols:])[0]
    grad_key = jnp.zeros((slab_rows, heads_here, HD), jnp.float32)
    grad_value = jnp.zeros((slab_rows, heads_here, HD), jnp.float32)
    block_id = 0
    first_row = block_id * QBLK
    last_row = first_row + QBLK
    probs_full = jnp.exp(block_scores(block_id) - log_totals[block_id])
    probs_low = probs_full.astype(jnp.bfloat16)
    grad_block = grad_mix
    grad_value = grad_value.at[:last_row].add(
        jnp.einsum("hqk,qhd->khd", probs_low, grad_block, preferred_element_type=jnp.float32)
    )
    grad_probs = jnp.einsum("qhd,khd->hqk", grad_block, values, preferred_element_type=jnp.float32)
    centre = jnp.sum(probs_full * grad_probs, axis=-1, keepdims=True)
    grad_scores = (probs_full * (grad_probs - centre)).astype(jnp.bfloat16)
    grad_queries = (
        jnp.einsum("hqk,khd->qhd", grad_scores, keys_rot, preferred_element_type=jnp.float32)
        * score_scale
    )
    grad_key = grad_key.at[:last_row].add(
        jnp.einsum("hqk,qhd->khd", grad_scores, queries, preferred_element_type=jnp.float32)
        * score_scale
    )
    turn_back = jax.vjp(lambda values_in: rotate(values_in, cos_table, sin_table), query_pre)[1]
    grad_query_pre = turn_back(grad_queries)[0]
    grad_key_pre = turn_back(grad_key)[0]
    grad_qkv = jnp.stack([grad_query_pre, grad_key_pre, grad_value], axis=2).reshape(
        slab_rows, qkv_cols
    )
    grad_first = jnp.concatenate([grad_qkv, grad_hidden], axis=1).astype(jnp.bfloat16)
    grad_first_all = lax.all_gather(grad_first, "row", axis=0, tiled=True)
    grad_qkv_all = grad_first_all[:, :qkv_cols]
    grad_hidden_all = grad_first_all[:, qkv_cols:]
    qkv_weight_grad = contract_rows(ln1_all, grad_qkv_all)
    qkv_bias_grad = jnp.sum(grad_qkv_all, axis=0, dtype=jnp.float32)
    fc1_weight_grad = contract_rows(ln2_all, grad_hidden_all)
    fc1_bias_grad = jnp.sum(grad_hidden_all, axis=0, dtype=jnp.float32)
    grad_block = grad_first_all
    summed = lax.psum_scatter(
        jnp.concatenate(
            [
                contract_cols(grad_block[:, :qkv_cols], qkv_weight),
                contract_cols(grad_block[:, qkv_cols:], fc1_weight),
            ],
            axis=1,
        ),
        "col",
        scatter_dimension=0,
        tiled=True,
    )
    grad_ln_one = summed[:, :own_feats]
    grad_ln_two = summed[:, own_feats:]
    gain_terms = (
        jnp.sum(grad_ln_one * normed_own, axis=0),
        jnp.sum(grad_ln_one, axis=0),
        jnp.sum(grad_ln_two * normed_own, axis=0),
        jnp.sum(grad_ln_two, axis=0),
    )
    grad_normed = grad_ln_one * ln1_gain + grad_ln_two * ln2_gain
    row_sums = lax.psum(
        (jnp.sum(grad_normed, axis=1), jnp.sum(grad_normed * normed_own, axis=1)), "row"
    )
    grad_dealt = cotangent.astype(jnp.float32) + inv_std_own[:, None] * (
        grad_normed - row_sums[0][:, None] / D - normed_own * row_sums[1][:, None] / D
    )
    gain_sums = lax.psum(
        (gain_terms[0], gain_terms[1], gain_terms[2], gain_terms[3]), ("dp", "col")
    )
    weights_summed = lax.psum(
        (
            qkv_weight_grad,
            qkv_bias_grad,
            dense_grad,
            fc1_weight_grad,
            fc1_bias_grad,
            fc2_grad,
            out_bias_grad,
        ),
        "dp",
    )
    pool_back = lax.all_gather(grad_dealt, "dp", axis=0, tiled=True).reshape(
        dp_count, own_rows, own_feats
    )
    back_here = jnp.sum(
        jnp.where(deal_table == group_id, jnp.arange(dp_count, dtype=jnp.int32)[None, :], 0), axis=1
    )
    target = jnp.sum(jnp.where(slab_hits, back_here[None, :], 0), axis=1)
    input_grad = pick_rows(pool_back, target)
    return (
        output,
        input_grad,
        gain_sums[0],
        gain_sums[1],
        weights_summed[0],
        weights_summed[1],
        weights_summed[2],
        weights_summed[6],
        gain_sums[2],
        gain_sums[3],
        weights_summed[3],
        weights_summed[4],
        weights_summed[5],
        weights_summed[6],
    )


UNIT = 256
TILE = 512


def product(left, right, dims):
    return lax.dot_general(left, right, (dims, ((), ())), preferred_element_type=F32)


def fold_lanes(values):
    total = values[:, :128]
    for at in range(128, values.shape[1], 128):
        total = total + values[:, at : at + 128]
    return total


class Copies:
    def __init__(self, send_sems, recv_sems):
        self.send_sems, self.recv_sems, self.used = send_sems, recv_sems, 0

    def make(self, source, target, device):
        number = self.used
        self.used += 1

        def build():
            return pltpu.make_async_remote_copy(
                src_ref=source(),
                dst_ref=target(),
                send_sem=self.send_sems.at[number],
                recv_sem=self.recv_sems.at[number],
                device_id=device,
                device_id_type=pl.DeviceIdType.MESH,
            )

        return build


def attention_head(qkv, back, cos, low, high, allowed):
    scale = 1.0 / math.sqrt(HD)

    def turn(values):
        return values * cos + pltpu.roll(values, HD - 16, 1) * low + pltpu.roll(values, 16, 1) * high

    def turn_back(values):
        return (
            values * cos
            + pltpu.roll(values * high, HD - 16, 1)
            + pltpu.roll(values * low, 16, 1)
        )

    query = turn(qkv[:, :HD]).astype(BF16)
    key = turn(qkv[:, HD : 2 * HD]).astype(BF16)
    value = qkv[:, 2 * HD :].astype(BF16)
    scores = product(query, key, ((1,), (1,))) * scale
    scores = jnp.where(allowed, scores, masked_score)
    weight = jnp.exp(scores - jnp.max(scores, axis=1, keepdims=True))
    probs = weight * (1.0 / jnp.sum(weight, axis=1, keepdims=True))
    probs_low = probs.astype(BF16)
    attn = product(probs_low, value, ((1,), (0,))).astype(BF16)
    grad_probs = product(back, value, ((1,), (1,)))
    centre = jnp.sum(probs * grad_probs, axis=1, keepdims=True)
    grad_scores = (probs * (grad_probs - centre)).astype(BF16)
    grad_query = product(grad_scores, key, ((1,), (0,))) * scale
    grad_key = product(grad_scores, query, ((0,), (0,))) * scale
    grad_value = product(probs_low, back, ((0,), (0,)))
    return attn, [turn_back(grad_query), turn_back(grad_key), grad_value]


def layer_kernel(
    codes,
    x_own,
    cot_in,
    norm_own,
    bias_in,
    out_bias,
    qkv_w,
    dense_w,
    fc1_w,
    fc2_w,
    cos_in,
    low_in,
    high_in,
    begin_in,
    first_sum,
    second_sum,
    output,
    grad_norm,
    cot_own,
    stats,
    gain_q,
    bias_q,
    gain_f,
    bias_f,
    unit_sums,
    x_all,
    cot_all,
    ln1,
    ln2,
    w1,
    w2,
    acts,
    grads,
    first_part,
    second_part,
    first_here,
    second_here,
    first_in,
    second_in,
    first_half,
    second_half,
    first_other,
    second_other,
    out_part,
    out_core,
    out_chip,
    out_x,
    out_half,
    out_y,
    out_item,
    dx_part,
    dx_core,
    dx_chip,
    dx_x,
    dx_half,
    dx_y,
    cot_up,
    cot_down,
    cot_far,
    cot_send,
    cot_edge,
    out_up,
    out_down,
    out_far,
    out_send,
    out_edge,
    acc,
    norm_all,
    gain_acc,
    sum_acc,
    send_sems,
    recv_sems,
    local_sems,
):
    z, r, c = lax.axis_index("dp"), lax.axis_index("row"), lax.axis_index("col")
    y, core = r // 2, r % 2
    mid = ((z + 1) // 2) % 2
    upper = z // 2
    z_in = mid * (3 - z) + (1 - mid) * (1 + upper)
    z_out = 3 * upper
    is_mid, is_edge = mid == 1, mid == 0
    peer = [r, 2 * y + (1 - core), 2 * (1 - y) + core, 2 * (1 - y) + (1 - core)]
    slabs, slab, feats = x_own.shape
    own_rows = slabs * slab
    rows = 2 * own_rows
    hidden_here = fc1_w.shape[1] // 4
    qkv_here = qkv_w.shape[1] // 4
    attn_here = dense_w.shape[0] // 4
    to_row = [{"row": peer[j]} for j in range(4)]
    to_col = {"col": 1 - c}
    to_in = {"dp": z_in}
    to_out = {"dp": z_out}
    copies = Copies(send_sems, recv_sems)
    sent = []

    barrier = pltpu.get_barrier_semaphore()

    def greet(device):
        pl.semaphore_signal(barrier, inc=1, device_id=device, device_id_type=pl.DeviceIdType.MESH)

    for j in (1, 2, 3):
        greet(to_row[j])
    greet(to_col)
    greet(to_in)

    @pl.when(is_mid)
    def _():
        greet(to_out)
        pl.semaphore_wait(barrier, 6)

    @pl.when(is_edge)
    def _():
        pl.semaphore_wait(barrier, 5)

    def start(copy):
        copy().start()
        sent.append(copy)

    def when(flag, action):
        pl.when(flag)(action)

    local_used = [0]

    def local(source, target):
        number = local_used[0]
        local_used[0] += 1

        def build():
            return pltpu.make_async_copy(source(), target(), local_sems.at[number])

        build().start()
        return build

    own_half = pl.ds(c * own_rows, own_rows)
    far_half = pl.ds((1 - c) * own_rows, own_rows)

    class Gather:
        def __init__(self, own, whole):
            self.whole = whole
            block = lambda j, half: whole.at[peer[j], pl.ds(slabs * half, slabs)]
            self.to_y = copies.make(lambda: own, lambda: block(0, c), to_row[2])
            self.to_x = copies.make(lambda: own, lambda: block(0, c), to_col)
            self.to_core = copies.make(lambda: own, lambda: block(0, c), to_row[1])
            self.y_to_x = copies.make(lambda: block(2, c), lambda: block(2, c), to_col)
            self.y_to_core = copies.make(
                lambda: block(2, c), lambda: block(2, c), to_row[1]
            )
            self.x_to_core = copies.make(
                lambda: block(0, 1 - c), lambda: block(0, 1 - c), to_row[1]
            )
            self.xy_to_core = copies.make(
                lambda: block(2, 1 - c), lambda: block(2, 1 - c), to_row[1]
            )
            self.own = own

        def begin(self):
            start(self.to_y)
            start(self.to_x)
            start(self.to_core)
            self.kept = local(lambda: self.own, lambda: self.whole.at[r, pl.ds(slabs * c, slabs)])

        def after_y(self):
            self.to_y().wait_recv()
            start(self.y_to_x)
            start(self.y_to_core)

        def after_x(self):
            self.to_x().wait_recv()
            start(self.x_to_core)
            self.y_to_x().wait_recv()
            start(self.xy_to_core)

        def end(self):
            self.kept().wait()
            for copy in (self.to_core, self.y_to_core, self.x_to_core, self.xy_to_core):
                copy().wait_recv()

    def choose(code_at, refs, target):
        def body(*blocks):
            code = codes[code_at + pl.program_id(0)]
            value = blocks[0][...]
            for which in range(1, len(refs)):
                value = jnp.where(code == which, blocks[which][...], value)
            blocks[-1][...] = value

        block = pl.BlockSpec((1, slab, feats), lambda q: (q, 0, 0))
        pltpu.emit_pipeline(
            body, grid=(2,), in_specs=[block] * len(refs), out_specs=[block]
        )(*refs, target)

    class Route:
        def __init__(self, item, code_at, up, down, far, send, edge, target):
            self.item, self.code_at, self.up, self.down = item, code_at, up, down
            self.far, self.send, self.edge, self.target = far, send, edge, target
            self.upward = copies.make(lambda: item, lambda: up, {"dp": z + 1})
            self.downward = copies.make(lambda: item, lambda: down, {"dp": z - 1})
            self.far_up = copies.make(lambda: up, lambda: far, to_in)
            self.far_down = copies.make(lambda: down, lambda: far, to_in)
            self.outward = copies.make(lambda: send, lambda: edge, to_out)

        def begin(self):
            when(z < 2, lambda: self.upward().start())
            when(z > 1, lambda: self.downward().start())

        def relay(self):
            def from_below():
                self.upward().wait_recv()
                self.far_up().start()
                self.downward().wait_recv()

            def from_above():
                self.downward().wait_recv()
                self.far_down().start()
                self.upward().wait_recv()

            when(z == 1, from_below)
            when(z == 2, from_above)

        def hand_out(self):
            def middle():
                when(z == 1, lambda: self.far_down().wait_recv())
                when(z == 2, lambda: self.far_up().wait_recv())
                choose(
                    self.code_at + 2, [self.item, self.up, self.down, self.far], self.send
                )
                self.outward().start()
                choose(self.code_at, [self.item, self.up, self.down, self.far], self.target)

            when(is_mid, middle)

        def take(self):
            def edge():
                self.outward().wait_recv()
                choose(self.code_at, [self.item, self.edge], self.target)

            when(is_edge, edge)

        def finish(self):
            when(z < 2, lambda: self.upward().wait_send())
            when(z > 1, lambda: self.downward().wait_send())
            when(z == 1, lambda: self.far_up().wait_send())
            when(z == 2, lambda: self.far_down().wait_send())
            when(is_mid, lambda: self.outward().wait_send())

    x_gather = Gather(x_own, x_all)
    cot_slabs = cot_in
    cot_route = Route(
        cot_slabs, 0, cot_up, cot_down, cot_far, cot_send, cot_edge, cot_own
    )
    norm_copies = [
        copies.make(lambda: norm_own, lambda: norm_all.at[r], to_row[j]) for j in (1, 2, 3)
    ]

    class Fetch:
        def __init__(self, first, first_at, first_width, at, second, second_at, second_width, low):
            def first_source(j):
                lanes = pl.multiple_of(peer[j] * first_width + first_at, 256)
                size = UNIT if first is fc1_w else qkv_here
                return first.at[:, pl.ds(lanes, size)]

            def second_source(j):
                size = UNIT
                begin = pl.multiple_of(peer[j] * second_width + second_at, 256)
                return second.at[pl.ds(begin, size)]

            size = UNIT if first is fc1_w else qkv_here
            first_target = lambda: w1.at[r, :, pl.ds(at, size)]
            second_target = lambda: w2.at[r, pl.ds(low, UNIT)]
            self.remote = []
            for j in (1, 2, 3):
                self.remote.append(
                    copies.make(partial(first_source, j), first_target, to_row[j])
                )
                self.remote.append(
                    copies.make(partial(second_source, j), second_target, to_row[j])
                )
            self.kept = [(partial(first_source, 0), first_target), (partial(second_source, 0), second_target)]

        def begin(self):
            for copy in self.remote:
                start(copy)
            self.kept = [local(*pair) for pair in self.kept]

        def end(self):
            for copy in self.remote:
                copy().wait_recv()
            for copy in self.kept:
                copy().wait()

    attn_fetch = Fetch(qkv_w, 0, qkv_here, 0, dense_w, 0, attn_here, 0)
    mlp_fetch = [
        Fetch(fc1_w, at, hidden_here, qkv_here + at, fc2_w, at, hidden_here, attn_here + at)
        for at in range(0, hidden_here, UNIT)
    ]

    class Unit:
        def __init__(self, kind, at):
            self.kind, self.at = kind, at
            if kind == 1:
                self.view = lambda ref, s: ref.at[s, :, pl.ds(at, UNIT)]
                self.whole = lambda ref: ref.at[:, :, pl.ds(at, UNIT)]
                self.block = pl.BlockSpec((1, feats, UNIT), lambda s: (s, 0, at // UNIT))
                self.refs = (first_part, first_here, first_in, first_half, first_other, first_sum)
            else:
                self.view = lambda ref, s: ref.at[s, pl.ds(at, UNIT)]
                self.whole = lambda ref: ref.at[:, pl.ds(at, UNIT)]
                self.block = pl.BlockSpec((1, UNIT, feats), lambda s: (s, at // UNIT, 0))
                self.refs = (
                    second_part,
                    second_here,
                    second_in,
                    second_half,
                    second_other,
                    second_sum,
                )
            part, here, arrived, half, other, total = self.refs
            self.spread = [
                copies.make(
                    partial(lambda j: self.view(part, peer[j]), j),
                    lambda: self.view(here, r),
                    to_row[j],
                )
                for j in (1, 2, 3)
            ]
            self.inward = copies.make(lambda: self.whole(here), lambda: self.whole(arrived), to_in)
            self.across = copies.make(lambda: self.whole(half), lambda: self.whole(other), to_in)
            self.outward = copies.make(lambda: self.whole(total), lambda: self.whole(total), to_out)

        def send(self):
            part, here = self.refs[:2]
            for copy in self.spread:
                start(copy)
            self.kept = local(lambda: self.view(part, r), lambda: self.view(here, r))

        def collect(self):
            for copy in self.spread:
                copy().wait_recv()
            self.kept().wait()
            when(is_edge, lambda: self.inward().start())

        def add(self, left, right, target):
            def body(left_block, right_block, target_block):
                target_block[...] = (
                    left_block[...].astype(F32) + right_block[...].astype(F32)
                ).astype(BF16)

            pltpu.emit_pipeline(
                body, grid=(4,), in_specs=[self.block] * 2, out_specs=[self.block]
            )(left, right, target)

        def halve(self):
            part, here, arrived, half, other, total = self.refs

            def middle():
                self.inward().wait_recv()
                self.add(here, arrived, half)
                self.across().start()

            when(is_mid, middle)

        def close(self):
            part, here, arrived, half, other, total = self.refs

            def middle():
                self.across().wait_recv()
                self.add(half, other, total)
                self.outward().start()

            when(is_mid, middle)

        def finish(self):
            def edge():
                self.outward().wait_recv()
                self.inward().wait_send()

            def middle():
                self.across().wait_send()
                self.outward().wait_send()

            when(is_edge, edge)
            when(is_mid, middle)

    mlp_units = [
        [Unit(2, attn_here + at), Unit(1, qkv_here + at)] for at in range(0, hidden_here, UNIT)
    ]
    attn_units = [Unit(2, 0)] + [Unit(1, at) for at in range(0, qkv_here, UNIT)]

    def norm_body(x_ref, one_ref, two_ref, stat_ref):
        wide = jnp.concatenate([x_ref[j, 0] for j in range(4)], axis=1).astype(F32)
        norms = jnp.concatenate([norm_all[j] for j in range(4)], axis=1)
        mean = jnp.sum(wide, axis=1, keepdims=True) / D
        square = jnp.sum(wide * wide, axis=1, keepdims=True) / D
        inv_std = lax.rsqrt(square - mean * mean + norm_epsilon)
        normed = (wide - mean) * inv_std
        one_ref[...] = (normed * norms[0:1] + norms[1:2]).astype(BF16)
        two_ref[...] = (normed * norms[2:3] + norms[3:4]).astype(BF16)
        lane = lax.broadcasted_iota(jnp.int32, stat_ref.shape, 1)
        stat_ref[...] = jnp.where(lane < 64, mean, inv_std)

    def norm_stage():
        tile = 256
        flat = pl.BlockSpec((tile, D), lambda i: (i, 0))
        pltpu.emit_pipeline(
            norm_body,
            grid=(rows // tile,),
            in_specs=[
                pl.BlockSpec(
                    (4, 1, tile, feats), lambda i: (0, i * tile // slab, i % (slab // tile), 0)
                )
            ],
            out_specs=[flat, flat, pl.BlockSpec((tile, 128), lambda i: (i, 0))],
        )(x_all, ln1, ln2, stats)

    def mlp_stage(k):
        at = k * UNIT
        bias = bias_in[0:1, qkv_here + at : qkv_here + at + UNIT]

        def body(ln_ref, cot_ref, first_ref, second_ref, act_ref, grad_ref):
            step = pl.program_id(0)

            @pl.when(step == 0)
            def _():
                acc[:, : 2 * UNIT, :] = jnp.zeros((4, 2 * UNIT, feats), F32)
                sum_acc[:, :UNIT] = jnp.zeros((8, UNIT), F32)

            hidden = bias
            grad_act = None
            for j in range(4):
                lanes = slice(j * feats, (j + 1) * feats)
                hidden = hidden + product(ln_ref[:, lanes], first_ref[j], ((1,), (0,)))
                term = product(cot_ref[j, 0], second_ref[j], ((1,), (1,)))
                grad_act = term if j == 0 else grad_act + term
            curve = 0.5 * (1.0 + lax.erf(hidden * math.sqrt(0.5)))
            bell = jnp.exp(-0.5 * hidden * hidden) * (1.0 / math.sqrt(2.0 * math.pi))
            act = (hidden * curve).astype(BF16)
            grad_hidden = (grad_act * (curve + hidden * bell)).astype(BF16)
            act_ref[...] = act
            grad_ref[...] = grad_hidden
            sum_acc[0:1, :UNIT] += jnp.sum(grad_hidden.astype(F32), axis=0, keepdims=True)
            for j in range(4):
                lanes = slice(j * feats, (j + 1) * feats)
                acc[j, :UNIT] += product(act, cot_ref[j, 0], ((0,), (0,)))
                acc[j, UNIT : 2 * UNIT] += product(grad_hidden, ln_ref[:, lanes], ((0,), (0,)))

        pltpu.emit_pipeline(
            body,
            grid=(rows // TILE,),
            in_specs=[
                pl.BlockSpec((TILE, D), lambda i: (i, 0)),
                pl.BlockSpec((4, 1, slab, feats), lambda i: (0, i, 0, 0)),
                pl.BlockSpec((4, feats, UNIT), lambda i: (0, 0, (qkv_here + at) // UNIT)),
                pl.BlockSpec((4, UNIT, feats), lambda i: (0, (attn_here + at) // UNIT, 0)),
            ],
            out_specs=[
                pl.BlockSpec((TILE, UNIT), lambda i: (i, (attn_here + at) // UNIT)),
                pl.BlockSpec((TILE, UNIT), lambda i: (i, (qkv_here + at) // UNIT)),
            ],
        )(ln2, cot_all, w1, w2, acts, grads)
        grad_stage(UNIT, qkv_here + at, attn_here + at, 1, k == 0)
        unit_sums[:, qkv_here + at : qkv_here + at + UNIT] = sum_acc[:, :UNIT]

    def grad_stage(width, first_at, second_at, which, fresh):
        def body(first_ref, part_one, part_two):
            j = pl.program_id(0)
            grad = acc[j, UNIT : UNIT + width].T
            weight = first_ref[0].astype(F32)
            part_one[0] = grad.astype(BF16)
            part_two[0] = acc[j, :UNIT].astype(BF16)
            here = pl.ds(j * feats, feats)
            gains = fold_lanes(grad * weight)
            biases = fold_lanes(weight * sum_acc[0:1, :width])
            if fresh:
                gain_acc[2 * which, here] = gains
                gain_acc[2 * which + 1, here] = biases
            else:
                gain_acc[2 * which, here] += gains
                gain_acc[2 * which + 1, here] += biases

        lanes = slice(first_at, first_at + width)
        block = pl.BlockSpec((1, feats, width), lambda j: (j, 0, 0))
        pltpu.emit_pipeline(
            body,
            grid=(4,),
            in_specs=[block],
            out_specs=[block, pl.BlockSpec((1, UNIT, feats), lambda j: (j, second_at // UNIT, 0))],
        )(w1.at[:, :, lanes], first_part.at[:, :, lanes], second_part)

    def attention_stage():
        heads = qkv_here // (3 * HD)
        bias = bias_in[0:1, :qkv_here]

        def body(
            ln_ref, cot_ref, first_ref, second_ref, cos, low, high, begin, act_ref, grad_ref
        ):
            step = pl.program_id(0)

            @pl.when(step == 0)
            def _():
                acc[...] = jnp.zeros(acc.shape, F32)
                sum_acc[...] = jnp.zeros(sum_acc.shape, F32)

            qkv = bias
            back = None
            for j in range(4):
                lanes = slice(j * feats, (j + 1) * feats)
                qkv = qkv + product(ln_ref[:, lanes], first_ref[j], ((1,), (0,)))
                term = product(cot_ref[j, 0], second_ref[j], ((1,), (1,)))
                back = term if j == 0 else back + term
            back = back.astype(BF16)
            at = lax.broadcasted_iota(jnp.int32, (TILE, TILE), 0)
            of = lax.broadcasted_iota(jnp.int32, (TILE, TILE), 1)
            allowed = (of <= at) & (of >= begin[:, :1])
            for h in range(heads):
                attn, grads_here = attention_head(
                    qkv[:, h * 3 * HD : (h + 1) * 3 * HD],
                    back[:, h * HD : (h + 1) * HD],
                    cos[...],
                    low[...],
                    high[...],
                    allowed,
                )
                act_ref[:, h * HD : (h + 1) * HD] = attn
                for i in range(3):
                    at_lane = (h * 3 + i) * HD
                    grad_ref[:, at_lane : at_lane + HD] = grads_here[i].astype(BF16)
            attn, grad = act_ref[...], grad_ref[...]
            sum_acc[0:1, :qkv_here] += jnp.sum(grad.astype(F32), axis=0, keepdims=True)
            for j in range(4):
                lanes = slice(j * feats, (j + 1) * feats)
                acc[j, :UNIT] += product(attn, cot_ref[j, 0], ((0,), (0,)))
                acc[j, UNIT:] += product(grad, ln_ref[:, lanes], ((0,), (0,)))

        table = pl.BlockSpec((TILE, HD), lambda i: (i, 0))
        pltpu.emit_pipeline(
            body,
            grid=(rows // TILE,),
            in_specs=[
                pl.BlockSpec((TILE, D), lambda i: (i, 0)),
                pl.BlockSpec((4, 1, slab, feats), lambda i: (0, i, 0, 0)),
                pl.BlockSpec((4, feats, qkv_here), lambda i: (0, 0, 0)),
                pl.BlockSpec((4, UNIT, feats), lambda i: (0, 0, 0)),
                table,
                table,
                table,
                table,
            ],
            out_specs=[
                pl.BlockSpec((TILE, UNIT), lambda i: (i, 0)),
                pl.BlockSpec((TILE, qkv_here), lambda i: (i, 0)),
            ],
        )(
            ln1,
            cot_all,
            w1.at[:, :, :qkv_here],
            w2,
            cos_in,
            low_in,
            high_in,
            begin_in,
            acts,
            grads.at[:, :qkv_here],
        )
        grad_stage(qkv_here, 0, 0, 0, True)
        unit_sums[:, :qkv_here] = sum_acc[:, :qkv_here]

    def out_stage():
        def body(act_ref, second_ref, part_ref):
            part_ref[0] = product(act_ref[...], second_ref[0], ((1,), (0,))).astype(BF16)

        pltpu.emit_pipeline(
            body,
            grid=(4, rows // TILE),
            in_specs=[
                pl.BlockSpec((TILE, acts.shape[1]), lambda n, i: (i, 0)),
                pl.BlockSpec((1, w2.shape[1], feats), lambda n, i: (n, 0, 0)),
            ],
            out_specs=[pl.BlockSpec((1, TILE, feats), lambda n, i: (n, i, 0))],
        )(acts, w2, out_part)

    def dx_stage():
        def body(grad_ref, first_ref, part_ref):
            norms = norm_all[pl.program_id(0)]
            one = product(grad_ref[:, :qkv_here], first_ref[0, :, :qkv_here], ((1,), (1,)))
            two = product(grad_ref[:, qkv_here:], first_ref[0, :, qkv_here:], ((1,), (1,)))
            part_ref[0] = (one * norms[0:1] + two * norms[2:3]).astype(BF16)

        pltpu.emit_pipeline(
            body,
            grid=(4, rows // TILE),
            in_specs=[
                pl.BlockSpec((TILE, grads.shape[1]), lambda n, i: (i, 0)),
                pl.BlockSpec((1, feats, w1.shape[2]), lambda n, i: (n, 0, 0)),
            ],
            out_specs=[pl.BlockSpec((1, TILE, feats), lambda n, i: (n, i, 0))],
        )(grads, w1, dx_part)

    class Scatter:
        def __init__(self, part, from_core, chip, from_x, half, from_y):
            self.part, self.from_core, self.chip = part, from_core, chip
            self.from_x, self.half, self.from_y = from_x, half, from_y
            self.to_core = [
                copies.make(
                    partial(lambda j: part.at[peer[j]], j),
                    partial(lambda j: from_core.at[peer[j] // 2], j),
                    to_row[1],
                )
                for j in (1, 3)
            ]
            self.to_x = copies.make(
                lambda: chip.at[:, far_half], lambda: from_x, to_col
            )
            self.to_y = copies.make(lambda: half.at[1 - y], lambda: from_y, to_row[2])

        def begin(self):
            for copy in self.to_core:
                start(copy)

        def second(self):
            for copy in self.to_core:
                copy().wait_recv()

            def body(left, right, target):
                target[...] = (left[...].astype(F32) + right[...].astype(F32)).astype(BF16)

            block = pl.BlockSpec((1, TILE, feats), lambda s, i: (s, i, 0))
            pltpu.emit_pipeline(
                body,
                grid=(2, rows // TILE),
                in_specs=[
                    pl.BlockSpec((1, TILE, feats), lambda s, i: (2 * s + core, i, 0)),
                    block,
                ],
                out_specs=[block],
            )(self.part, self.from_core, self.chip)
            start(self.to_x)

        def third(self):
            self.to_x().wait_recv()

            def body(left, right, target):
                target[...] = (left[...].astype(F32) + right[...].astype(F32)).astype(BF16)

            block = pl.BlockSpec((1, TILE, feats), lambda s, i: (s, i, 0))
            tiles = own_rows // TILE
            pltpu.emit_pipeline(
                body,
                grid=(2, tiles),
                in_specs=[
                    pl.BlockSpec((1, TILE, feats), lambda s, i: (s, c * tiles + i, 0)),
                    block,
                ],
                out_specs=[block],
            )(self.chip, self.from_x, self.half)
            start(self.to_y)

        def last(self, body, extra, target):
            self.to_y().wait_recv()
            flat = pl.BlockSpec((1, slab, feats), lambda i: (i, 0, 0))
            pltpu.emit_pipeline(
                body,
                grid=(own_rows // TILE,),
                in_specs=[
                    pl.BlockSpec((1, TILE, feats), lambda i: (y, i, 0)),
                    pl.BlockSpec((TILE, feats), lambda i: (i, 0)),
                    flat,
                ],
                out_specs=[flat],
            )(self.half, self.from_y, extra, target)

    out_scatter = Scatter(out_part, out_core, out_chip, out_x, out_half, out_y)
    dx_scatter = Scatter(dx_part, dx_core, dx_chip, dx_x, dx_half, dx_y)
    out_route = Route(
        out_item, 4, out_up, out_down, out_far, out_send, out_edge, output
    )

    def finish_output():
        def body(half_ref, y_ref, x_ref, item_ref):
            item_ref[0] = (
                half_ref[0].astype(F32)
                + y_ref[...].astype(F32)
                + x_ref[0].astype(F32)
                + out_bias[0:1]
            ).astype(BF16)

        out_scatter.last(body, x_own, out_item)

    def finish_grad():
        def body(half_ref, y_ref, x_ref, target_ref):
            target_ref[0] = half_ref[0].astype(F32) + y_ref[...].astype(F32)

        dx_scatter.last(body, x_own, grad_norm)

    x_gather.begin()
    cot_route.begin()
    norm_all[r] = norm_own[...]
    for copy in norm_copies:
        start(copy)
    x_gather.after_y()
    mlp_fetch[0].begin()
    cot_route.relay()
    x_gather.after_x()
    cot_route.hand_out()
    cot_route.take()
    cot_gather = Gather(cot_own, cot_all)
    cot_gather.begin()
    mlp_fetch[1].begin()
    x_gather.end()
    for copy in norm_copies:
        copy().wait_recv()
    norm_stage()
    cot_gather.after_y()
    attn_fetch.begin()
    cot_gather.after_x()
    cot_gather.end()
    mlp_fetch[0].end()
    mlp_stage(0)
    for unit in mlp_units[0]:
        unit.send()
    mlp_fetch[1].end()
    mlp_stage(1)
    for unit in mlp_units[0]:
        unit.collect()
    for unit in mlp_units[1]:
        unit.send()
    mlp_fetch[2].begin()
    mlp_fetch[3].begin()
    mlp_units[0][0].halve()
    attn_fetch.end()
    attention_stage()
    for unit in mlp_units[1]:
        unit.collect()
    for unit in attn_units:
        unit.send()
    mlp_units[0][1].halve()
    mlp_units[0][0].close()
    mlp_units[1][0].halve()
    mlp_units[0][1].close()
    mlp_fetch[2].end()
    mlp_stage(2)
    for unit in attn_units:
        unit.collect()
    for unit in mlp_units[2]:
        unit.send()
    mlp_units[1][1].halve()
    mlp_units[1][0].close()
    mlp_fetch[3].end()
    mlp_stage(3)
    for unit in mlp_units[2]:
        unit.collect()
    for unit in mlp_units[3]:
        unit.send()
    attn_units[0].halve()
    mlp_units[1][1].close()
    out_stage()
    out_scatter.begin()
    dx_stage()
    for unit in mlp_units[3]:
        unit.collect()
    attn_units[1].halve()
    attn_units[0].close()
    out_scatter.second()
    dx_scatter.begin()
    attn_units[2].halve()
    attn_units[1].close()
    out_scatter.third()
    dx_scatter.second()
    attn_units[3].halve()
    attn_units[2].close()
    finish_output()
    out_route.begin()
    dx_scatter.third()
    mlp_units[2][0].halve()
    attn_units[3].close()
    out_route.relay()
    finish_grad()
    mlp_units[2][1].halve()
    mlp_units[2][0].close()
    out_route.hand_out()
    mlp_units[3][0].halve()
    mlp_units[2][1].close()
    out_route.take()
    mlp_units[3][1].halve()
    mlp_units[3][0].close()
    gain_q[...] = gain_acc[0]
    bias_q[...] = gain_acc[1]
    gain_f[...] = gain_acc[2]
    bias_f[...] = gain_acc[3]
    mlp_units[3][1].close()
    for unit in sum(mlp_units, []) + attn_units:
        unit.finish()
    cot_route.finish()
    out_route.finish()
    for copy in sent:
        copy().wait_send()


def line_codes(sources, plane):
    middle = (plane == 1) | (plane == 2)
    own = sources[:, 0] * 0

    def code(wanted):
        up, down = plane - 1, plane + 1
        coded = jnp.where(wanted == up, 1, jnp.where(wanted == down, 2, 3))
        coded = jnp.where(middle, coded, 1)
        return jnp.where(wanted == plane, own, coded)

    take = lax.dynamic_index_in_dim(sources, plane, 1, keepdims=False)
    hand = jnp.where(plane == 1, sources[:, 0], sources[:, 3])
    return jnp.concatenate([code(take), code(hand)]).astype(jnp.int32)


def dealt_layer(
    layer_input,
    lengths,
    deal_table,
    ln1_gain,
    ln1_bias,
    qkv_weight,
    qkv_bias,
    dense_weight,
    dense_bias,
    ln2_gain,
    ln2_bias,
    fc1_weight,
    fc1_bias,
    fc2_weight,
    fc2_bias,
    cotangent,
):
    plane = lax.axis_index("dp")
    row = lax.axis_index("row")
    col = lax.axis_index("col")
    own_rows, feats = layer_input.shape
    rows = 2 * own_rows
    slab = own_rows // 2
    qkv_cols = qkv_weight.shape[1]
    qkv_here = qkv_cols // 4
    attn_here = dense_weight.shape[0] // 4
    hidden_cols = fc1_weight.shape[1]
    hidden_here = hidden_cols // 4
    first_cols = qkv_here + hidden_here
    second_rows = attn_here + hidden_here

    deal_here = lax.dynamic_slice_in_dim(deal_table, 2 * col, 2, 0)
    undeal_here = jnp.argmax(
        deal_here[:, None, :] == jnp.arange(4, dtype=jnp.int32)[None, :, None], axis=2
    ).astype(jnp.int32)
    codes = jnp.concatenate([line_codes(undeal_here, plane), line_codes(deal_here, plane)])
    lengths_here = lax.dynamic_slice_in_dim(lengths, plane * 4, 4, 0)
    positions = jnp.concatenate([segment_layout(lengths_here[s], slab)[1] for s in range(4)])
    begins = jnp.tile(jnp.arange(slab, dtype=jnp.int32), 4) - positions
    cos_table, sin_table = rotary_tables(positions)
    lane = jnp.arange(HD)
    cos_table = jnp.pad(cos_table, ((0, 0), (0, HD - ROT)), constant_values=1.0)
    sin_table = jnp.pad(sin_table, ((0, 0), (0, HD - ROT)))
    low_table = jnp.where(lane < ROT // 2, -sin_table, 0.0)
    high_table = jnp.where(lane < ROT // 2, 0.0, sin_table)
    begins = jnp.broadcast_to(begins[:, None], (rows, HD))
    norms = jnp.stack([ln1_gain, ln1_bias, ln2_gain, ln2_bias])
    norms = jnp.concatenate([norms, norms])
    bias_here = jnp.concatenate(
        [
            lax.dynamic_slice_in_dim(qkv_bias, row * qkv_here, qkv_here, 0),
            lax.dynamic_slice_in_dim(fc1_bias, row * hidden_here, hidden_here, 0),
        ]
    )
    bias_here = jnp.broadcast_to(bias_here[None], (8, first_cols))
    out_bias = jnp.broadcast_to((dense_bias + fc2_bias)[None], (8, feats))

    low = lambda *shape: jax.ShapeDtypeStruct(shape, BF16)
    wide = lambda *shape: jax.ShapeDtypeStruct(shape, F32)
    first = low(4, feats, first_cols)
    second = low(4, second_rows, feats)
    item = low(2, slab, feats)
    outputs = [first, second, item, wide(2, slab, feats), item, wide(rows, 128)]
    in_vmem = [wide(D, 128)] * 4 + [wide(8, first_cols)]
    scatter = [
        low(4, rows, feats),
        low(2, rows, feats),
        low(2, rows, feats),
        low(2, own_rows, feats),
        low(2, own_rows, feats),
        low(own_rows, feats),
    ]
    buffers = (
        [low(4, 4, slab, feats)] * 2
        + [low(rows, D)] * 2
        + [first, second, low(rows, second_rows), low(rows, first_cols)]
        + [first, second] * 5
        + scatter
        + [item]
        + scatter
        + [item] * 10
    )
    any_space = pl.BlockSpec(memory_space=pl.ANY)
    vmem = pl.BlockSpec(memory_space=pltpu.VMEM)
    copies = 150
    results = pl.pallas_call(
        layer_kernel,
        in_specs=[pl.BlockSpec(memory_space=pltpu.SMEM)]
        + [any_space] * 2
        + [vmem] * 3
        + [any_space] * 8,
        out_specs=[any_space] * len(outputs)
        + [vmem] * len(in_vmem)
        + [any_space] * len(buffers),
        out_shape=outputs + in_vmem + buffers,
        scratch_shapes=[
            pltpu.VMEM((4, UNIT + qkv_here, feats), F32),
            pltpu.VMEM((4, 8, feats), F32),
            pltpu.VMEM((4, D, 128), F32),
            pltpu.VMEM((8, qkv_here), F32),
            pltpu.SemaphoreType.DMA((copies,)),
            pltpu.SemaphoreType.DMA((copies,)),
            pltpu.SemaphoreType.DMA((32,)),
        ],
        compiler_params=pltpu.CompilerParams(
            collective_id=0, has_side_effects=True, vmem_limit_bytes=60 * 1024 * 1024
        ),
        cost_estimate=pl.CostEstimate(
            flops=6 * rows * D * (first_cols + second_rows),
            bytes_accessed=200 * 1024 * 1024,
            transcendentals=rows * hidden_here,
        ),
    )(
        codes,
        layer_input.reshape(2, slab, feats),
        cotangent.reshape(2, slab, feats),
        norms,
        bias_here,
        out_bias,
        qkv_weight,
        dense_weight,
        fc1_weight,
        fc2_weight,
        cos_table,
        low_table,
        high_table,
        begins,
    )
    first_sum, second_sum, output, grad_norm, cot_own, stats = results[:6]
    gain1, bias1, gain2, bias2 = [jnp.sum(part, axis=1) for part in results[6:10]]
    unit_sums = results[10][0]
    output = output.reshape(own_rows, feats)

    def first_grad(part):
        return part.transpose(1, 0, 2).reshape(feats, -1).astype(F32)

    def second_grad(part):
        return part.reshape(-1, feats).astype(F32)

    qkv_grad = first_grad(first_sum[:, :, :qkv_here])
    fc1_grad = first_grad(first_sum[:, :, qkv_here:])
    dense_grad = second_grad(second_sum[:, :attn_here])
    fc2_grad = second_grad(second_sum[:, attn_here:])

    stats_own = lax.dynamic_slice_in_dim(stats, col * own_rows, own_rows, 0)
    mean, inv_std = stats_own[:, :1], stats_own[:, 127:]
    normed_own = (layer_input.astype(F32) - mean) * inv_std
    grad_normed = grad_norm.reshape(own_rows, feats)
    row_sums = lax.psum(
        (jnp.sum(grad_normed, axis=1), jnp.sum(grad_normed * normed_own, axis=1)), "row"
    )
    input_grad = cot_own.reshape(own_rows, feats).astype(F32) + inv_std * (
        grad_normed - row_sums[0][:, None] / D - normed_own * row_sums[1][:, None] / D
    )

    norm_sums = jnp.stack([gain1, bias1, gain2, bias2])
    bias_part = jnp.sum(cotangent, axis=0, dtype=F32)
    bias_sum = jnp.zeros((4, feats), F32).at[row].set(bias_part)
    qkv_sums = jnp.zeros((2, 4, qkv_here), F32).at[col, row].set(unit_sums[:qkv_here])
    hidden_sums = jnp.zeros((2, 4, hidden_here), F32).at[col, row].set(unit_sums[qkv_here:])
    small = lax.psum(
        jnp.concatenate(
            [
                norm_sums.reshape(-1),
                bias_sum.reshape(-1),
                qkv_sums.reshape(-1),
                hidden_sums.reshape(-1),
            ]
        ),
        ("dp", "row", "col"),
    )
    norm_sums, bias_sum, qkv_sums, hidden_sums = jnp.split(
        small, [4 * D, 5 * D, 5 * D + 2 * qkv_cols]
    )
    norm_sums = lax.dynamic_index_in_dim(norm_sums.reshape(4, 4, feats), row, 1, keepdims=False)
    bias_sum = lax.dynamic_index_in_dim(bias_sum.reshape(4, feats), row, 0, keepdims=False)
    qkv_bias_grad = lax.dynamic_index_in_dim(qkv_sums.reshape(2, qkv_cols), col, 0, keepdims=False)
    fc1_bias_grad = lax.dynamic_index_in_dim(
        hidden_sums.reshape(2, hidden_cols), col, 0, keepdims=False
    )
    gain1 = (norm_sums[0] - ln1_bias * norm_sums[1]) / ln1_gain
    gain2 = (norm_sums[2] - ln2_bias * norm_sums[3]) / ln2_gain
    return (
        output,
        input_grad,
        gain1,
        norm_sums[1],
        qkv_grad,
        qkv_bias_grad,
        dense_grad,
        bias_sum,
        gain2,
        norm_sums[3],
        fc1_grad,
        fc1_bias_grad,
        fc2_grad,
        bias_sum,
    )


def solution(mesh):
    grid = tuple(mesh.shape[axis] for axis in ("dp", "row", "col"))
    placed = (
        P(("dp", "col"), "row"),
        P(),
        P(),
        P("row"),
        P("row"),
        P("row", "col"),
        P("col"),
        P("col", "row"),
        P("row"),
        P("row"),
        P("row"),
        P("row", "col"),
        P("col"),
        P("col", "row"),
        P("row"),
        P(("dp", "col"), "row"),
    )
    return jax.shard_map(
        dealt_layer if grid == (4, 4, 2) else local,
        mesh=mesh,
        in_specs=placed,
        out_specs=(
            P(("dp", "col"), "row"),
            P(("dp", "col"), "row"),
            P("row"),
            P("row"),
            P("row", "col"),
            P("col"),
            P("col", "row"),
            P("row"),
            P("row"),
            P("row"),
            P("row", "col"),
            P("col"),
            P("col", "row"),
            P("row"),
        ),
        check_vma=False,
    )
```

```python
from functools import partial
import math

import jax
import jax.numpy as jnp
import numpy as np
from jax import lax
from jax.experimental import pallas as pl
from jax.experimental.pallas import tpu as pltpu
from jax.sharding import PartitionSpec as P

D = 2048
HD = 128
ROT = 32
QBLK = 512
CHUNK = 256
BF16 = jnp.bfloat16
F32 = jnp.float32


norm_epsilon = 1e-05
masked_score = -1000000000.0


def rotary_tables(positions):
    frequency = 1.0 / 10000.0 ** (jnp.arange(0, ROT, 2, dtype=jnp.float32) / ROT)
    angles = positions.astype(jnp.float32)[:, None] * frequency[None, :]
    angles = jnp.concatenate([angles, angles], axis=1)
    return (jnp.cos(angles), jnp.sin(angles))


def rotate(values, cos_table, sin_table):
    half_rot = ROT // 2
    rotated = values[..., :ROT]
    turned = jnp.concatenate([-rotated[..., half_rot:], rotated[..., :half_rot]], axis=-1)
    rotated = rotated * cos_table[:, None, :] + turned * sin_table[:, None, :]
    return jnp.concatenate([rotated, values[..., ROT:]], axis=-1)


def segment_layout(seq_lengths, length):
    seq_ends = jnp.cumsum(seq_lengths)
    token_place = jnp.arange(length, dtype=jnp.int32)
    sequence_ids = jnp.sum((token_place[:, None] >= seq_ends[None, :]).astype(jnp.int32), axis=1)
    starts = seq_ends - seq_lengths
    seq_hits = sequence_ids[:, None] == jnp.arange(seq_lengths.shape[0], dtype=jnp.int32)[None, :]
    seq_begin = jnp.sum(jnp.where(seq_hits, starts[None, :], 0), axis=1)
    return (sequence_ids, token_place - seq_begin)


def contract_rows(left_side, right_side):
    return lax.dot_general(
        left_side, right_side, (((0,), (0,)), ((), ())), preferred_element_type=jnp.float32
    )


def contract_cols(left_side, right_side):
    return lax.dot_general(
        left_side, right_side, (((1,), (1,)), ((), ())), preferred_element_type=jnp.float32
    )


def pick_rows(pooled, chosen):
    row_hits = chosen[None, :] == jnp.arange(pooled.shape[0], dtype=jnp.int32)[:, None]
    return jnp.sum(jnp.where(row_hits[:, :, None], pooled.astype(jnp.float32), 0.0), axis=0)


def local(
    layer_input,
    lengths,
    deal_table,
    ln1_gain,
    ln1_bias,
    qkv_weight,
    qkv_bias,
    dense_weight,
    dense_bias,
    ln2_gain,
    ln2_bias,
    fc1_weight,
    fc1_bias,
    fc2_weight,
    fc2_bias,
    cotangent,
):
    dp_count = lax.axis_size("dp")
    row_count = lax.axis_size("row")
    col_count = lax.axis_size("col")
    group_id = lax.axis_index("dp")
    row_id = lax.axis_index("row")
    col_id = lax.axis_index("col")
    own_rows, own_feats = layer_input.shape
    group_rows = own_rows * col_count
    slab_rows = group_rows // row_count
    qkv_cols = qkv_weight.shape[1]
    attn_cols = dense_weight.shape[0]
    heads_here = qkv_cols // (3 * HD)
    score_scale = 1.0 / math.sqrt(HD)
    local_slab = (col_id * own_rows + jnp.arange(own_rows, dtype=jnp.int32)) // slab_rows
    slab_hits = local_slab[:, None] == jnp.arange(row_count, dtype=jnp.int32)[None, :]
    deal_here = lax.dynamic_index_in_dim(deal_table, group_id, 1, keepdims=False)
    source = jnp.sum(jnp.where(slab_hits, deal_here[None, :], 0), axis=1)
    pooled = lax.all_gather(layer_input, "dp", axis=0, tiled=True).reshape(
        dp_count, own_rows, own_feats
    )
    mine_rows = pick_rows(pooled, source).astype(jnp.bfloat16)
    input_all = lax.all_gather(mine_rows, "col", axis=0, tiled=True)
    input_wide = input_all.astype(jnp.float32)
    row_stats = lax.psum(
        (jnp.sum(input_wide, axis=1), jnp.sum(input_wide * input_wide, axis=1)), "row"
    )
    row_mean = row_stats[0] / D
    inv_std = lax.rsqrt(row_stats[1] / D - row_mean * row_mean + norm_epsilon)
    normed = (input_wide - row_mean[:, None]) * inv_std[:, None]
    own_start = col_id * own_rows
    normed_own = lax.dynamic_slice_in_dim(normed, own_start, own_rows, 0)
    inv_std_own = lax.dynamic_slice_in_dim(inv_std, own_start, own_rows, 0)
    ln1_all = (normed * ln1_gain + ln1_bias).astype(jnp.bfloat16)
    ln2_all = (normed * ln2_gain + ln2_bias).astype(jnp.bfloat16)
    part_one = ln1_all
    part_two = ln2_all
    first_sums = lax.psum_scatter(
        jnp.concatenate(
            [
                jnp.dot(part_one, qkv_weight, preferred_element_type=jnp.float32),
                jnp.dot(part_two, fc1_weight, preferred_element_type=jnp.float32),
            ],
            axis=1,
        ),
        "row",
        scatter_dimension=0,
        tiled=True,
    )
    qkv_out = first_sums[:, :qkv_cols] + qkv_bias
    hidden = first_sums[:, qkv_cols:] + fc1_bias
    slab_source = (
        lax.dynamic_index_in_dim(deal_here, row_id, 0, keepdims=False) * row_count + row_id
    )
    seq_lengths = lax.dynamic_index_in_dim(lengths, slab_source, 0, keepdims=False)
    sequence_ids, positions = segment_layout(seq_lengths, slab_rows)
    token_place = jnp.arange(slab_rows, dtype=jnp.int32)
    cos_table, sin_table = rotary_tables(positions)
    packed = qkv_out.reshape(slab_rows, heads_here, 3, HD)
    query_pre = packed[:, :, 0]
    key_pre = packed[:, :, 1]
    queries = rotate(query_pre, cos_table, sin_table).astype(jnp.bfloat16)
    keys_rot = rotate(key_pre, cos_table, sin_table).astype(jnp.bfloat16)
    values = packed[:, :, 2].astype(jnp.bfloat16)

    def block_scores(block_id):
        first_row = block_id * QBLK
        last_row = first_row + QBLK
        allowed = (sequence_ids[first_row:last_row, None] == sequence_ids[None, :last_row]) & (
            token_place[None, :last_row] <= token_place[first_row:last_row, None]
        )
        scores = (
            jnp.einsum("qhd,khd->hqk", queries, keys_rot, preferred_element_type=jnp.float32)
            * score_scale
        )
        return jnp.where(allowed[None], scores, masked_score)

    block_id = 0
    last_row = (block_id + 1) * QBLK
    scores = block_scores(block_id)
    row_top = jnp.max(scores, axis=-1, keepdims=True)
    exp_total = jnp.sum(jnp.exp(scores - row_top), axis=-1, keepdims=True)
    log_total = row_top + jnp.log(exp_total)
    probs_low = jnp.exp(scores - log_total).astype(jnp.bfloat16)
    mixtures = jnp.einsum("hqk,khd->qhd", probs_low, values, preferred_element_type=jnp.float32)
    log_totals = [log_total]
    attn_out = mixtures.reshape(slab_rows, attn_cols).astype(jnp.bfloat16)
    activated = jax.nn.gelu(hidden, approximate=False).astype(jnp.bfloat16)
    attn_all, act_all = (
        lax.all_gather(attn_out, "row", axis=0, tiled=True),
        lax.all_gather(activated, "row", axis=0, tiled=True),
    )
    part_one = attn_all
    part_two = act_all
    branch_sum = lax.psum_scatter(
        jnp.dot(part_one, dense_weight, preferred_element_type=jnp.float32)
        + jnp.dot(part_two, fc2_weight, preferred_element_type=jnp.float32),
        "col",
        scatter_dimension=0,
        tiled=True,
    )
    output = (mine_rows.astype(jnp.float32) + branch_sum + dense_bias + fc2_bias).astype(
        jnp.bfloat16
    )
    grad_all = lax.all_gather(cotangent, "col", axis=0, tiled=True)
    dense_grad = contract_rows(attn_all, grad_all)
    fc2_grad = contract_rows(act_all, grad_all)
    out_bias_grad = jnp.sum(grad_all, axis=0, dtype=jnp.float32)
    grad_block = grad_all
    grad_second = lax.psum_scatter(
        jnp.concatenate(
            [contract_cols(grad_block, dense_weight), contract_cols(grad_block, fc2_weight)], axis=1
        ),
        "row",
        scatter_dimension=0,
        tiled=True,
    )
    grad_mix = grad_second[:, :attn_cols].astype(jnp.bfloat16).reshape(slab_rows, heads_here, HD)
    gelu_back = jax.vjp(partial(jax.nn.gelu, approximate=False), hidden)[1]
    grad_hidden = gelu_back(grad_second[:, attn_cols:])[0]
    grad_key = jnp.zeros((slab_rows, heads_here, HD), jnp.float32)
    grad_value = jnp.zeros((slab_rows, heads_here, HD), jnp.float32)
    block_id = 0
    first_row = block_id * QBLK
    last_row = first_row + QBLK
    probs_full = jnp.exp(block_scores(block_id) - log_totals[block_id])
    probs_low = probs_full.astype(jnp.bfloat16)
    grad_block = grad_mix
    grad_value = grad_value.at[:last_row].add(
        jnp.einsum("hqk,qhd->khd", probs_low, grad_block, preferred_element_type=jnp.float32)
    )
    grad_probs = jnp.einsum("qhd,khd->hqk", grad_block, values, preferred_element_type=jnp.float32)
    centre = jnp.sum(probs_full * grad_probs, axis=-1, keepdims=True)
    grad_scores = (probs_full * (grad_probs - centre)).astype(jnp.bfloat16)
    grad_queries = (
        jnp.einsum("hqk,khd->qhd", grad_scores, keys_rot, preferred_element_type=jnp.float32)
        * score_scale
    )
    grad_key = grad_key.at[:last_row].add(
        jnp.einsum("hqk,qhd->khd", grad_scores, queries, preferred_element_type=jnp.float32)
        * score_scale
    )
    turn_back = jax.vjp(lambda values_in: rotate(values_in, cos_table, sin_table), query_pre)[1]
    grad_query_pre = turn_back(grad_queries)[0]
    grad_key_pre = turn_back(grad_key)[0]
    grad_qkv = jnp.stack([grad_query_pre, grad_key_pre, grad_value], axis=2).reshape(
        slab_rows, qkv_cols
    )
    grad_first = jnp.concatenate([grad_qkv, grad_hidden], axis=1).astype(jnp.bfloat16)
    grad_first_all = lax.all_gather(grad_first, "row", axis=0, tiled=True)
    grad_qkv_all = grad_first_all[:, :qkv_cols]
    grad_hidden_all = grad_first_all[:, qkv_cols:]
    qkv_weight_grad = contract_rows(ln1_all, grad_qkv_all)
    qkv_bias_grad = jnp.sum(grad_qkv_all, axis=0, dtype=jnp.float32)
    fc1_weight_grad = contract_rows(ln2_all, grad_hidden_all)
    fc1_bias_grad = jnp.sum(grad_hidden_all, axis=0, dtype=jnp.float32)
    grad_block = grad_first_all
    summed = lax.psum_scatter(
        jnp.concatenate(
            [
                contract_cols(grad_block[:, :qkv_cols], qkv_weight),
                contract_cols(grad_block[:, qkv_cols:], fc1_weight),
            ],
            axis=1,
        ),
        "col",
        scatter_dimension=0,
        tiled=True,
    )
    grad_ln_one = summed[:, :own_feats]
    grad_ln_two = summed[:, own_feats:]
    gain_terms = (
        jnp.sum(grad_ln_one * normed_own, axis=0),
        jnp.sum(grad_ln_one, axis=0),
        jnp.sum(grad_ln_two * normed_own, axis=0),
        jnp.sum(grad_ln_two, axis=0),
    )
    grad_normed = grad_ln_one * ln1_gain + grad_ln_two * ln2_gain
    row_sums = lax.psum(
        (jnp.sum(grad_normed, axis=1), jnp.sum(grad_normed * normed_own, axis=1)), "row"
    )
    grad_dealt = cotangent.astype(jnp.float32) + inv_std_own[:, None] * (
        grad_normed - row_sums[0][:, None] / D - normed_own * row_sums[1][:, None] / D
    )
    gain_sums = lax.psum(
        (gain_terms[0], gain_terms[1], gain_terms[2], gain_terms[3]), ("dp", "col")
    )
    weights_summed = lax.psum(
        (
            qkv_weight_grad,
            qkv_bias_grad,
            dense_grad,
            fc1_weight_grad,
            fc1_bias_grad,
            fc2_grad,
            out_bias_grad,
        ),
        "dp",
    )
    pool_back = lax.all_gather(grad_dealt, "dp", axis=0, tiled=True).reshape(
        dp_count, own_rows, own_feats
    )
    back_here = jnp.sum(
        jnp.where(deal_table == group_id, jnp.arange(dp_count, dtype=jnp.int32)[None, :], 0), axis=1
    )
    target = jnp.sum(jnp.where(slab_hits, back_here[None, :], 0), axis=1)
    input_grad = pick_rows(pool_back, target)
    return (
        output,
        input_grad,
        gain_sums[0],
        gain_sums[1],
        weights_summed[0],
        weights_summed[1],
        weights_summed[2],
        weights_summed[6],
        gain_sums[2],
        gain_sums[3],
        weights_summed[3],
        weights_summed[4],
        weights_summed[5],
        weights_summed[6],
    )


UNIT = 256
TILE = 512


def product(left, right, dims):
    return lax.dot_general(left, right, (dims, ((), ())), preferred_element_type=F32)


def fold_lanes(values):
    total = values[:, :128]
    for at in range(128, values.shape[1], 128):
        total = total + values[:, at : at + 128]
    return total


class Copies:
    def __init__(self, send_sems, recv_sems):
        self.send_sems, self.recv_sems, self.used = send_sems, recv_sems, 0

    def make(self, source, target, device):
        number = self.used
        self.used += 1

        def build():
            return pltpu.make_async_remote_copy(
                src_ref=source(),
                dst_ref=target(),
                send_sem=self.send_sems.at[number],
                recv_sem=self.recv_sems.at[number],
                device_id=device,
                device_id_type=pl.DeviceIdType.MESH,
            )

        return build


def attention_head(qkv, back, cos, low, high, allowed):
    scale = 1.0 / math.sqrt(HD)

    def turn(values):
        return values * cos + pltpu.roll(values, HD - 16, 1) * low + pltpu.roll(values, 16, 1) * high

    def turn_back(values):
        return (
            values * cos
            + pltpu.roll(values * high, HD - 16, 1)
            + pltpu.roll(values * low, 16, 1)
        )

    query = turn(qkv[:, :HD]).astype(BF16)
    key = turn(qkv[:, HD : 2 * HD]).astype(BF16)
    value = qkv[:, 2 * HD :].astype(BF16)
    scores = product(query, key, ((1,), (1,))) * scale
    scores = jnp.where(allowed, scores, masked_score)
    weight = jnp.exp(scores - jnp.max(scores, axis=1, keepdims=True))
    probs = weight * (1.0 / jnp.sum(weight, axis=1, keepdims=True))
    probs_low = probs.astype(BF16)
    attn = product(probs_low, value, ((1,), (0,))).astype(BF16)
    grad_probs = product(back, value, ((1,), (1,)))
    centre = jnp.sum(probs * grad_probs, axis=1, keepdims=True)
    grad_scores = (probs * (grad_probs - centre)).astype(BF16)
    grad_query = product(grad_scores, key, ((1,), (0,))) * scale
    grad_key = product(grad_scores, query, ((0,), (0,))) * scale
    grad_value = product(probs_low, back, ((0,), (0,)))
    return attn, [turn_back(grad_query), turn_back(grad_key), grad_value]


def layer_kernel(
    lengths,
    deal_table,
    x_own,
    cot_in,
    norm_own,
    qkv_bias,
    fc1_bias,
    out_bias,
    turns,
    qkv_w,
    dense_w,
    fc1_w,
    fc2_w,
    first_sum,
    second_sum,
    output,
    input_grad,
    small_sum,
    grad_norm,
    cot_own,
    stats,
    x_all,
    cot_all,
    ln1,
    ln2,
    w1,
    w2,
    acts,
    grads,
    first_part,
    second_part,
    first_here,
    second_here,
    first_in,
    second_in,
    first_half,
    second_half,
    first_other,
    second_other,
    out_part,
    out_core,
    out_chip,
    out_x,
    out_half,
    out_y,
    out_item,
    dx_part,
    dx_core,
    dx_chip,
    dx_x,
    dx_half,
    dx_y,
    cot_up,
    cot_down,
    cot_far,
    cot_send,
    cot_edge,
    out_up,
    out_down,
    out_far,
    out_send,
    out_edge,
    acc,
    norm_all,
    gain_acc,
    sum_acc,
    unit_sums,
    small_part,
    small_row,
    small_units,
    small_col,
    small_here,
    small_in,
    small_half,
    small_other,
    row_part,
    row_sums,
    send_sems,
    recv_sems,
    local_sems,
):
    z, r, c = lax.axis_index("dp"), lax.axis_index("row"), lax.axis_index("col")
    y, core = r // 2, r % 2
    mid = ((z + 1) // 2) % 2
    upper = z // 2
    z_in = mid * (3 - z) + (1 - mid) * (1 + upper)
    z_out = 3 * upper
    is_mid, is_edge = mid == 1, mid == 0
    peer = [r, 2 * y + (1 - core), 2 * (1 - y) + core, 2 * (1 - y) + (1 - core)]
    slabs, slab, feats = x_own.shape
    own_rows = slabs * slab
    rows = 2 * own_rows
    hidden_here = fc1_w.shape[1] // 4
    qkv_here = qkv_w.shape[1] // 4
    attn_here = dense_w.shape[0] // 4
    to_row = [{"row": peer[j]} for j in range(4)]
    to_col = {"col": 1 - c}
    to_in = {"dp": z_in}
    to_out = {"dp": z_out}
    copies = Copies(send_sems, recv_sems)
    sent = []

    barrier = pltpu.get_barrier_semaphore()

    def greet(device):
        pl.semaphore_signal(barrier, inc=1, device_id=device, device_id_type=pl.DeviceIdType.MESH)

    for j in (1, 2, 3):
        greet(to_row[j])
    greet(to_col)
    greet(to_in)

    @pl.when(is_mid)
    def _():
        greet(to_out)
        pl.semaphore_wait(barrier, 6)

    @pl.when(is_edge)
    def _():
        pl.semaphore_wait(barrier, 5)

    def start(copy):
        copy().start()
        sent.append(copy)

    def when(flag, action):
        pl.when(flag)(action)

    local_used = [0]

    def local(source, target):
        number = local_used[0]
        local_used[0] += 1

        def build():
            return pltpu.make_async_copy(source(), target(), local_sems.at[number])

        build().start()
        return build

    own_half = pl.ds(c * own_rows, own_rows)
    far_half = pl.ds((1 - c) * own_rows, own_rows)

    class Gather:
        def __init__(self, own, whole, by_row):
            self.own, self.whole = own, whole

            def place(j, half, q):
                return lambda: whole.at[peer[j], slabs * half + q]

            def own_slab(q):
                return lambda: own.at[q]

            ids = range(slabs)
            self.to_y = [copies.make(own_slab(q), place(0, c, q), to_row[2]) for q in ids]
            self.to_x = [copies.make(own_slab(q), place(0, c, q), to_col) for q in ids]
            self.to_core = [copies.make(own_slab(q), place(0, c, q), to_row[1]) for q in ids]
            self.y_core = [copies.make(place(2, c, q), place(2, c, q), to_row[1]) for q in ids]
            self.x_core = [
                copies.make(place(0, 1 - c, q), place(0, 1 - c, q), to_row[1]) for q in ids
            ]
            self.far_core = [
                copies.make(place(2, 1 - c, q), place(2, 1 - c, q), to_row[1]) for q in ids
            ]
            self.by_row = by_row
            self.far = [
                copies.make(place(0, 1 - c, q), place(0, 1 - c, q), to_row[2])
                if q in by_row
                else copies.make(place(2, c, q), place(2, c, q), to_col)
                for q in ids
            ]
            self.kept = [None] * slabs

        def begin(self, q):
            start(self.to_y[q])
            start(self.to_x[q])
            start(self.to_core[q])
            self.kept[q] = local(
                lambda: self.own.at[q], lambda: self.whole.at[r, slabs * c + q]
            )

        def after_y(self, q):
            self.to_y[q]().wait_recv()
            if q not in self.by_row:
                start(self.far[q])
            start(self.y_core[q])

        def after_x(self, q):
            self.to_x[q]().wait_recv()
            if q in self.by_row:
                start(self.far[q])
            start(self.x_core[q])

        def after_far(self, q):
            self.far[q]().wait_recv()
            start(self.far_core[q])

        def end(self, q):
            self.kept[q]().wait()
            for group in (self.to_core, self.y_core, self.x_core, self.far_core):
                group[q]().wait_recv()

    def choose(q, goes, plane, refs, target):
        def body(*blocks):
            value = blocks[0][...]
            for (source, _), block in zip(refs[1:], blocks[1:]):
                value = jnp.where(goes(q, source, plane), block[...], value)
            blocks[-1][...] = value

        tile = slab // 4
        block = pl.BlockSpec((tile, feats), lambda i: (i, 0))
        pltpu.emit_pipeline(
            body, grid=(4,), in_specs=[block] * len(refs), out_specs=[block]
        )(*[ref.at[q] for _, ref in refs], target.at[q])

    class Route:
        def __init__(self, item, goes, up, down, far, send, edge, target):
            self.item, self.goes, self.up, self.down = item, goes, up, down
            self.far, self.send, self.edge, self.target = far, send, edge, target

            def at(ref, q):
                return lambda: ref.at[q]

            ids = range(slabs)
            self.upward = [copies.make(at(item, q), at(up, q), {"dp": z + 1}) for q in ids]
            self.downward = [copies.make(at(item, q), at(down, q), {"dp": z - 1}) for q in ids]
            self.far_up = [copies.make(at(up, q), at(far, q), to_in) for q in ids]
            self.far_down = [copies.make(at(down, q), at(far, q), to_in) for q in ids]
            self.outward = [copies.make(at(send, q), at(edge, q), to_out) for q in ids]

        def begin(self, q):
            when(z < 2, lambda: self.upward[q]().start())
            when(z > 1, lambda: self.downward[q]().start())

        def relay(self, q):
            def from_below():
                self.upward[q]().wait_recv()
                self.far_up[q]().start()

            def from_above():
                self.downward[q]().wait_recv()
                self.far_down[q]().start()

            when(z == 1, from_below)
            when(z == 2, from_above)

        def hand_out(self, q):
            def middle():
                def below():
                    self.downward[q]().wait_recv()
                    self.far_down[q]().wait_recv()

                def above():
                    self.upward[q]().wait_recv()
                    self.far_up[q]().wait_recv()

                when(z == 1, below)
                when(z == 2, above)
                refs = [
                    (z, self.item),
                    (z - 1, self.up),
                    (z + 1, self.down),
                    (3 * (2 - z), self.far),
                ]
                choose(q, self.goes, z_out, refs, self.send)
                self.outward[q]().start()
                choose(q, self.goes, z, refs, self.target)

            when(is_mid, middle)

        def take(self, q):
            def edge():
                self.outward[q]().wait_recv()
                block = pl.BlockSpec((slab // 4, feats), lambda i: (i, 0))

                def body(edge_ref, item_ref, target_ref):
                    mine = self.goes(q, z, z)
                    target_ref[...] = jnp.where(mine, item_ref[...], edge_ref[...])

                pltpu.emit_pipeline(
                    body, grid=(4,), in_specs=[block] * 2, out_specs=[block]
                )(self.edge.at[q], self.item.at[q], self.target.at[q])

            when(is_edge, edge)

        def finish(self):
            for q in range(slabs):
                when(z < 2, lambda: self.upward[q]().wait_send())
                when(z > 1, lambda: self.downward[q]().wait_send())
                when(z == 1, lambda: self.far_up[q]().wait_send())
                when(z == 2, lambda: self.far_down[q]().wait_send())
                when(is_mid, lambda: self.outward[q]().wait_send())

    def undealt(q, source, plane):
        return deal_table[slabs * c + q, source] == plane

    def dealt(q, source, plane):
        return deal_table[slabs * c + q, plane] == source

    x_gather = Gather(x_own, x_all, ())
    cot_gather = Gather(cot_own, cot_all, (1,))
    cot_route = Route(
        cot_in, undealt, cot_up, cot_down, cot_far, cot_send, cot_edge, cot_own
    )
    norm_copies = [
        copies.make(lambda: norm_own, lambda: norm_all.at[r], to_row[j]) for j in (1, 2, 3)
    ]

    class Fetch:
        def __init__(self, first, first_at, first_width, at, second, second_at, second_width, low):
            def first_source(j):
                lanes = pl.multiple_of(peer[j] * first_width + first_at, 256)
                size = UNIT if first is fc1_w else qkv_here
                return first.at[:, pl.ds(lanes, size)]

            def second_source(j):
                size = UNIT
                begin = pl.multiple_of(peer[j] * second_width + second_at, 256)
                return second.at[pl.ds(begin, size)]

            size = UNIT if first is fc1_w else qkv_here
            first_target = lambda: w1.at[r, :, pl.ds(at, size)]
            second_target = lambda: w2.at[r, pl.ds(low, UNIT)]
            self.remote = []
            for j in (1, 2, 3):
                self.remote.append(
                    copies.make(partial(first_source, j), first_target, to_row[j])
                )
                self.remote.append(
                    copies.make(partial(second_source, j), second_target, to_row[j])
                )
            self.kept = [(partial(first_source, 0), first_target), (partial(second_source, 0), second_target)]

        def begin(self):
            for copy in self.remote:
                start(copy)
            self.kept = [local(*pair) for pair in self.kept]

        def end(self):
            for copy in self.remote:
                copy().wait_recv()
            for copy in self.kept:
                copy().wait()

    attn_fetch = Fetch(qkv_w, 0, qkv_here, 0, dense_w, 0, attn_here, 0)
    mlp_fetch = [
        Fetch(fc1_w, at, hidden_here, qkv_here + at, fc2_w, at, hidden_here, attn_here + at)
        for at in range(0, hidden_here, UNIT)
    ]

    class Unit:
        def __init__(self, kind, at):
            self.kind, self.at = kind, at
            if kind == 1:
                self.view = lambda ref, s: ref.at[s, :, pl.ds(at, UNIT)]
                self.refs = (first_part, first_here, first_in, first_half, first_other, first_sum)
            else:
                self.view = lambda ref, s: ref.at[s, pl.ds(at, UNIT)]
                self.refs = (
                    second_part,
                    second_here,
                    second_in,
                    second_half,
                    second_other,
                    second_sum,
                )
            part, here, arrived, half, other, total = self.refs
            self.spread = [
                copies.make(
                    partial(lambda j: self.view(part, peer[j]), j),
                    lambda: self.view(here, r),
                    to_row[j],
                )
                for j in (1, 2, 3)
            ]
            def half_of(ref, which):
                first_slot = 2 * (y if which == 0 else 1 - y)
                if kind == 1:
                    return ref.at[pl.ds(first_slot, 2), :, pl.ds(at, UNIT)]
                return ref.at[pl.ds(first_slot, 2), pl.ds(at, UNIT)]

            def half_copy(source, target, which, device):
                return copies.make(
                    lambda: half_of(source, which), lambda: half_of(target, which), device
                )

            self.inward = [half_copy(here, arrived, which, to_in) for which in (0, 1)]
            self.across = [half_copy(half, other, which, to_in) for which in (0, 1)]
            self.outward = [half_copy(total, total, which, to_out) for which in (0, 1)]

        def send(self, which):
            part, here = self.refs[:2]
            if which == 0:
                start(self.spread[0])
                self.kept = local(lambda: self.view(part, r), lambda: self.view(here, r))
            else:
                self.spread[1]().start()
                self.spread[2]().start()

        def sent_far(self):
            self.spread[1]().wait_send()
            self.spread[2]().wait_send()

        def collect(self, which):
            if which == 0:
                self.spread[0]().wait_recv()
                self.kept().wait()
            else:
                self.spread[1]().wait_recv()
                self.spread[2]().wait_recv()

        def add(self, which, left, right, target):
            first_slot = 2 * (y if which == 0 else 1 - y)
            if self.kind == 1:
                block = pl.BlockSpec(
                    (1, feats, UNIT), lambda s: (first_slot + s, 0, self.at // UNIT)
                )
            else:
                block = pl.BlockSpec(
                    (1, UNIT, feats), lambda s: (first_slot + s, self.at // UNIT, 0)
                )

            def body(left_block, right_block, target_block):
                target_block[...] = (
                    left_block[...].astype(F32) + right_block[...].astype(F32)
                ).astype(BF16)

            pltpu.emit_pipeline(body, grid=(2,), in_specs=[block] * 2, out_specs=[block])(
                left, right, target
            )

        def halve(self, which):
            part, here, arrived, half, other, total = self.refs

            def middle():
                self.collect(which)
                self.inward[which]().wait_recv()
                self.add(which, here, arrived, half)
                self.across[which]().start()

            when(is_mid, middle)

        def close(self, which):
            part, here, arrived, half, other, total = self.refs

            def middle():
                self.across[which]().wait_recv()
                self.add(which, half, other, total)
                self.outward[which]().start()

            when(is_mid, middle)

        def finish(self, which, unsent):
            def edge():
                self.outward[which]().wait_recv()
                if unsent:
                    self.inward[which]().wait_send()

            def middle():
                self.across[which]().wait_send()
                self.outward[which]().wait_send()

            when(is_edge, edge)
            when(is_mid, middle)

    mlp_units = [
        [Unit(2, attn_here + at), Unit(1, qkv_here + at)] for at in range(0, hidden_here, UNIT)
    ]
    attn_units = [Unit(2, 0)] + [Unit(1, at) for at in range(0, qkv_here, UNIT)]

    def norm_body(x_ref, one_ref, two_ref, stat_ref):
        wide = jnp.concatenate([x_ref[j, 0] for j in range(4)], axis=1).astype(F32)
        norms = jnp.concatenate([norm_all[j] for j in range(4)], axis=1)
        mean = jnp.sum(wide, axis=1, keepdims=True) / D
        square = jnp.sum(wide * wide, axis=1, keepdims=True) / D
        inv_std = lax.rsqrt(square - mean * mean + norm_epsilon)
        normed = (wide - mean) * inv_std
        one_ref[...] = (normed * norms[0:1] + norms[1:2]).astype(BF16)
        two_ref[...] = (normed * norms[2:3] + norms[3:4]).astype(BF16)
        lane = lax.broadcasted_iota(jnp.int32, stat_ref.shape, 1)
        stat_ref[...] = jnp.where(lane < 64, mean, inv_std)

    def norm_stage():
        tile = 256
        flat = pl.BlockSpec((tile, D), lambda i: (i, 0))
        pltpu.emit_pipeline(
            norm_body,
            grid=(rows // tile,),
            in_specs=[
                pl.BlockSpec(
                    (4, 1, tile, feats), lambda i: (0, i * tile // slab, i % (slab // tile), 0)
                )
            ],
            out_specs=[flat, flat, pl.BlockSpec((tile, 128), lambda i: (i, 0))],
        )(x_all, ln1, ln2, stats)

    def mlp_stage(k):
        at = k * UNIT
        bias = fc1_bias[r, :, at : at + UNIT]

        def body(ln_ref, cot_ref, first_ref, second_ref, act_ref, grad_ref):
            step = pl.program_id(0)

            @pl.when(step == 0)
            def _():
                acc[:, : 2 * UNIT, :] = jnp.zeros((4, 2 * UNIT, feats), F32)
                sum_acc[:, :UNIT] = jnp.zeros((8, UNIT), F32)

            hidden = bias
            grad_act = None
            for j in range(4):
                lanes = slice(j * feats, (j + 1) * feats)
                hidden = hidden + product(ln_ref[:, lanes], first_ref[j], ((1,), (0,)))
                term = product(cot_ref[j, 0], second_ref[j], ((1,), (1,)))
                grad_act = term if j == 0 else grad_act + term
            curve = 0.5 * (1.0 + lax.erf(hidden * math.sqrt(0.5)))
            bell = jnp.exp(-0.5 * hidden * hidden) * (1.0 / math.sqrt(2.0 * math.pi))
            act = (hidden * curve).astype(BF16)
            grad_hidden = (grad_act * (curve + hidden * bell)).astype(BF16)
            act_ref[...] = act
            grad_ref[...] = grad_hidden
            sum_acc[0:1, :UNIT] += jnp.sum(grad_hidden.astype(F32), axis=0, keepdims=True)
            for j in range(4):
                lanes = slice(j * feats, (j + 1) * feats)
                acc[j, :UNIT] += product(act, cot_ref[j, 0], ((0,), (0,)))
                acc[j, UNIT : 2 * UNIT] += product(grad_hidden, ln_ref[:, lanes], ((0,), (0,)))

        pltpu.emit_pipeline(
            body,
            grid=(rows // TILE,),
            in_specs=[
                pl.BlockSpec((TILE, D), lambda i: (i, 0)),
                pl.BlockSpec((4, 1, slab, feats), lambda i: (0, i, 0, 0)),
                pl.BlockSpec((4, feats, UNIT), lambda i: (0, 0, (qkv_here + at) // UNIT)),
                pl.BlockSpec((4, UNIT, feats), lambda i: (0, (attn_here + at) // UNIT, 0)),
            ],
            out_specs=[
                pl.BlockSpec((TILE, UNIT), lambda i: (i, (attn_here + at) // UNIT)),
                pl.BlockSpec((TILE, UNIT), lambda i: (i, (qkv_here + at) // UNIT)),
            ],
        )(ln2, cot_all, w1, w2, acts, grads)
        grad_stage(UNIT, qkv_here + at, attn_here + at, 1, k == 0)
        unit_sums[0:1, qkv_here + at : qkv_here + at + UNIT] = sum_acc[0:1, :UNIT]

    def grad_stage(width, first_at, second_at, which, fresh):
        def body(first_ref, part_one, part_two):
            j = pl.program_id(0)
            grad = acc[j, UNIT : UNIT + width].T
            weight = first_ref[0].astype(F32)
            part_one[0] = grad.astype(BF16)
            part_two[0] = acc[j, :UNIT].astype(BF16)
            here = pl.ds(j * feats, feats)
            gains = fold_lanes(grad * weight)
            biases = fold_lanes(weight * sum_acc[0:1, :width])
            if fresh:
                gain_acc[2 * which, here] = gains
                gain_acc[2 * which + 1, here] = biases
            else:
                gain_acc[2 * which, here] += gains
                gain_acc[2 * which + 1, here] += biases

        lanes = slice(first_at, first_at + width)
        block = pl.BlockSpec((1, feats, width), lambda j: (j, 0, 0))
        pltpu.emit_pipeline(
            body,
            grid=(4,),
            in_specs=[block],
            out_specs=[block, pl.BlockSpec((1, UNIT, feats), lambda j: (j, second_at // UNIT, 0))],
        )(w1.at[:, :, lanes], first_part.at[:, :, lanes], second_part)

    def attention_slab(s):
        heads = qkv_here // (3 * HD)
        bias = qkv_bias[r]

        def body(ln_ref, cot_ref, first_ref, second_ref, act_ref, grad_ref):
            qkv = bias
            back = None
            for j in range(4):
                lanes = slice(j * feats, (j + 1) * feats)
                qkv = qkv + product(ln_ref[:, lanes], first_ref[j], ((1,), (0,)))
                term = product(cot_ref[j, 0], second_ref[j], ((1,), (1,)))
                back = term if j == 0 else back + term
            back = back.astype(BF16)
            at = lax.broadcasted_iota(jnp.int32, (TILE, TILE), 0)
            of = lax.broadcasted_iota(jnp.int32, (TILE, TILE), 1)
            token = lax.broadcasted_iota(jnp.int32, (TILE, HD), 0)
            lane = lax.broadcasted_iota(jnp.int32, (TILE, HD), 1)
            begin = jnp.zeros((TILE, HD), jnp.int32)
            edge = 0
            for k in range(lengths.shape[1] - 1):
                edge = edge + lengths[4 * z + s, k]
                begin = jnp.where(token >= edge, edge, begin)
            allowed = (of <= at) & (of >= begin[:, :1])
            angle = (token - begin).astype(F32) * turns[0:1]
            cos, sin = jnp.cos(angle), jnp.sin(angle)
            low = jnp.where(lane < ROT // 2, -sin, 0.0)
            high = jnp.where(lane < ROT // 2, 0.0, sin)
            for h in range(heads):
                attn, grads_here = attention_head(
                    qkv[:, h * 3 * HD : (h + 1) * 3 * HD],
                    back[:, h * HD : (h + 1) * HD],
                    cos,
                    low,
                    high,
                    allowed,
                )
                act_ref[:, h * HD : (h + 1) * HD] = attn
                for i in range(3):
                    at_lane = (h * 3 + i) * HD
                    grad_ref[:, at_lane : at_lane + HD] = grads_here[i].astype(BF16)
            attn, grad = act_ref[...], grad_ref[...]
            sums = jnp.sum(grad.astype(F32), axis=0, keepdims=True)
            sum_acc[0:1, :qkv_here] = sums if s == 0 else sum_acc[0:1, :qkv_here] + sums
            for j in range(4):
                lanes = slice(j * feats, (j + 1) * feats)
                second_term = product(attn, cot_ref[j, 0], ((0,), (0,)))
                first_term = product(grad, ln_ref[:, lanes], ((0,), (0,)))
                acc[j, :UNIT] = second_term if s == 0 else acc[j, :UNIT] + second_term
                acc[j, UNIT:] = first_term if s == 0 else acc[j, UNIT:] + first_term

        pltpu.emit_pipeline(
            body,
            grid=(1,),
            in_specs=[
                pl.BlockSpec((TILE, D), lambda i: (s, 0)),
                pl.BlockSpec((4, 1, slab, feats), lambda i: (0, s, 0, 0)),
                pl.BlockSpec((4, feats, qkv_here), lambda i: (0, 0, 0)),
                pl.BlockSpec((4, UNIT, feats), lambda i: (0, 0, 0)),
            ],
            out_specs=[
                pl.BlockSpec((TILE, UNIT), lambda i: (s, 0)),
                pl.BlockSpec((TILE, qkv_here), lambda i: (s, 0)),
            ],
        )(
            ln1,
            cot_all,
            w1.at[:, :, :qkv_here],
            w2,
            acts,
            grads.at[:, :qkv_here],
        )
        if s == 3:
            grad_stage(qkv_here, 0, 0, 0, True)
            unit_sums[0:1, :qkv_here] = sum_acc[0:1, :qkv_here]

    def out_stage(n):
        def body(act_ref, second_ref, part_ref):
            part_ref[0] = product(act_ref[...], second_ref[0], ((1,), (0,))).astype(BF16)

        pltpu.emit_pipeline(
            body,
            grid=(rows // TILE,),
            in_specs=[
                pl.BlockSpec((TILE, acts.shape[1]), lambda i: (i, 0)),
                pl.BlockSpec((1, w2.shape[1], feats), lambda i: (n, 0, 0)),
            ],
            out_specs=[pl.BlockSpec((1, TILE, feats), lambda i: (n, i, 0))],
        )(acts, w2, out_part)

    def dx_stage(n):
        def body(grad_ref, first_ref, part_ref):
            norms = norm_all[n]
            one = product(grad_ref[:, :qkv_here], first_ref[0, :, :qkv_here], ((1,), (1,)))
            two = product(grad_ref[:, qkv_here:], first_ref[0, :, qkv_here:], ((1,), (1,)))
            part_ref[0] = (one * norms[0:1] + two * norms[2:3]).astype(BF16)

        pltpu.emit_pipeline(
            body,
            grid=(rows // TILE,),
            in_specs=[
                pl.BlockSpec((TILE, grads.shape[1]), lambda i: (i, 0)),
                pl.BlockSpec((1, feats, w1.shape[2]), lambda i: (n, 0, 0)),
            ],
            out_specs=[pl.BlockSpec((1, TILE, feats), lambda i: (n, i, 0))],
        )(grads, w1, dx_part)

    class Scatter:
        def __init__(self, part, from_core, chip, from_x, half, from_y):
            self.part, self.from_core, self.chip = part, from_core, chip
            self.from_x, self.half, self.from_y = from_x, half, from_y
            self.to_core = [
                copies.make(
                    partial(lambda j: part.at[peer[j]], j),
                    partial(lambda j: from_core.at[peer[j] // 2], j),
                    to_row[1],
                )
                for j in (1, 3)
            ]
            self.to_x = copies.make(
                lambda: chip.at[:, far_half], lambda: from_x, to_col
            )
            self.to_y = copies.make(lambda: half.at[1 - y], lambda: from_y, to_row[2])

        def begin(self):
            for copy in self.to_core:
                start(copy)

        def second(self):
            for copy in self.to_core:
                copy().wait_recv()

            def body(left, right, target):
                target[...] = (left[...].astype(F32) + right[...].astype(F32)).astype(BF16)

            block = pl.BlockSpec((1, TILE, feats), lambda s, i: (s, i, 0))
            pltpu.emit_pipeline(
                body,
                grid=(2, rows // TILE),
                in_specs=[
                    pl.BlockSpec((1, TILE, feats), lambda s, i: (2 * s + core, i, 0)),
                    block,
                ],
                out_specs=[block],
            )(self.part, self.from_core, self.chip)
            start(self.to_x)

        def third(self):
            self.to_x().wait_recv()

            def body(left, right, target):
                target[...] = (left[...].astype(F32) + right[...].astype(F32)).astype(BF16)

            block = pl.BlockSpec((1, TILE, feats), lambda s, i: (s, i, 0))
            tiles = own_rows // TILE
            pltpu.emit_pipeline(
                body,
                grid=(2, tiles),
                in_specs=[
                    pl.BlockSpec((1, TILE, feats), lambda s, i: (s, c * tiles + i, 0)),
                    block,
                ],
                out_specs=[block],
            )(self.chip, self.from_x, self.half)
            start(self.to_y)

        def last(self, body, extra, target):
            self.to_y().wait_recv()
            flat = pl.BlockSpec((1, slab, feats), lambda i: (i, 0, 0))
            pltpu.emit_pipeline(
                body,
                grid=(own_rows // TILE,),
                in_specs=[
                    pl.BlockSpec((1, TILE, feats), lambda i: (y, i, 0)),
                    pl.BlockSpec((TILE, feats), lambda i: (i, 0)),
                    flat,
                ],
                out_specs=[flat],
            )(self.half, self.from_y, extra, target)

    out_scatter = Scatter(out_part, out_core, out_chip, out_x, out_half, out_y)
    dx_scatter = Scatter(dx_part, dx_core, dx_chip, dx_x, dx_half, dx_y)
    out_route = Route(
        out_item, dealt, out_up, out_down, out_far, out_send, out_edge, output
    )

    def finish_output():
        def body(half_ref, y_ref, x_ref, item_ref):
            item_ref[0] = (
                half_ref[0].astype(F32)
                + y_ref[...].astype(F32)
                + x_ref[0].astype(F32)
                + out_bias[0:1]
            ).astype(BF16)

        out_scatter.last(body, x_own, out_item)

    row_copies = [
        copies.make(lambda: row_part, lambda: row_sums.at[r], to_row[j]) for j in (1, 2, 3)
    ]

    def sum_grad():
        dx_scatter.to_y().wait_recv()

        def body(half_ref, y_ref, x_ref, stat_ref, target_ref):
            grad = half_ref[0].astype(F32) + y_ref[...].astype(F32)
            target_ref[...] = grad
            normed = (x_ref[0].astype(F32) - stat_ref[:, :1]) * stat_ref[:, 127:]
            one = jnp.sum(grad, axis=1, keepdims=True)
            two = jnp.sum(grad * normed, axis=1, keepdims=True)
            lane = lax.broadcasted_iota(jnp.int32, (TILE, 128), 1)
            both = jnp.where(lane == 0, one, jnp.where(lane == 1, two, 0.0))
            row_part[pl.program_id(0)] = both.T[:8]

        pltpu.emit_pipeline(
            body,
            grid=(own_rows // TILE,),
            in_specs=[
                pl.BlockSpec((1, TILE, feats), lambda i: (y, i, 0)),
                pl.BlockSpec((TILE, feats), lambda i: (i, 0)),
                pl.BlockSpec((1, slab, feats), lambda i: (i, 0, 0)),
                pl.BlockSpec((TILE, 128), lambda i: (slabs * c + i, 0)),
            ],
            out_specs=[pl.BlockSpec((TILE, feats), lambda i: (i, 0))],
        )(dx_half, dx_y, x_own, stats, grad_norm)
        for copy in row_copies:
            start(copy)
        row_sums[r] = row_part[...]

    def finish_grad():
        for copy in row_copies:
            copy().wait_recv()

        def body(grad_ref, cot_ref, x_ref, stat_ref, target_ref):
            step = pl.program_id(0)
            sums = row_sums[0, step] + row_sums[1, step] + row_sums[2, step] + row_sums[3, step]
            sums = jnp.concatenate([sums, jnp.zeros((120, TILE), F32)], axis=0).T * (1.0 / D)
            normed = (x_ref[0].astype(F32) - stat_ref[:, :1]) * stat_ref[:, 127:]
            target_ref[0] = cot_ref[0].astype(F32) + stat_ref[:, 127:] * (
                grad_ref[...] - sums[:, 0:1] - normed * sums[:, 1:2]
            )

        flat = pl.BlockSpec((1, slab, feats), lambda i: (i, 0, 0))
        pltpu.emit_pipeline(
            body,
            grid=(own_rows // TILE,),
            in_specs=[
                pl.BlockSpec((TILE, feats), lambda i: (i, 0)),
                flat,
                flat,
                pl.BlockSpec((TILE, 128), lambda i: (slabs * c + i, 0)),
            ],
            out_specs=[flat],
        )(grad_norm, cot_own, x_own, stats, input_grad)

    sums_wide = small_units.shape[2]
    small_copies = [
        copies.make(
            partial(lambda j: small_part.at[peer[j]], j), lambda: small_row.at[r], to_row[j]
        )
        for j in (1, 2, 3)
    ]
    unit_copies = [
        copies.make(lambda: unit_sums, lambda: small_units.at[r], to_row[j]) for j in (1, 2, 3)
    ]
    col_copy = copies.make(
        lambda: small_here.at[:, pl.ds(sums_wide, feats)], lambda: small_col, to_col
    )
    small_inward = copies.make(lambda: small_here, lambda: small_in, to_in)
    small_across = copies.make(lambda: small_half, lambda: small_other, to_in)
    small_outward = copies.make(lambda: small_in, lambda: small_in, to_out)

    def small_begin():
        for j in range(4):
            rows_here = [
                jnp.sum(gain_acc[k, j * feats : (j + 1) * feats].T, axis=0, keepdims=True)
                for k in range(4)
            ]
            small_part[j] = jnp.concatenate(rows_here + [jnp.zeros((4, feats), F32)], axis=0)
        for copy in small_copies + unit_copies:
            start(copy)
        small_row[r] = small_part[r]
        small_units[r] = unit_sums[...]

    def small_second():
        for copy in small_copies + unit_copies:
            copy().wait_recv()
        small_here[...] = jnp.zeros(small_here.shape, F32)
        for j in range(4):
            small_here[j : j + 1, :sums_wide] = small_units[j, 0:1]
        small_here[:, sums_wide:] = small_row[0] + small_row[1] + small_row[2] + small_row[3]

        def body(cot_ref):
            total = jnp.sum(cot_ref[0].astype(F32), axis=0, keepdims=True)
            small_here[4:5, sums_wide:] += total

        pltpu.emit_pipeline(
            body,
            grid=(slabs,),
            in_specs=[pl.BlockSpec((1, slab, feats), lambda i: (i, 0, 0))],
        )(cot_own)
        start(col_copy)

    def small_third():
        col_copy().wait_recv()
        col_copy().wait_send()
        small_here[:, sums_wide:] += small_col[...]
        when(is_edge, lambda: small_inward().start())

    def small_halve():
        def middle():
            small_inward().wait_recv()
            small_half[...] = small_here[...] + small_in[...]
            small_across().start()

        when(is_mid, middle)

    def small_close():
        def middle():
            small_across().wait_recv()
            small_in[...] = small_half[...] + small_other[...]
            small_outward().start()

        when(is_mid, middle)

    def small_finish():
        def edge():
            small_outward().wait_recv()
            small_inward().wait_send()

        def middle():
            small_across().wait_send()
            small_outward().wait_send()

        when(is_edge, edge)
        when(is_mid, middle)
        total = small_in[...]
        small_sum[:, :sums_wide] = total[:, :sums_wide]
        norms = norm_own[...]
        sums = total[:, sums_wide:]
        gains = [
            (sums[k : k + 1] - norms[k + 1 : k + 2] * sums[k + 1 : k + 2]) / norms[k : k + 1]
            for k in (0, 2)
        ]
        small_sum[:, sums_wide:] = jnp.concatenate(
            [gains[0], sums[1:2], gains[1], sums[3:4], sums[4:]], axis=0
        )

    near, far = 0, 1
    line, crossing = [], []
    begun, halved, closed, crossed = [0], [0], [0], [0]
    flight = 2

    def queue(units, which):
        for unit in units:
            if which == near:
                unit.send(near)
                crossing.append(unit)
            line.append((unit, which))

    def cross(count):
        for _ in range(min(count, len(crossing) - crossed[0])):
            at = crossed[0]
            if at >= flight:
                crossing[at - flight].sent_far()
            crossing[at].send(far)
            crossed[0] += 1

    def lead():
        while begun[0] < min(len(line), halved[0] + 3):
            at = begun[0]

            def edge():
                unit, which = line[at]
                unit.collect(which)
                if at >= flight:
                    before, its_half = line[at - flight]
                    before.inward[its_half]().wait_send()
                unit.inward[which]().start()

            when(is_edge, edge)
            begun[0] += 1

    def serve(count):
        for _ in range(count):
            lead()
            ahead = halved[0]
            if ahead < len(line):
                line[ahead][0].halve(line[ahead][1])
                halved[0] += 1
            if closed[0] < ahead:
                line[closed[0]][0].close(line[closed[0]][1])
                closed[0] += 1

    slab_ids = range(slabs)
    for q in slab_ids:
        x_gather.begin(q)
    cot_route.begin(0)
    norm_all[r] = norm_own[...]
    for copy in norm_copies:
        start(copy)
    cot_route.relay(0)
    cot_route.begin(1)
    for q in slab_ids:
        x_gather.after_y(q)
    mlp_fetch[0].begin()
    cot_route.relay(1)
    cot_route.hand_out(0)
    for q in slab_ids:
        x_gather.after_x(q)
    cot_route.take(0)
    cot_gather.begin(0)
    for q in slab_ids:
        x_gather.after_far(q)
    cot_route.hand_out(1)
    for q in slab_ids:
        x_gather.end(q)
    for copy in norm_copies:
        copy().wait_recv()
    when(is_mid, norm_stage)
    cot_route.take(1)
    cot_gather.begin(1)
    cot_gather.after_y(0)
    cot_gather.after_x(0)
    when(is_edge, norm_stage)
    cot_gather.after_y(1)
    mlp_fetch[1].begin()
    cot_gather.after_x(1)
    for q in slab_ids:
        cot_gather.after_far(q)
    for q in slab_ids:
        cot_gather.end(q)
    mlp_fetch[0].end()
    mlp_fetch[2].begin()
    mlp_stage(0)
    queue(mlp_units[0], near)
    lead()
    mlp_fetch[1].end()
    mlp_fetch[3].begin()
    mlp_stage(1)
    queue(mlp_units[1], near)
    serve(1)
    mlp_fetch[2].end()
    attn_fetch.begin()
    mlp_stage(2)
    queue(mlp_units[2], near)
    serve(2)
    mlp_fetch[3].end()
    mlp_stage(3)
    queue(mlp_units[3], near)
    serve(4)
    attn_fetch.end()
    cross(2)
    attention_slab(0)
    serve(1)
    cross(1)
    queue(mlp_units[0], far)
    attention_slab(1)
    serve(1)
    cross(1)
    queue(mlp_units[1][:1], far)
    attention_slab(2)
    serve(1)
    cross(1)
    attention_slab(3)
    queue(attn_units, near)
    serve(1)
    cross(1)
    for n in range(4):
        out_stage(n)
        if n % 2:
            serve(1)
            cross(1)
    out_scatter.begin()
    queue(mlp_units[1][1:] + mlp_units[2], far)
    dx_stage(0)
    out_scatter.second()
    dx_stage(1)
    serve(1)
    cross(1)
    dx_stage(2)
    serve(1)
    dx_stage(3)
    dx_scatter.begin()
    small_begin()
    serve(1)
    cross(1)
    small_second()
    queue(mlp_units[3], far)
    serve(1)
    out_scatter.third()
    cross(1)
    dx_scatter.second()
    serve(1)
    small_third()
    serve(1)
    cross(1)
    queue(attn_units, far)
    finish_output()
    out_route.begin(0)
    serve(1)
    cross(1)
    small_halve()
    out_route.relay(0)
    out_route.begin(1)
    dx_scatter.third()
    serve(1)
    cross(1)
    small_close()
    out_route.relay(1)
    serve(1)
    cross(4)
    out_route.hand_out(0)
    serve(1)
    sum_grad()
    out_route.hand_out(1)
    serve(1)
    out_route.take(0)
    finish_grad()
    serve(1)
    out_route.take(1)
    while closed[0] < len(line):
        serve(1)
    for at, (unit, which) in enumerate(line):
        unit.finish(which, at >= len(line) - flight)
    for unit in crossing[len(crossing) - flight :]:
        unit.sent_far()
    small_finish()
    cot_route.finish()
    out_route.finish()
    for copy in sent:
        if copy is not col_copy:
            copy().wait_send()


def widen_body(first_ref, dense_ref, fc2_ref, qkv_out, fc1_out, dense_out, fc2_out):
    qkv_here = qkv_out.shape[1]
    qkv_out[...] = first_ref[0, :, :qkv_here].astype(F32)
    fc1_out[...] = first_ref[0, :, qkv_here:].astype(F32)
    dense_out[...] = dense_ref[0].astype(F32)
    fc2_out[...] = fc2_ref[0].astype(F32)


def widen(first_sum, second_sum, qkv_here, attn_here):
    feats, first_cols = first_sum.shape[1:]
    hidden_here = first_cols - qkv_here
    tiles = hidden_here // attn_here
    tile = feats // tiles
    return pl.pallas_call(
        widen_body,
        grid=(4, tiles),
        in_specs=[
            pl.BlockSpec((1, tile, first_cols), lambda s, i: (s, i, 0)),
            pl.BlockSpec((1, attn_here // tiles, feats), lambda s, i: (s, i, 0)),
            pl.BlockSpec((1, attn_here, feats), lambda s, i: (s, 1 + i, 0)),
        ],
        out_specs=[
            pl.BlockSpec((tile, qkv_here), lambda s, i: (i, s)),
            pl.BlockSpec((tile, hidden_here), lambda s, i: (i, s)),
            pl.BlockSpec((attn_here // tiles, feats), lambda s, i: (s * tiles + i, 0)),
            pl.BlockSpec((attn_here, feats), lambda s, i: (s * tiles + i, 0)),
        ],
        out_shape=[
            jax.ShapeDtypeStruct((feats, 4 * qkv_here), F32),
            jax.ShapeDtypeStruct((feats, 4 * hidden_here), F32),
            jax.ShapeDtypeStruct((4 * attn_here, feats), F32),
            jax.ShapeDtypeStruct((4 * hidden_here, feats), F32),
        ],
        compiler_params=pltpu.CompilerParams(vmem_limit_bytes=32 * 1024 * 1024),
    )(first_sum, second_sum, second_sum)


def dealt_layer(
    layer_input,
    lengths,
    deal_table,
    ln1_gain,
    ln1_bias,
    qkv_weight,
    qkv_bias,
    dense_weight,
    dense_bias,
    ln2_gain,
    ln2_bias,
    fc1_weight,
    fc1_bias,
    fc2_weight,
    fc2_bias,
    cotangent,
):
    own_rows, feats = layer_input.shape
    rows = 2 * own_rows
    slab = own_rows // 2
    qkv_cols = qkv_weight.shape[1]
    qkv_here = qkv_cols // 4
    attn_here = dense_weight.shape[0] // 4
    hidden_cols = fc1_weight.shape[1]
    hidden_here = hidden_cols // 4
    first_cols = qkv_here + hidden_here
    second_rows = attn_here + hidden_here

    norms = jnp.stack([ln1_gain, ln1_bias, ln2_gain, ln2_bias] * 2)
    out_bias = (dense_bias + fc2_bias).reshape(1, feats)
    turns = 1.0 / 10000.0 ** (np.arange(0, ROT, 2) / ROT)
    turns = np.concatenate([turns, turns, np.zeros(HD - ROT)])
    turns = np.broadcast_to(turns.astype(np.float32), (8, HD))

    low = lambda *shape: jax.ShapeDtypeStruct(shape, BF16)
    wide = lambda *shape: jax.ShapeDtypeStruct(shape, F32)
    first = low(4, feats, first_cols)
    second = low(4, second_rows, feats)
    item = low(2, slab, feats)
    small_shape = (8, first_cols + feats)
    outputs = [first, second, item, wide(2, slab, feats)]
    scatter = [
        low(4, rows, feats),
        low(2, rows, feats),
        low(2, rows, feats),
        low(2, own_rows, feats),
        low(2, own_rows, feats),
        low(own_rows, feats),
    ]
    buffers = (
        [wide(own_rows, feats), item, wide(rows, 128)]
        + [low(4, 4, slab, feats)] * 2
        + [low(rows, D)] * 2
        + [first, second, low(rows, second_rows), low(rows, first_cols)]
        + [first, second] * 5
        + scatter
        + [item]
        + scatter
        + [item] * 10
    )
    any_space = pl.BlockSpec(memory_space=pl.ANY)
    vmem = pl.BlockSpec(memory_space=pltpu.VMEM)
    smem = pl.BlockSpec(memory_space=pltpu.SMEM)
    copies = 250
    results = pl.pallas_call(
        layer_kernel,
        in_specs=[smem] * 2 + [any_space] * 2 + [vmem] * 5 + [any_space] * 4,
        out_specs=[any_space] * 4 + [vmem] + [any_space] * len(buffers),
        out_shape=outputs + [wide(*small_shape)] + buffers,
        scratch_shapes=[
            pltpu.VMEM((4, UNIT + qkv_here, feats), F32),
            pltpu.VMEM((4, 8, feats), F32),
            pltpu.VMEM((4, D, 128), F32),
            pltpu.VMEM((8, qkv_here), F32),
            pltpu.VMEM((8, first_cols), F32),
            pltpu.VMEM((4, 8, feats), F32),
            pltpu.VMEM((4, 8, feats), F32),
            pltpu.VMEM((4, 8, first_cols), F32),
            pltpu.VMEM((8, feats), F32),
            pltpu.VMEM(small_shape, F32),
            pltpu.VMEM(small_shape, F32),
            pltpu.VMEM(small_shape, F32),
            pltpu.VMEM(small_shape, F32),
            pltpu.VMEM((2, 8, slab), F32),
            pltpu.VMEM((4, 2, 8, slab), F32),
            pltpu.SemaphoreType.DMA((copies,)),
            pltpu.SemaphoreType.DMA((copies,)),
            pltpu.SemaphoreType.DMA((32,)),
        ],
        compiler_params=pltpu.CompilerParams(
            collective_id=0, has_side_effects=True, vmem_limit_bytes=60 * 1024 * 1024
        ),
        cost_estimate=pl.CostEstimate(
            flops=6 * rows * D * (first_cols + second_rows),
            bytes_accessed=200 * 1024 * 1024,
            transcendentals=rows * hidden_here,
        ),
    )(
        lengths,
        deal_table,
        layer_input.reshape(2, slab, feats),
        cotangent.reshape(2, slab, feats),
        norms,
        qkv_bias.reshape(4, 1, qkv_here),
        fc1_bias.reshape(4, 1, hidden_here),
        out_bias,
        turns,
        qkv_weight,
        dense_weight,
        fc1_weight,
        fc2_weight,
    )
    first_sum, second_sum, output, input_grad, small = results[:5]
    qkv_grad, fc1_grad, dense_grad, fc2_grad = widen(first_sum, second_sum, qkv_here, attn_here)
    norm_sums = small[:5, first_cols:]
    return (
        output.reshape(own_rows, feats),
        input_grad.reshape(own_rows, feats),
        norm_sums[0],
        norm_sums[1],
        qkv_grad,
        small[:4, :qkv_here].reshape(qkv_cols),
        dense_grad,
        norm_sums[4],
        norm_sums[2],
        norm_sums[3],
        fc1_grad,
        small[:4, qkv_here:first_cols].reshape(hidden_cols),
        fc2_grad,
        norm_sums[4],
    )


def solution(mesh):
    grid = tuple(mesh.shape[axis] for axis in ("dp", "row", "col"))
    placed = (
        P(("dp", "col"), "row"),
        P(),
        P(),
        P("row"),
        P("row"),
        P("row", "col"),
        P("col"),
        P("col", "row"),
        P("row"),
        P("row"),
        P("row"),
        P("row", "col"),
        P("col"),
        P("col", "row"),
        P("row"),
        P(("dp", "col"), "row"),
    )
    return jax.shard_map(
        dealt_layer if grid == (4, 4, 2) else local,
        mesh=mesh,
        in_specs=placed,
        out_specs=(
            P(("dp", "col"), "row"),
            P(("dp", "col"), "row"),
            P("row"),
            P("row"),
            P("row", "col"),
            P("col"),
            P("col", "row"),
            P("row"),
            P("row"),
            P("row"),
            P("row", "col"),
            P("col"),
            P("col", "row"),
            P("row"),
        ),
        check_vma=False,
    )
```

```python
from functools import partial
import math

import jax
import jax.numpy as jnp
import numpy as np
from jax import lax
from jax.experimental import pallas as pl
from jax.experimental.pallas import tpu as pltpu
from jax.sharding import PartitionSpec as P

D = 2048
HD = 128
ROT = 32
QBLK = 512
CHUNK = 256
BF16 = jnp.bfloat16
F32 = jnp.float32


norm_epsilon = 1e-05
masked_score = -1000000000.0


def rotary_tables(positions):
    frequency = 1.0 / 10000.0 ** (jnp.arange(0, ROT, 2, dtype=jnp.float32) / ROT)
    angles = positions.astype(jnp.float32)[:, None] * frequency[None, :]
    angles = jnp.concatenate([angles, angles], axis=1)
    return (jnp.cos(angles), jnp.sin(angles))


def rotate(values, cos_table, sin_table):
    half_rot = ROT // 2
    rotated = values[..., :ROT]
    turned = jnp.concatenate([-rotated[..., half_rot:], rotated[..., :half_rot]], axis=-1)
    rotated = rotated * cos_table[:, None, :] + turned * sin_table[:, None, :]
    return jnp.concatenate([rotated, values[..., ROT:]], axis=-1)


def segment_layout(seq_lengths, length):
    seq_ends = jnp.cumsum(seq_lengths)
    token_place = jnp.arange(length, dtype=jnp.int32)
    sequence_ids = jnp.sum((token_place[:, None] >= seq_ends[None, :]).astype(jnp.int32), axis=1)
    starts = seq_ends - seq_lengths
    seq_hits = sequence_ids[:, None] == jnp.arange(seq_lengths.shape[0], dtype=jnp.int32)[None, :]
    seq_begin = jnp.sum(jnp.where(seq_hits, starts[None, :], 0), axis=1)
    return (sequence_ids, token_place - seq_begin)


def contract_rows(left_side, right_side):
    return lax.dot_general(
        left_side, right_side, (((0,), (0,)), ((), ())), preferred_element_type=jnp.float32
    )


def contract_cols(left_side, right_side):
    return lax.dot_general(
        left_side, right_side, (((1,), (1,)), ((), ())), preferred_element_type=jnp.float32
    )


def pick_rows(pooled, chosen):
    row_hits = chosen[None, :] == jnp.arange(pooled.shape[0], dtype=jnp.int32)[:, None]
    return jnp.sum(jnp.where(row_hits[:, :, None], pooled.astype(jnp.float32), 0.0), axis=0)


def local(
    layer_input,
    lengths,
    deal_table,
    ln1_gain,
    ln1_bias,
    qkv_weight,
    qkv_bias,
    dense_weight,
    dense_bias,
    ln2_gain,
    ln2_bias,
    fc1_weight,
    fc1_bias,
    fc2_weight,
    fc2_bias,
    cotangent,
):
    dp_count = lax.axis_size("dp")
    row_count = lax.axis_size("row")
    col_count = lax.axis_size("col")
    group_id = lax.axis_index("dp")
    row_id = lax.axis_index("row")
    col_id = lax.axis_index("col")
    own_rows, own_feats = layer_input.shape
    group_rows = own_rows * col_count
    slab_rows = group_rows // row_count
    qkv_cols = qkv_weight.shape[1]
    attn_cols = dense_weight.shape[0]
    heads_here = qkv_cols // (3 * HD)
    score_scale = 1.0 / math.sqrt(HD)
    local_slab = (col_id * own_rows + jnp.arange(own_rows, dtype=jnp.int32)) // slab_rows
    slab_hits = local_slab[:, None] == jnp.arange(row_count, dtype=jnp.int32)[None, :]
    deal_here = lax.dynamic_index_in_dim(deal_table, group_id, 1, keepdims=False)
    source = jnp.sum(jnp.where(slab_hits, deal_here[None, :], 0), axis=1)
    pooled = lax.all_gather(layer_input, "dp", axis=0, tiled=True).reshape(
        dp_count, own_rows, own_feats
    )
    mine_rows = pick_rows(pooled, source).astype(jnp.bfloat16)
    input_all = lax.all_gather(mine_rows, "col", axis=0, tiled=True)
    input_wide = input_all.astype(jnp.float32)
    row_stats = lax.psum(
        (jnp.sum(input_wide, axis=1), jnp.sum(input_wide * input_wide, axis=1)), "row"
    )
    row_mean = row_stats[0] / D
    inv_std = lax.rsqrt(row_stats[1] / D - row_mean * row_mean + norm_epsilon)
    normed = (input_wide - row_mean[:, None]) * inv_std[:, None]
    own_start = col_id * own_rows
    normed_own = lax.dynamic_slice_in_dim(normed, own_start, own_rows, 0)
    inv_std_own = lax.dynamic_slice_in_dim(inv_std, own_start, own_rows, 0)
    ln1_all = (normed * ln1_gain + ln1_bias).astype(jnp.bfloat16)
    ln2_all = (normed * ln2_gain + ln2_bias).astype(jnp.bfloat16)
    part_one = ln1_all
    part_two = ln2_all
    first_sums = lax.psum_scatter(
        jnp.concatenate(
            [
                jnp.dot(part_one, qkv_weight, preferred_element_type=jnp.float32),
                jnp.dot(part_two, fc1_weight, preferred_element_type=jnp.float32),
            ],
            axis=1,
        ),
        "row",
        scatter_dimension=0,
        tiled=True,
    )
    qkv_out = first_sums[:, :qkv_cols] + qkv_bias
    hidden = first_sums[:, qkv_cols:] + fc1_bias
    slab_source = (
        lax.dynamic_index_in_dim(deal_here, row_id, 0, keepdims=False) * row_count + row_id
    )
    seq_lengths = lax.dynamic_index_in_dim(lengths, slab_source, 0, keepdims=False)
    sequence_ids, positions = segment_layout(seq_lengths, slab_rows)
    token_place = jnp.arange(slab_rows, dtype=jnp.int32)
    cos_table, sin_table = rotary_tables(positions)
    packed = qkv_out.reshape(slab_rows, heads_here, 3, HD)
    query_pre = packed[:, :, 0]
    key_pre = packed[:, :, 1]
    queries = rotate(query_pre, cos_table, sin_table).astype(jnp.bfloat16)
    keys_rot = rotate(key_pre, cos_table, sin_table).astype(jnp.bfloat16)
    values = packed[:, :, 2].astype(jnp.bfloat16)

    def block_scores(block_id):
        first_row = block_id * QBLK
        last_row = first_row + QBLK
        allowed = (sequence_ids[first_row:last_row, None] == sequence_ids[None, :last_row]) & (
            token_place[None, :last_row] <= token_place[first_row:last_row, None]
        )
        scores = (
            jnp.einsum("qhd,khd->hqk", queries, keys_rot, preferred_element_type=jnp.float32)
            * score_scale
        )
        return jnp.where(allowed[None], scores, masked_score)

    block_id = 0
    last_row = (block_id + 1) * QBLK
    scores = block_scores(block_id)
    row_top = jnp.max(scores, axis=-1, keepdims=True)
    exp_total = jnp.sum(jnp.exp(scores - row_top), axis=-1, keepdims=True)
    log_total = row_top + jnp.log(exp_total)
    probs_low = jnp.exp(scores - log_total).astype(jnp.bfloat16)
    mixtures = jnp.einsum("hqk,khd->qhd", probs_low, values, preferred_element_type=jnp.float32)
    log_totals = [log_total]
    attn_out = mixtures.reshape(slab_rows, attn_cols).astype(jnp.bfloat16)
    activated = jax.nn.gelu(hidden, approximate=False).astype(jnp.bfloat16)
    attn_all, act_all = (
        lax.all_gather(attn_out, "row", axis=0, tiled=True),
        lax.all_gather(activated, "row", axis=0, tiled=True),
    )
    part_one = attn_all
    part_two = act_all
    branch_sum = lax.psum_scatter(
        jnp.dot(part_one, dense_weight, preferred_element_type=jnp.float32)
        + jnp.dot(part_two, fc2_weight, preferred_element_type=jnp.float32),
        "col",
        scatter_dimension=0,
        tiled=True,
    )
    output = (mine_rows.astype(jnp.float32) + branch_sum + dense_bias + fc2_bias).astype(
        jnp.bfloat16
    )
    grad_all = lax.all_gather(cotangent, "col", axis=0, tiled=True)
    dense_grad = contract_rows(attn_all, grad_all)
    fc2_grad = contract_rows(act_all, grad_all)
    out_bias_grad = jnp.sum(grad_all, axis=0, dtype=jnp.float32)
    grad_block = grad_all
    grad_second = lax.psum_scatter(
        jnp.concatenate(
            [contract_cols(grad_block, dense_weight), contract_cols(grad_block, fc2_weight)], axis=1
        ),
        "row",
        scatter_dimension=0,
        tiled=True,
    )
    grad_mix = grad_second[:, :attn_cols].astype(jnp.bfloat16).reshape(slab_rows, heads_here, HD)
    gelu_back = jax.vjp(partial(jax.nn.gelu, approximate=False), hidden)[1]
    grad_hidden = gelu_back(grad_second[:, attn_cols:])[0]
    grad_key = jnp.zeros((slab_rows, heads_here, HD), jnp.float32)
    grad_value = jnp.zeros((slab_rows, heads_here, HD), jnp.float32)
    block_id = 0
    first_row = block_id * QBLK
    last_row = first_row + QBLK
    probs_full = jnp.exp(block_scores(block_id) - log_totals[block_id])
    probs_low = probs_full.astype(jnp.bfloat16)
    grad_block = grad_mix
    grad_value = grad_value.at[:last_row].add(
        jnp.einsum("hqk,qhd->khd", probs_low, grad_block, preferred_element_type=jnp.float32)
    )
    grad_probs = jnp.einsum("qhd,khd->hqk", grad_block, values, preferred_element_type=jnp.float32)
    centre = jnp.sum(probs_full * grad_probs, axis=-1, keepdims=True)
    grad_scores = (probs_full * (grad_probs - centre)).astype(jnp.bfloat16)
    grad_queries = (
        jnp.einsum("hqk,khd->qhd", grad_scores, keys_rot, preferred_element_type=jnp.float32)
        * score_scale
    )
    grad_key = grad_key.at[:last_row].add(
        jnp.einsum("hqk,qhd->khd", grad_scores, queries, preferred_element_type=jnp.float32)
        * score_scale
    )
    turn_back = jax.vjp(lambda values_in: rotate(values_in, cos_table, sin_table), query_pre)[1]
    grad_query_pre = turn_back(grad_queries)[0]
    grad_key_pre = turn_back(grad_key)[0]
    grad_qkv = jnp.stack([grad_query_pre, grad_key_pre, grad_value], axis=2).reshape(
        slab_rows, qkv_cols
    )
    grad_first = jnp.concatenate([grad_qkv, grad_hidden], axis=1).astype(jnp.bfloat16)
    grad_first_all = lax.all_gather(grad_first, "row", axis=0, tiled=True)
    grad_qkv_all = grad_first_all[:, :qkv_cols]
    grad_hidden_all = grad_first_all[:, qkv_cols:]
    qkv_weight_grad = contract_rows(ln1_all, grad_qkv_all)
    qkv_bias_grad = jnp.sum(grad_qkv_all, axis=0, dtype=jnp.float32)
    fc1_weight_grad = contract_rows(ln2_all, grad_hidden_all)
    fc1_bias_grad = jnp.sum(grad_hidden_all, axis=0, dtype=jnp.float32)
    grad_block = grad_first_all
    summed = lax.psum_scatter(
        jnp.concatenate(
            [
                contract_cols(grad_block[:, :qkv_cols], qkv_weight),
                contract_cols(grad_block[:, qkv_cols:], fc1_weight),
            ],
            axis=1,
        ),
        "col",
        scatter_dimension=0,
        tiled=True,
    )
    grad_ln_one = summed[:, :own_feats]
    grad_ln_two = summed[:, own_feats:]
    gain_terms = (
        jnp.sum(grad_ln_one * normed_own, axis=0),
        jnp.sum(grad_ln_one, axis=0),
        jnp.sum(grad_ln_two * normed_own, axis=0),
        jnp.sum(grad_ln_two, axis=0),
    )
    grad_normed = grad_ln_one * ln1_gain + grad_ln_two * ln2_gain
    row_sums = lax.psum(
        (jnp.sum(grad_normed, axis=1), jnp.sum(grad_normed * normed_own, axis=1)), "row"
    )
    grad_dealt = cotangent.astype(jnp.float32) + inv_std_own[:, None] * (
        grad_normed - row_sums[0][:, None] / D - normed_own * row_sums[1][:, None] / D
    )
    gain_sums = lax.psum(
        (gain_terms[0], gain_terms[1], gain_terms[2], gain_terms[3]), ("dp", "col")
    )
    weights_summed = lax.psum(
        (
            qkv_weight_grad,
            qkv_bias_grad,
            dense_grad,
            fc1_weight_grad,
            fc1_bias_grad,
            fc2_grad,
            out_bias_grad,
        ),
        "dp",
    )
    pool_back = lax.all_gather(grad_dealt, "dp", axis=0, tiled=True).reshape(
        dp_count, own_rows, own_feats
    )
    back_here = jnp.sum(
        jnp.where(deal_table == group_id, jnp.arange(dp_count, dtype=jnp.int32)[None, :], 0), axis=1
    )
    target = jnp.sum(jnp.where(slab_hits, back_here[None, :], 0), axis=1)
    input_grad = pick_rows(pool_back, target)
    return (
        output,
        input_grad,
        gain_sums[0],
        gain_sums[1],
        weights_summed[0],
        weights_summed[1],
        weights_summed[2],
        weights_summed[6],
        gain_sums[2],
        gain_sums[3],
        weights_summed[3],
        weights_summed[4],
        weights_summed[5],
        weights_summed[6],
    )


UNIT = 256
TILE = 512


def product(left, right, dims):
    return lax.dot_general(left, right, (dims, ((), ())), preferred_element_type=F32)


def fold_lanes(values):
    total = values[:, :128]
    for at in range(128, values.shape[1], 128):
        total = total + values[:, at : at + 128]
    return total


class Copies:
    def __init__(self, send_sems, recv_sems):
        self.send_sems, self.recv_sems, self.used = send_sems, recv_sems, 0

    def make(self, source, target, device):
        number = self.used
        self.used += 1

        def build():
            return pltpu.make_async_remote_copy(
                src_ref=source(),
                dst_ref=target(),
                send_sem=self.send_sems.at[number],
                recv_sem=self.recv_sems.at[number],
                device_id=device,
                device_id_type=pl.DeviceIdType.MESH,
            )

        return build


def attention_head(qkv, back, cos, low, high, allowed):
    scale = 1.0 / math.sqrt(HD)

    def turn(values):
        return values * cos + pltpu.roll(values, HD - 16, 1) * low + pltpu.roll(values, 16, 1) * high

    def turn_back(values):
        return (
            values * cos
            + pltpu.roll(values * high, HD - 16, 1)
            + pltpu.roll(values * low, 16, 1)
        )

    query = turn(qkv[:, :HD]).astype(BF16)
    key = turn(qkv[:, HD : 2 * HD]).astype(BF16)
    value = qkv[:, 2 * HD :].astype(BF16)
    scores = product(query, key, ((1,), (1,))) * scale
    scores = jnp.where(allowed, scores, masked_score)
    weight = jnp.exp(scores - jnp.max(scores, axis=1, keepdims=True))
    probs = weight * (1.0 / jnp.sum(weight, axis=1, keepdims=True))
    probs_low = probs.astype(BF16)
    attn = product(probs_low, value, ((1,), (0,))).astype(BF16)
    grad_probs = product(back, value, ((1,), (1,)))
    centre = jnp.sum(probs * grad_probs, axis=1, keepdims=True)
    grad_scores = (probs * (grad_probs - centre)).astype(BF16)
    grad_query = product(grad_scores, key, ((1,), (0,))) * scale
    grad_key = product(grad_scores, query, ((0,), (0,))) * scale
    grad_value = product(probs_low, back, ((0,), (0,)))
    return attn, [turn_back(grad_query), turn_back(grad_key), grad_value]


def layer_kernel(
    lengths,
    deal_table,
    x_own,
    cot_in,
    norm_own,
    qkv_bias,
    fc1_bias,
    out_bias,
    turns,
    qkv_w,
    dense_w,
    fc1_w,
    fc2_w,
    first_sum,
    second_sum,
    output,
    input_grad,
    small_sum,
    grad_norm,
    cot_own,
    stats,
    x_all,
    cot_all,
    ln1,
    ln2,
    w1,
    w2,
    acts,
    grads,
    first_part,
    second_part,
    out_part,
    out_core,
    out_chip,
    out_x,
    out_half,
    out_y,
    out_item,
    dx_part,
    dx_core,
    dx_chip,
    dx_x,
    dx_half,
    dx_y,
    cot_up,
    cot_down,
    cot_far,
    cot_send,
    cot_edge,
    out_up,
    out_down,
    out_far,
    out_send,
    out_edge,
    acc,
    norm_all,
    first_in,
    second_in,
    first_other,
    second_other,
    first_slot,
    second_slot,
    sum_acc,
    unit_sums,
    small_part,
    small_row,
    small_units,
    small_col,
    small_here,
    small_in,
    small_half,
    small_other,
    row_part,
    row_sums,
    send_sems,
    recv_sems,
    local_sems,
):
    z, r, c = lax.axis_index("dp"), lax.axis_index("row"), lax.axis_index("col")
    y, core = r // 2, r % 2
    mid = ((z + 1) // 2) % 2
    upper = z // 2
    z_in = mid * (3 - z) + (1 - mid) * (1 + upper)
    z_out = 3 * upper
    is_mid, is_edge = mid == 1, mid == 0
    peer = [r, 2 * y + (1 - core), 2 * (1 - y) + core, 2 * (1 - y) + (1 - core)]
    slabs, slab, feats = x_own.shape
    own_rows = slabs * slab
    rows = 2 * own_rows
    hidden_here = fc1_w.shape[1] // 4
    qkv_here = qkv_w.shape[1] // 4
    attn_here = dense_w.shape[0] // 4
    to_row = [{"row": peer[j]} for j in range(4)]
    to_col = {"col": 1 - c}
    to_in = {"dp": z_in}
    to_out = {"dp": z_out}
    copies = Copies(send_sems, recv_sems)
    sent = []

    barrier = pltpu.get_barrier_semaphore()

    def greet(device):
        pl.semaphore_signal(barrier, inc=1, device_id=device, device_id_type=pl.DeviceIdType.MESH)

    for j in (1, 2, 3):
        greet(to_row[j])
    greet(to_col)
    greet(to_in)

    @pl.when(is_mid)
    def _():
        greet(to_out)
        pl.semaphore_wait(barrier, 6)

    @pl.when(is_edge)
    def _():
        pl.semaphore_wait(barrier, 5)

    def start(copy):
        copy().start()
        sent.append(copy)

    def when(flag, action):
        pl.when(flag)(action)

    local_used = [0]

    def local(source, target):
        number = local_used[0]
        local_used[0] += 1

        def build():
            return pltpu.make_async_copy(source(), target(), local_sems.at[number])

        build().start()
        return build

    own_half = pl.ds(c * own_rows, own_rows)
    far_half = pl.ds((1 - c) * own_rows, own_rows)

    class Gather:
        def __init__(self, own, whole, by_row):
            self.own, self.whole = own, whole

            def place(j, half, q):
                return lambda: whole.at[peer[j], slabs * half + q]

            def own_slab(q):
                return lambda: own.at[q]

            ids = range(slabs)
            self.to_y = [copies.make(own_slab(q), place(0, c, q), to_row[2]) for q in ids]
            self.to_x = [copies.make(own_slab(q), place(0, c, q), to_col) for q in ids]
            self.to_core = [copies.make(own_slab(q), place(0, c, q), to_row[1]) for q in ids]
            self.y_core = [copies.make(place(2, c, q), place(2, c, q), to_row[1]) for q in ids]
            self.x_core = [
                copies.make(place(0, 1 - c, q), place(0, 1 - c, q), to_row[1]) for q in ids
            ]
            self.far_core = [
                copies.make(place(2, 1 - c, q), place(2, 1 - c, q), to_row[1]) for q in ids
            ]
            self.by_row = by_row
            self.far = [
                copies.make(place(0, 1 - c, q), place(0, 1 - c, q), to_row[2])
                if q in by_row
                else copies.make(place(2, c, q), place(2, c, q), to_col)
                for q in ids
            ]
            self.kept = [None] * slabs

        def begin(self, q):
            start(self.to_y[q])
            start(self.to_x[q])
            start(self.to_core[q])
            self.kept[q] = local(
                lambda: self.own.at[q], lambda: self.whole.at[r, slabs * c + q]
            )

        def after_y(self, q):
            self.to_y[q]().wait_recv()
            if q not in self.by_row:
                start(self.far[q])
            start(self.y_core[q])

        def after_x(self, q):
            self.to_x[q]().wait_recv()
            if q in self.by_row:
                start(self.far[q])
            start(self.x_core[q])

        def after_far(self, q):
            self.far[q]().wait_recv()
            start(self.far_core[q])

        def end(self, q):
            self.kept[q]().wait()
            for group in (self.to_core, self.y_core, self.x_core, self.far_core):
                group[q]().wait_recv()

    def choose(q, goes, plane, refs, target):
        def body(*blocks):
            value = blocks[0][...]
            for (source, _), block in zip(refs[1:], blocks[1:]):
                value = jnp.where(goes(q, source, plane), block[...], value)
            blocks[-1][...] = value

        tile = slab // 4
        block = pl.BlockSpec((tile, feats), lambda i: (i, 0))
        pltpu.emit_pipeline(
            body, grid=(4,), in_specs=[block] * len(refs), out_specs=[block]
        )(*[ref.at[q] for _, ref in refs], target.at[q])

    class Route:
        def __init__(self, item, goes, up, down, far, send, edge, target):
            self.item, self.goes, self.up, self.down = item, goes, up, down
            self.far, self.send, self.edge, self.target = far, send, edge, target

            def at(ref, q):
                return lambda: ref.at[q]

            ids = range(slabs)
            self.upward = [copies.make(at(item, q), at(up, q), {"dp": z + 1}) for q in ids]
            self.downward = [copies.make(at(item, q), at(down, q), {"dp": z - 1}) for q in ids]
            self.far_up = [copies.make(at(up, q), at(far, q), to_in) for q in ids]
            self.far_down = [copies.make(at(down, q), at(far, q), to_in) for q in ids]
            self.outward = [copies.make(at(send, q), at(edge, q), to_out) for q in ids]

        def begin(self, q):
            when(z < 2, lambda: self.upward[q]().start())
            when(z > 1, lambda: self.downward[q]().start())

        def relay(self, q):
            def from_below():
                self.upward[q]().wait_recv()
                self.far_up[q]().start()

            def from_above():
                self.downward[q]().wait_recv()
                self.far_down[q]().start()

            when(z == 1, from_below)
            when(z == 2, from_above)

        def hand_out(self, q):
            def middle():
                def below():
                    self.downward[q]().wait_recv()
                    self.far_down[q]().wait_recv()

                def above():
                    self.upward[q]().wait_recv()
                    self.far_up[q]().wait_recv()

                when(z == 1, below)
                when(z == 2, above)
                refs = [
                    (z, self.item),
                    (z - 1, self.up),
                    (z + 1, self.down),
                    (3 * (2 - z), self.far),
                ]
                choose(q, self.goes, z_out, refs, self.send)
                self.outward[q]().start()
                choose(q, self.goes, z, refs, self.target)

            when(is_mid, middle)

        def take(self, q):
            def edge():
                self.outward[q]().wait_recv()
                block = pl.BlockSpec((slab // 4, feats), lambda i: (i, 0))

                def body(edge_ref, item_ref, target_ref):
                    mine = self.goes(q, z, z)
                    target_ref[...] = jnp.where(mine, item_ref[...], edge_ref[...])

                pltpu.emit_pipeline(
                    body, grid=(4,), in_specs=[block] * 2, out_specs=[block]
                )(self.edge.at[q], self.item.at[q], self.target.at[q])

            when(is_edge, edge)

        def finish(self):
            for q in range(slabs):
                when(z < 2, lambda: self.upward[q]().wait_send())
                when(z > 1, lambda: self.downward[q]().wait_send())
                when(z == 1, lambda: self.far_up[q]().wait_send())
                when(z == 2, lambda: self.far_down[q]().wait_send())
                when(is_mid, lambda: self.outward[q]().wait_send())

    def undealt(q, source, plane):
        return deal_table[slabs * c + q, source] == plane

    def dealt(q, source, plane):
        return deal_table[slabs * c + q, plane] == source

    x_gather = Gather(x_own, x_all, ())
    cot_gather = Gather(cot_own, cot_all, (1,))
    cot_route = Route(
        cot_in, undealt, cot_up, cot_down, cot_far, cot_send, cot_edge, cot_own
    )
    norm_copies = [
        copies.make(lambda: norm_own, lambda: norm_all.at[r], to_row[j]) for j in (1, 2, 3)
    ]

    odd = z % 2
    across_row = 2 * (1 - y) + core + odd * (1 - 2 * core)
    to_across = {"row": across_row}
    to_pair = {"dp": z + 1 - 2 * odd}

    class Fetch:
        def __init__(
            self, paired, first, first_at, first_width, at, second, second_at, second_width, low
        ):
            size = UNIT if first is fc1_w else qkv_here

            def first_source(taker):
                lanes = pl.multiple_of(taker * first_width + first_at, 256)
                return lambda: first.at[:, pl.ds(lanes, size)]

            def second_source(taker):
                begin = pl.multiple_of(taker * second_width + second_at, 256)
                return lambda: second.at[pl.ds(begin, UNIT)]

            def first_target(giver):
                return lambda: w1.at[giver, :, pl.ds(at, size)]

            def second_target(giver):
                return lambda: w2.at[giver, pl.ds(low, UNIT)]

            pairs = ((first_source, first_target), (second_source, second_target))
            self.beside = [copies.make(f(peer[1]), t(r), to_row[1]) for f, t in pairs]
            self.paired = paired
            if paired:
                self.over = [copies.make(f(across_row), t(r), to_across) for f, t in pairs]
                self.shared = [
                    copies.make(t(across_row), t(across_row), to_pair) for _, t in pairs
                ]
            else:
                self.over = [
                    copies.make(f(peer[j]), t(r), to_row[j]) for f, t in pairs for j in (2, 3)
                ]
            self.kept = [(f(r), t(r)) for f, t in pairs]

        def begin(self):
            for copy in self.over + self.beside:
                start(copy)
            self.kept = [local(*pair) for pair in self.kept]

        def share(self):
            for copy, onward in zip(self.over, self.shared):
                copy().wait_recv()
                start(onward)

        def end(self):
            for copy in self.beside + (self.shared if self.paired else self.over):
                copy().wait_recv()
            for copy in self.kept:
                copy().wait()

    attn_fetch = Fetch(False, qkv_w, 0, qkv_here, 0, dense_w, 0, attn_here, 0)
    mlp_fetch = [
        Fetch(at < 3 * UNIT, fc1_w, at, hidden_here, qkv_here + at, fc2_w, at, hidden_here, attn_here + at)
        for at in range(0, hidden_here, UNIT)
    ]

    kinds = [0, 0, 0]
    keep = upper

    class Unit:
        def __init__(self, kind, at, width=UNIT):
            place, offset = kinds[kind] // UNIT, kinds[kind] % UNIT
            kinds[kind] += width
            if kind == 1:
                part, self.total = first_part, first_sum

                def held(ref, index):
                    return ref.at[index, :, :, pl.ds(offset, width)]

                self.arrived, self.other = held(first_in, place), held(first_other, place)
                self.slot = partial(held, first_slot)
                half = feats // 2
                self.whole = lambda: part.at[:, :, pl.ds(at, width)]

                def region(which, index):
                    return self.total.at[index, pl.ds(which * half, half), pl.ds(at, width)]

            else:
                part, self.total = second_part, second_sum
                self.arrived = second_in.at[place, :, pl.ds(offset, width)]
                self.other = second_other.at[place, :, pl.ds(offset // 2, width // 2)]
                self.slot = lambda index: second_slot.at[index, :, pl.ds(offset, width)]
                half = width // 2
                self.whole = lambda: part.at[:, pl.ds(at, width)]

                def region(which, index):
                    return self.total.at[index, pl.ds(at + which * half, half)]

            self.half, self.region = half, region
            every = slice(None)
            self.inward = copies.make(self.whole, lambda: self.arrived, to_in)
            self.across = copies.make(
                lambda: self.arrived.at[:, pl.ds((1 - keep) * half, half)],
                lambda: self.other,
                to_in,
            )
            self.spread = [
                copies.make(
                    partial(lambda j: self.other.at[peer[j]], j),
                    lambda: region(keep, r),
                    to_row[j],
                )
                for j in (1, 2, 3)
            ]
            self.over = copies.make(
                lambda: region(keep, every), lambda: region(keep, every), to_in
            )
            self.outward = [
                copies.make(lambda: region(keep, every), lambda: region(keep, every), to_out),
                copies.make(
                    lambda: region(1 - keep, every), lambda: region(1 - keep, every), to_out
                ),
            ]
            self.load, self.store = local_used[0], local_used[0] + 1
            local_used[0] += 2

        def loading(self, turn):
            return pltpu.make_async_copy(
                self.whole(), self.slot(turn % 2), local_sems.at[self.load]
            )

        def storing(self):
            return pltpu.make_async_copy(
                self.other.at[r], self.region(keep, r), local_sems.at[self.store]
            )

        def add(self, target, term, offset):
            step = 64

            def body(i, carry):
                here = pl.ds(pl.multiple_of(i * step, step), step)
                there = pl.ds(pl.multiple_of(offset + i * step, step), step)
                target[:, here] = (target[:, here].astype(F32) + term[:, there].astype(F32)).astype(BF16)
                return carry

            lax.fori_loop(0, target.shape[1] // step, body, 0)

        def sum_chip_pair(self, turn):
            self.loading(turn).wait()
            self.inward().wait_recv()
            self.add(self.arrived, self.slot(turn % 2), 0)
            self.across().start()

        def sum_line(self):
            self.across().wait_recv()
            self.add(self.other, self.arrived, keep * self.half)
            for copy in self.spread:
                copy().start()
            self.storing().start()

        def pass_kept(self):
            for copy in self.spread:
                copy().wait_recv()
            self.storing().wait()
            self.over().start()
            self.outward[0]().start()

        def pass_other(self):
            self.over().wait_recv()
            self.outward[1]().start()

        def finish(self, unsent):
            def edge():
                for copy in self.outward:
                    copy().wait_recv()
                if unsent:
                    self.inward().wait_send()

            def middle():
                for copy in [self.across, self.over] + self.spread + self.outward:
                    copy().wait_send()

            when(is_edge, edge)
            when(is_mid, middle)

    def chunk_units(at):
        width = UNIT // 2 if at in (0, hidden_here - UNIT) else UNIT
        parts = range(at, at + UNIT, width)
        return [Unit(2, attn_here + part, width) for part in parts] + [
            Unit(1, qkv_here + part, width) for part in parts
        ]

    mlp_units = [chunk_units(at) for at in range(0, hidden_here, UNIT)]
    attn_units = [Unit(2, 0)] + [Unit(1, at) for at in range(0, qkv_here, UNIT)]

    def norm_body(x_ref, one_ref, two_ref, stat_ref):
        wide = jnp.concatenate([x_ref[j, 0] for j in range(4)], axis=1).astype(F32)
        norms = jnp.concatenate([norm_all[j] for j in range(4)], axis=1)
        mean = jnp.sum(wide, axis=1, keepdims=True) / D
        square = jnp.sum(wide * wide, axis=1, keepdims=True) / D
        inv_std = lax.rsqrt(square - mean * mean + norm_epsilon)
        normed = (wide - mean) * inv_std
        one_ref[...] = (normed * norms[0:1] + norms[1:2]).astype(BF16)
        two_ref[...] = (normed * norms[2:3] + norms[3:4]).astype(BF16)
        lane = lax.broadcasted_iota(jnp.int32, stat_ref.shape, 1)
        stat_ref[...] = jnp.where(lane < 64, mean, inv_std)

    def norm_stage():
        tile = 256
        flat = pl.BlockSpec((tile, D), lambda i: (i, 0))
        pltpu.emit_pipeline(
            norm_body,
            grid=(rows // tile,),
            in_specs=[
                pl.BlockSpec(
                    (4, 1, tile, feats), lambda i: (0, i * tile // slab, i % (slab // tile), 0)
                )
            ],
            out_specs=[flat, flat, pl.BlockSpec((tile, 128), lambda i: (i, 0))],
        )(x_all, ln1, ln2, stats)

    def mlp_stage(k):
        at = k * UNIT
        bias = fc1_bias[r, :, at : at + UNIT]

        def body(ln_ref, cot_ref, first_ref, second_ref, act_ref, grad_ref):
            step = pl.program_id(0)

            @pl.when(step == 0)
            def _():
                acc[:, : 2 * UNIT, :] = jnp.zeros((4, 2 * UNIT, feats), F32)
                sum_acc[:, :UNIT] = jnp.zeros((8, UNIT), F32)

            hidden = bias
            grad_act = None
            for j in range(4):
                lanes = slice(j * feats, (j + 1) * feats)
                hidden = hidden + product(ln_ref[:, lanes], first_ref[j], ((1,), (0,)))
                term = product(cot_ref[j, 0], second_ref[j], ((1,), (1,)))
                grad_act = term if j == 0 else grad_act + term
            curve = 0.5 * (1.0 + lax.erf(hidden * math.sqrt(0.5)))
            bell = jnp.exp(-0.5 * hidden * hidden) * (1.0 / math.sqrt(2.0 * math.pi))
            act = (hidden * curve).astype(BF16)
            grad_hidden = (grad_act * (curve + hidden * bell)).astype(BF16)
            act_ref[...] = act
            grad_ref[...] = grad_hidden
            sum_acc[0:1, :UNIT] += jnp.sum(grad_hidden.astype(F32), axis=0, keepdims=True)
            for j in range(4):
                lanes = slice(j * feats, (j + 1) * feats)
                acc[j, :UNIT] += product(act, cot_ref[j, 0], ((0,), (0,)))
                acc[j, UNIT : 2 * UNIT] += product(grad_hidden, ln_ref[:, lanes], ((0,), (0,)))

        pltpu.emit_pipeline(
            body,
            grid=(rows // TILE,),
            in_specs=[
                pl.BlockSpec((TILE, D), lambda i: (i, 0)),
                pl.BlockSpec((4, 1, slab, feats), lambda i: (0, i, 0, 0)),
                pl.BlockSpec((4, feats, UNIT), lambda i: (0, 0, (qkv_here + at) // UNIT)),
                pl.BlockSpec((4, UNIT, feats), lambda i: (0, (attn_here + at) // UNIT, 0)),
            ],
            out_specs=[
                pl.BlockSpec((TILE, UNIT), lambda i: (i, (attn_here + at) // UNIT)),
                pl.BlockSpec((TILE, UNIT), lambda i: (i, (qkv_here + at) // UNIT)),
            ],
        )(ln2, cot_all, w1, w2, acts, grads)
        grad_stage(UNIT, qkv_here + at, attn_here + at, 1, k == 0)
        unit_sums[0:1, qkv_here + at : qkv_here + at + UNIT] = sum_acc[0:1, :UNIT]

    def grad_stage(width, first_at, second_at, which, fresh):
        def body(first_ref, part_one, part_two):
            j = pl.program_id(0)
            grad = acc[j, UNIT : UNIT + width].T
            weight = first_ref[0].astype(F32)
            part_one[0] = grad.astype(BF16)
            part_two[0] = acc[j, :UNIT].astype(BF16)
            terms = [fold_lanes(grad * weight), fold_lanes(weight * sum_acc[0:1, :width])]
            ones = jnp.ones((8, 128), F32)
            for k in (0, 1):
                sums = lax.dot_general(
                    ones,
                    terms[k],
                    (((1,), (1,)), ((), ())),
                    precision=lax.Precision.HIGHEST,
                    preferred_element_type=F32,
                )[0:1]
                at = 2 * which + k
                if not fresh:
                    sums = sums + small_part[j, at : at + 1]
                small_part[j, at : at + 1] = sums

        lanes = slice(first_at, first_at + width)
        block = pl.BlockSpec((1, feats, width), lambda j: (j, 0, 0))
        pltpu.emit_pipeline(
            body,
            grid=(4,),
            in_specs=[block],
            out_specs=[block, pl.BlockSpec((1, UNIT, feats), lambda j: (j, second_at // UNIT, 0))],
        )(w1.at[:, :, lanes], first_part.at[:, :, lanes], second_part)

    def attention_slab(s):
        once = pl.Buffered(1)
        heads = qkv_here // (3 * HD)
        bias = qkv_bias[r]

        def body(ln_ref, cot_ref, first_ref, second_ref, act_ref, grad_ref):
            qkv = bias
            back = None
            for j in range(4):
                lanes = slice(j * feats, (j + 1) * feats)
                qkv = qkv + product(ln_ref[:, lanes], first_ref[j], ((1,), (0,)))
                term = product(cot_ref[j, 0], second_ref[j], ((1,), (1,)))
                back = term if j == 0 else back + term
            back = back.astype(BF16)
            at = lax.broadcasted_iota(jnp.int32, (TILE, TILE), 0)
            of = lax.broadcasted_iota(jnp.int32, (TILE, TILE), 1)
            token = lax.broadcasted_iota(jnp.int32, (TILE, HD), 0)
            lane = lax.broadcasted_iota(jnp.int32, (TILE, HD), 1)
            begin = jnp.zeros((TILE, HD), jnp.int32)
            edge = 0
            for k in range(lengths.shape[1] - 1):
                edge = edge + lengths[4 * z + s, k]
                begin = jnp.where(token >= edge, edge, begin)
            allowed = (of <= at) & (of >= begin[:, :1])
            angle = (token - begin).astype(F32) * turns[0:1]
            cos, sin = jnp.cos(angle), jnp.sin(angle)
            low = jnp.where(lane < ROT // 2, -sin, 0.0)
            high = jnp.where(lane < ROT // 2, 0.0, sin)
            for h in range(heads):
                attn, grads_here = attention_head(
                    qkv[:, h * 3 * HD : (h + 1) * 3 * HD],
                    back[:, h * HD : (h + 1) * HD],
                    cos,
                    low,
                    high,
                    allowed,
                )
                act_ref[:, h * HD : (h + 1) * HD] = attn
                for i in range(3):
                    at_lane = (h * 3 + i) * HD
                    grad_ref[:, at_lane : at_lane + HD] = grads_here[i].astype(BF16)
            attn, grad = act_ref[...], grad_ref[...]
            sums = jnp.sum(grad.astype(F32), axis=0, keepdims=True)
            sum_acc[0:1, :qkv_here] = sums if s == 0 else sum_acc[0:1, :qkv_here] + sums
            for j in range(4):
                lanes = slice(j * feats, (j + 1) * feats)
                second_term = product(attn, cot_ref[j, 0], ((0,), (0,)))
                first_term = product(grad, ln_ref[:, lanes], ((0,), (0,)))
                acc[j, :UNIT] = second_term if s == 0 else acc[j, :UNIT] + second_term
                acc[j, UNIT:] = first_term if s == 0 else acc[j, UNIT:] + first_term

        pltpu.emit_pipeline(
            body,
            grid=(1,),
            in_specs=[
                pl.BlockSpec((TILE, D), lambda i: (s, 0), pipeline_mode=once),
                pl.BlockSpec((4, 1, slab, feats), lambda i: (0, s, 0, 0), pipeline_mode=once),
                pl.BlockSpec((4, feats, qkv_here), lambda i: (0, 0, 0), pipeline_mode=once),
                pl.BlockSpec((4, UNIT, feats), lambda i: (0, 0, 0), pipeline_mode=once),
            ],
            out_specs=[
                pl.BlockSpec((TILE, UNIT), lambda i: (s, 0), pipeline_mode=once),
                pl.BlockSpec((TILE, qkv_here), lambda i: (s, 0), pipeline_mode=once),
            ],
        )(
            ln1,
            cot_all,
            w1.at[:, :, :qkv_here],
            w2,
            acts,
            grads.at[:, :qkv_here],
        )
        if s == 3:
            grad_stage(qkv_here, 0, 0, 0, True)
            unit_sums[0:1, :qkv_here] = sum_acc[0:1, :qkv_here]

    def out_stage(n):
        def body(act_ref, second_ref, part_ref):
            part_ref[0] = product(act_ref[...], second_ref[0], ((1,), (0,))).astype(BF16)

        pltpu.emit_pipeline(
            body,
            grid=(rows // TILE,),
            in_specs=[
                pl.BlockSpec((TILE, acts.shape[1]), lambda i: (i, 0)),
                pl.BlockSpec((1, w2.shape[1], feats), lambda i: (n, 0, 0)),
            ],
            out_specs=[pl.BlockSpec((1, TILE, feats), lambda i: (n, i, 0))],
        )(acts, w2, out_part)

    def dx_stage(n):
        def body(grad_ref, first_ref, part_ref):
            norms = norm_all[n]
            one = product(grad_ref[:, :qkv_here], first_ref[0, :, :qkv_here], ((1,), (1,)))
            two = product(grad_ref[:, qkv_here:], first_ref[0, :, qkv_here:], ((1,), (1,)))
            part_ref[0] = (one * norms[0:1] + two * norms[2:3]).astype(BF16)

        pltpu.emit_pipeline(
            body,
            grid=(rows // TILE,),
            in_specs=[
                pl.BlockSpec((TILE, grads.shape[1]), lambda i: (i, 0)),
                pl.BlockSpec((1, feats, w1.shape[2]), lambda i: (n, 0, 0)),
            ],
            out_specs=[pl.BlockSpec((1, TILE, feats), lambda i: (n, i, 0))],
        )(grads, w1, dx_part)

    class Scatter:
        def __init__(self, part, from_core, chip, from_x, half, from_y):
            self.part, self.from_core, self.chip = part, from_core, chip
            self.from_x, self.half, self.from_y = from_x, half, from_y
            self.to_core = [
                copies.make(
                    partial(lambda j: part.at[peer[j]], j),
                    partial(lambda j: from_core.at[peer[j] // 2], j),
                    to_row[1],
                )
                for j in (1, 3)
            ]
            self.to_x = copies.make(
                lambda: chip.at[:, far_half], lambda: from_x, to_col
            )
            self.to_y = copies.make(lambda: half.at[1 - y], lambda: from_y, to_row[2])

        def begin(self):
            for copy in self.to_core:
                start(copy)

        def second(self):
            for copy in self.to_core:
                copy().wait_recv()

            def body(left, right, target):
                target[...] = (left[...].astype(F32) + right[...].astype(F32)).astype(BF16)

            block = pl.BlockSpec((1, TILE, feats), lambda s, i: (s, i, 0))
            pltpu.emit_pipeline(
                body,
                grid=(2, rows // TILE),
                in_specs=[
                    pl.BlockSpec((1, TILE, feats), lambda s, i: (2 * s + core, i, 0)),
                    block,
                ],
                out_specs=[block],
            )(self.part, self.from_core, self.chip)
            start(self.to_x)

        def third(self):
            self.to_x().wait_recv()

            def body(left, right, target):
                target[...] = (left[...].astype(F32) + right[...].astype(F32)).astype(BF16)

            block = pl.BlockSpec((1, TILE, feats), lambda s, i: (s, i, 0))
            tiles = own_rows // TILE
            pltpu.emit_pipeline(
                body,
                grid=(2, tiles),
                in_specs=[
                    pl.BlockSpec((1, TILE, feats), lambda s, i: (s, c * tiles + i, 0)),
                    block,
                ],
                out_specs=[block],
            )(self.chip, self.from_x, self.half)
            start(self.to_y)

        def last(self, body, extra, target):
            self.to_y().wait_recv()
            flat = pl.BlockSpec((1, slab, feats), lambda i: (i, 0, 0))
            pltpu.emit_pipeline(
                body,
                grid=(own_rows // TILE,),
                in_specs=[
                    pl.BlockSpec((1, TILE, feats), lambda i: (y, i, 0)),
                    pl.BlockSpec((TILE, feats), lambda i: (i, 0)),
                    flat,
                ],
                out_specs=[flat],
            )(self.half, self.from_y, extra, target)

    out_scatter = Scatter(out_part, out_core, out_chip, out_x, out_half, out_y)
    dx_scatter = Scatter(dx_part, dx_core, dx_chip, dx_x, dx_half, dx_y)
    out_route = Route(
        out_item, dealt, out_up, out_down, out_far, out_send, out_edge, output
    )

    def finish_output():
        def body(half_ref, y_ref, x_ref, item_ref):
            item_ref[0] = (
                half_ref[0].astype(F32)
                + y_ref[...].astype(F32)
                + x_ref[0].astype(F32)
                + out_bias[0:1]
            ).astype(BF16)

        out_scatter.last(body, x_own, out_item)

    row_copies = [
        copies.make(lambda: row_part, lambda: row_sums.at[r], to_row[j]) for j in (1, 2, 3)
    ]

    def sum_grad():
        dx_scatter.to_y().wait_recv()

        def body(half_ref, y_ref, x_ref, stat_ref, target_ref):
            grad = half_ref[0].astype(F32) + y_ref[...].astype(F32)
            target_ref[...] = grad
            normed = (x_ref[0].astype(F32) - stat_ref[:, :1]) * stat_ref[:, 127:]
            one = jnp.sum(grad, axis=1, keepdims=True)
            two = jnp.sum(grad * normed, axis=1, keepdims=True)
            lane = lax.broadcasted_iota(jnp.int32, (TILE, 128), 1)
            both = jnp.where(lane == 0, one, jnp.where(lane == 1, two, 0.0))
            row_part[pl.program_id(0)] = both.T[:8]

        pltpu.emit_pipeline(
            body,
            grid=(own_rows // TILE,),
            in_specs=[
                pl.BlockSpec((1, TILE, feats), lambda i: (y, i, 0)),
                pl.BlockSpec((TILE, feats), lambda i: (i, 0)),
                pl.BlockSpec((1, slab, feats), lambda i: (i, 0, 0)),
                pl.BlockSpec((TILE, 128), lambda i: (slabs * c + i, 0)),
            ],
            out_specs=[pl.BlockSpec((TILE, feats), lambda i: (i, 0))],
        )(dx_half, dx_y, x_own, stats, grad_norm)
        for copy in row_copies:
            start(copy)
        row_sums[r] = row_part[...]

    def finish_grad():
        for copy in row_copies:
            copy().wait_recv()

        def body(grad_ref, cot_ref, x_ref, stat_ref, target_ref):
            step = pl.program_id(0)
            sums = row_sums[0, step] + row_sums[1, step] + row_sums[2, step] + row_sums[3, step]
            sums = jnp.concatenate([sums, jnp.zeros((120, TILE), F32)], axis=0).T * (1.0 / D)
            normed = (x_ref[0].astype(F32) - stat_ref[:, :1]) * stat_ref[:, 127:]
            target_ref[0] = cot_ref[0].astype(F32) + stat_ref[:, 127:] * (
                grad_ref[...] - sums[:, 0:1] - normed * sums[:, 1:2]
            )

        flat = pl.BlockSpec((1, slab, feats), lambda i: (i, 0, 0))
        pltpu.emit_pipeline(
            body,
            grid=(own_rows // TILE,),
            in_specs=[
                pl.BlockSpec((TILE, feats), lambda i: (i, 0)),
                flat,
                flat,
                pl.BlockSpec((TILE, 128), lambda i: (slabs * c + i, 0)),
            ],
            out_specs=[flat],
        )(grad_norm, cot_own, x_own, stats, input_grad)

    sums_wide = small_units.shape[2]
    small_copies = [
        copies.make(
            partial(lambda j: small_part.at[peer[j]], j), lambda: small_row.at[r], to_row[j]
        )
        for j in (1, 2, 3)
    ]
    unit_copies = [
        copies.make(lambda: unit_sums, lambda: small_units.at[r], to_row[j]) for j in (1, 2, 3)
    ]
    col_copy = copies.make(
        lambda: small_here.at[:, pl.ds(sums_wide, feats)], lambda: small_col, to_col
    )
    small_inward = copies.make(lambda: small_here, lambda: small_in, to_in)
    small_across = copies.make(lambda: small_half, lambda: small_other, to_in)
    small_outward = copies.make(lambda: small_in, lambda: small_in, to_out)

    def small_begin():
        small_part[:, 4:] = jnp.zeros((4, 4, feats), F32)
        for copy in small_copies + unit_copies:
            start(copy)
        small_row[r] = small_part[r]
        small_units[r] = unit_sums[...]

    def small_second():
        for copy in small_copies + unit_copies:
            copy().wait_recv()
        small_here[...] = jnp.zeros(small_here.shape, F32)
        for j in range(4):
            small_here[j : j + 1, :sums_wide] = small_units[j, 0:1]
        small_here[:, sums_wide:] = small_row[0] + small_row[1] + small_row[2] + small_row[3]

        def body(cot_ref):
            total = jnp.sum(cot_ref[0].astype(F32), axis=0, keepdims=True)
            small_here[4:5, sums_wide:] += total

        pltpu.emit_pipeline(
            body,
            grid=(slabs,),
            in_specs=[pl.BlockSpec((1, slab, feats), lambda i: (i, 0, 0))],
        )(cot_own)
        start(col_copy)

    def small_third():
        col_copy().wait_recv()
        col_copy().wait_send()
        small_here[:, sums_wide:] += small_col[...]
        when(is_edge, lambda: small_inward().start())

    def small_halve():
        def middle():
            small_inward().wait_recv()
            small_half[...] = small_here[...] + small_in[...]
            small_across().start()

        when(is_mid, middle)

    def small_close():
        def middle():
            small_across().wait_recv()
            small_in[...] = small_half[...] + small_other[...]
            small_outward().start()

        when(is_mid, middle)

    def small_finish():
        def edge():
            small_outward().wait_recv()
            small_inward().wait_send()

        def middle():
            small_across().wait_send()
            small_outward().wait_send()

        when(is_edge, edge)
        when(is_mid, middle)
        total = small_in[...]
        small_sum[:, :sums_wide] = total[:, :sums_wide]
        norms = norm_own[...]
        sums = total[:, sums_wide:]
        gains = [
            (sums[k : k + 1] - norms[k + 1 : k + 2] * sums[k + 1 : k + 2]) / norms[k : k + 1]
            for k in (0, 2)
        ]
        small_sum[:, sums_wide:] = jnp.concatenate(
            [gains[0], sums[1:2], gains[1], sums[3:4], sums[4:]], axis=0
        )

    line = []
    begun, loaded, served = [0], [0], [0]
    flight = 2

    def lead():
        while begun[0] < min(len(line), served[0] + 2):
            at = begun[0]

            def edge():
                if at >= flight:
                    line[at - flight].inward().wait_send()
                line[at].inward().start()

            when(is_edge, edge)
            begun[0] += 1
        while loaded[0] < min(len(line), served[0] + 2):
            at = loaded[0]
            when(is_mid, lambda: line[at].loading(at).start())
            loaded[0] += 1

    def queue(units):
        line.extend(units)
        lead()

    def serve(count, closing=False):
        for _ in range(count):
            at = served[0]
            if at >= len(line) and not closing:
                return
            lead()

            def middle():
                if 0 <= at - 3 < len(line):
                    line[at - 3].pass_other()
                if 0 <= at - 2 < len(line):
                    line[at - 2].pass_kept()
                if 0 <= at - 1 < len(line):
                    line[at - 1].sum_line()
                if at < len(line):
                    line[at].sum_chip_pair(at)

            when(is_mid, middle)
            served[0] += 1
            lead()

    slab_ids = range(slabs)
    for q in slab_ids:
        x_gather.begin(q)
    cot_route.begin(0)
    norm_all[r] = norm_own[...]
    for copy in norm_copies:
        start(copy)
    cot_route.relay(0)
    cot_route.begin(1)
    for q in slab_ids:
        x_gather.after_y(q)
    mlp_fetch[0].begin()
    cot_route.relay(1)
    cot_route.hand_out(0)
    for q in slab_ids:
        x_gather.after_x(q)
    cot_route.take(0)
    cot_gather.begin(0)
    cot_route.hand_out(1)
    mlp_fetch[0].share()
    for q in slab_ids:
        x_gather.after_far(q)
    cot_route.take(1)
    cot_gather.begin(1)
    mlp_fetch[1].begin()
    cot_gather.after_y(0)
    cot_gather.after_x(0)
    cot_gather.after_y(1)
    cot_gather.after_x(1)
    for q in slab_ids:
        x_gather.end(q)
    for copy in norm_copies:
        copy().wait_recv()
    mlp_fetch[1].share()
    norm_stage()
    for q in slab_ids:
        cot_gather.after_far(q)
    mlp_fetch[2].begin()
    for q in slab_ids:
        cot_gather.end(q)
    mlp_fetch[0].end()
    mlp_stage(0)
    queue(mlp_units[0])
    mlp_fetch[2].share()
    attn_fetch.begin()
    mlp_fetch[1].end()
    mlp_stage(1)
    queue(mlp_units[1])
    serve(1)
    mlp_fetch[2].end()
    mlp_stage(2)
    mlp_fetch[3].begin()
    queue(mlp_units[2])
    serve(2)
    attn_fetch.end()
    attention_slab(0)
    serve(1)
    attention_slab(1)
    serve(1)
    attention_slab(2)
    serve(1)
    attention_slab(3)
    queue(attn_units)
    serve(1)
    mlp_fetch[3].end()
    mlp_stage(3)
    queue(mlp_units[3])
    serve(1)
    out_stage(0)
    out_stage(1)
    serve(1)
    out_stage(2)
    out_stage(3)
    out_scatter.begin()
    serve(1)
    dx_stage(0)
    out_scatter.second()
    dx_stage(1)
    serve(1)
    dx_stage(2)
    dx_stage(3)
    serve(1)
    small_begin()
    out_scatter.third()
    dx_scatter.begin()
    small_second()
    serve(1)
    finish_output()
    out_route.begin(0)
    dx_scatter.second()
    small_third()
    serve(1)
    out_route.relay(0)
    out_route.begin(1)
    small_halve()
    serve(1)
    out_route.relay(1)
    out_route.hand_out(0)
    serve(1)
    small_close()
    dx_scatter.third()
    serve(1)
    out_route.hand_out(1)
    serve(1)
    sum_grad()
    serve(1, True)
    out_route.take(0)
    finish_grad()
    serve(1, True)
    out_route.take(1)
    while served[0] < len(line) + 3:
        serve(1, True)
    for at, unit in enumerate(line):
        unit.finish(at >= len(line) - flight)
    small_finish()
    cot_route.finish()
    out_route.finish()
    for copy in sent:
        if copy is not col_copy:
            copy().wait_send()


def widen_body(first_ref, dense_ref, fc2_ref, qkv_out, fc1_out, dense_out, fc2_out):
    qkv_here = qkv_out.shape[1]
    qkv_out[...] = first_ref[0, :, :qkv_here].astype(F32)
    fc1_out[...] = first_ref[0, :, qkv_here:].astype(F32)
    dense_out[...] = dense_ref[0].astype(F32)
    fc2_out[...] = fc2_ref[0].astype(F32)


def widen(first_sum, second_sum, qkv_here, attn_here):
    feats, first_cols = first_sum.shape[1:]
    hidden_here = first_cols - qkv_here
    tiles = hidden_here // attn_here
    tile = feats // tiles
    return pl.pallas_call(
        widen_body,
        grid=(4, tiles),
        in_specs=[
            pl.BlockSpec((1, tile, first_cols), lambda s, i: (s, i, 0)),
            pl.BlockSpec((1, attn_here // tiles, feats), lambda s, i: (s, i, 0)),
            pl.BlockSpec((1, attn_here, feats), lambda s, i: (s, 1 + i, 0)),
        ],
        out_specs=[
            pl.BlockSpec((tile, qkv_here), lambda s, i: (i, s)),
            pl.BlockSpec((tile, hidden_here), lambda s, i: (i, s)),
            pl.BlockSpec((attn_here // tiles, feats), lambda s, i: (s * tiles + i, 0)),
            pl.BlockSpec((attn_here, feats), lambda s, i: (s * tiles + i, 0)),
        ],
        out_shape=[
            jax.ShapeDtypeStruct((feats, 4 * qkv_here), F32),
            jax.ShapeDtypeStruct((feats, 4 * hidden_here), F32),
            jax.ShapeDtypeStruct((4 * attn_here, feats), F32),
            jax.ShapeDtypeStruct((4 * hidden_here, feats), F32),
        ],
        compiler_params=pltpu.CompilerParams(vmem_limit_bytes=32 * 1024 * 1024),
    )(first_sum, second_sum, second_sum)


def dealt_layer(
    layer_input,
    lengths,
    deal_table,
    ln1_gain,
    ln1_bias,
    qkv_weight,
    qkv_bias,
    dense_weight,
    dense_bias,
    ln2_gain,
    ln2_bias,
    fc1_weight,
    fc1_bias,
    fc2_weight,
    fc2_bias,
    cotangent,
):
    own_rows, feats = layer_input.shape
    rows = 2 * own_rows
    slab = own_rows // 2
    qkv_cols = qkv_weight.shape[1]
    qkv_here = qkv_cols // 4
    attn_here = dense_weight.shape[0] // 4
    hidden_cols = fc1_weight.shape[1]
    hidden_here = hidden_cols // 4
    first_cols = qkv_here + hidden_here
    second_rows = attn_here + hidden_here

    norms = jnp.stack([ln1_gain, ln1_bias, ln2_gain, ln2_bias] * 2)
    out_bias = (dense_bias + fc2_bias).reshape(1, feats)
    turns = 1.0 / 10000.0 ** (np.arange(0, ROT, 2) / ROT)
    turns = np.concatenate([turns, turns, np.zeros(HD - ROT)])
    turns = np.broadcast_to(turns.astype(np.float32), (8, HD))

    low = lambda *shape: jax.ShapeDtypeStruct(shape, BF16)
    wide = lambda *shape: jax.ShapeDtypeStruct(shape, F32)
    first = low(4, feats, first_cols)
    second = low(4, second_rows, feats)
    item = low(2, slab, feats)
    small_shape = (8, first_cols + feats)
    outputs = [first, second, item, wide(2, slab, feats)]
    scatter = [
        low(4, rows, feats),
        low(2, rows, feats),
        low(2, rows, feats),
        low(2, own_rows, feats),
        low(2, own_rows, feats),
        low(own_rows, feats),
    ]
    buffers = (
        [wide(own_rows, feats), item, wide(rows, 128)]
        + [low(4, 4, slab, feats)] * 2
        + [low(rows, D)] * 2
        + [first, second, low(rows, second_rows), low(rows, first_cols)]
        + [first, second]
        + scatter
        + [item]
        + scatter
        + [item] * 10
    )
    any_space = pl.BlockSpec(memory_space=pl.ANY)
    vmem = pl.BlockSpec(memory_space=pltpu.VMEM)
    smem = pl.BlockSpec(memory_space=pltpu.SMEM)
    copies = 250
    first_units, second_units = first_cols // UNIT, second_rows // UNIT
    results = pl.pallas_call(
        layer_kernel,
        in_specs=[smem] * 2 + [any_space] * 2 + [vmem] * 5 + [any_space] * 4,
        out_specs=[any_space] * 4 + [vmem] + [any_space] * len(buffers),
        out_shape=outputs + [wide(*small_shape)] + buffers,
        scratch_shapes=[
            pltpu.VMEM((4, UNIT + qkv_here, feats), F32),
            pltpu.VMEM((4, 8, feats), F32),
            pltpu.VMEM((first_units, 4, feats, UNIT), BF16),
            pltpu.VMEM((second_units, 4, UNIT, feats), BF16),
            pltpu.VMEM((first_units, 4, feats // 2, UNIT), BF16),
            pltpu.VMEM((second_units, 4, UNIT // 2, feats), BF16),
            pltpu.VMEM((2, 4, feats, UNIT), BF16),
            pltpu.VMEM((2, 4, UNIT, feats), BF16),
            pltpu.VMEM((8, qkv_here), F32),
            pltpu.VMEM((8, first_cols), F32),
            pltpu.VMEM((4, 8, feats), F32),
            pltpu.VMEM((4, 8, feats), F32),
            pltpu.VMEM((4, 8, first_cols), F32),
            pltpu.VMEM((8, feats), F32),
            pltpu.VMEM(small_shape, F32),
            pltpu.VMEM(small_shape, F32),
            pltpu.VMEM(small_shape, F32),
            pltpu.VMEM(small_shape, F32),
            pltpu.VMEM((2, 8, slab), F32),
            pltpu.VMEM((4, 2, 8, slab), F32),
            pltpu.SemaphoreType.DMA((copies,)),
            pltpu.SemaphoreType.DMA((copies,)),
            pltpu.SemaphoreType.DMA((96,)),
        ],
        compiler_params=pltpu.CompilerParams(
            collective_id=0, has_side_effects=True, vmem_limit_bytes=60 * 1024 * 1024
        ),
        cost_estimate=pl.CostEstimate(
            flops=6 * rows * D * (first_cols + second_rows),
            bytes_accessed=200 * 1024 * 1024,
            transcendentals=rows * hidden_here,
        ),
    )(
        lengths,
        deal_table,
        layer_input.reshape(2, slab, feats),
        cotangent.reshape(2, slab, feats),
        norms,
        qkv_bias.reshape(4, 1, qkv_here),
        fc1_bias.reshape(4, 1, hidden_here),
        out_bias,
        turns,
        qkv_weight,
        dense_weight,
        fc1_weight,
        fc2_weight,
    )
    first_sum, second_sum, output, input_grad, small = results[:5]
    qkv_grad, fc1_grad, dense_grad, fc2_grad = widen(first_sum, second_sum, qkv_here, attn_here)
    norm_sums = small[:5, first_cols:]
    return (
        output.reshape(own_rows, feats),
        input_grad.reshape(own_rows, feats),
        norm_sums[0],
        norm_sums[1],
        qkv_grad,
        small[:4, :qkv_here].reshape(qkv_cols),
        dense_grad,
        norm_sums[4],
        norm_sums[2],
        norm_sums[3],
        fc1_grad,
        small[:4, qkv_here:first_cols].reshape(hidden_cols),
        fc2_grad,
        norm_sums[4],
    )


def solution(mesh):
    grid = tuple(mesh.shape[axis] for axis in ("dp", "row", "col"))
    placed = (
        P(("dp", "col"), "row"),
        P(),
        P(),
        P("row"),
        P("row"),
        P("row", "col"),
        P("col"),
        P("col", "row"),
        P("row"),
        P("row"),
        P("row"),
        P("row", "col"),
        P("col"),
        P("col", "row"),
        P("row"),
        P(("dp", "col"), "row"),
    )
    return jax.shard_map(
        dealt_layer if grid == (4, 4, 2) else local,
        mesh=mesh,
        in_specs=placed,
        out_specs=(
            P(("dp", "col"), "row"),
            P(("dp", "col"), "row"),
            P("row"),
            P("row"),
            P("row", "col"),
            P("col"),
            P("col", "row"),
            P("row"),
            P("row"),
            P("row"),
            P("row", "col"),
            P("col"),
            P("col", "row"),
            P("row"),
        ),
        check_vma=False,
    )
```

```python
from functools import partial
import math

import jax
import jax.numpy as jnp
import numpy as np
from jax import lax
from jax.experimental import pallas as pl
from jax.experimental.pallas import tpu as pltpu
from jax.sharding import PartitionSpec as P

D = 2048
HD = 128
ROT = 32
QBLK = 512
CHUNK = 256
BF16 = jnp.bfloat16
F32 = jnp.float32


norm_epsilon = 1e-05
masked_score = -1000000000.0


def rotary_tables(positions):
    frequency = 1.0 / 10000.0 ** (jnp.arange(0, ROT, 2, dtype=jnp.float32) / ROT)
    angles = positions.astype(jnp.float32)[:, None] * frequency[None, :]
    angles = jnp.concatenate([angles, angles], axis=1)
    return (jnp.cos(angles), jnp.sin(angles))


def rotate(values, cos_table, sin_table):
    half_rot = ROT // 2
    rotated = values[..., :ROT]
    turned = jnp.concatenate([-rotated[..., half_rot:], rotated[..., :half_rot]], axis=-1)
    rotated = rotated * cos_table[:, None, :] + turned * sin_table[:, None, :]
    return jnp.concatenate([rotated, values[..., ROT:]], axis=-1)


def segment_layout(seq_lengths, length):
    seq_ends = jnp.cumsum(seq_lengths)
    token_place = jnp.arange(length, dtype=jnp.int32)
    sequence_ids = jnp.sum((token_place[:, None] >= seq_ends[None, :]).astype(jnp.int32), axis=1)
    starts = seq_ends - seq_lengths
    seq_hits = sequence_ids[:, None] == jnp.arange(seq_lengths.shape[0], dtype=jnp.int32)[None, :]
    seq_begin = jnp.sum(jnp.where(seq_hits, starts[None, :], 0), axis=1)
    return (sequence_ids, token_place - seq_begin)


def contract_rows(left_side, right_side):
    return lax.dot_general(
        left_side, right_side, (((0,), (0,)), ((), ())), preferred_element_type=jnp.float32
    )


def contract_cols(left_side, right_side):
    return lax.dot_general(
        left_side, right_side, (((1,), (1,)), ((), ())), preferred_element_type=jnp.float32
    )


def pick_rows(pooled, chosen):
    row_hits = chosen[None, :] == jnp.arange(pooled.shape[0], dtype=jnp.int32)[:, None]
    return jnp.sum(jnp.where(row_hits[:, :, None], pooled.astype(jnp.float32), 0.0), axis=0)


def local(
    layer_input,
    lengths,
    deal_table,
    ln1_gain,
    ln1_bias,
    qkv_weight,
    qkv_bias,
    dense_weight,
    dense_bias,
    ln2_gain,
    ln2_bias,
    fc1_weight,
    fc1_bias,
    fc2_weight,
    fc2_bias,
    cotangent,
):
    dp_count = lax.axis_size("dp")
    row_count = lax.axis_size("row")
    col_count = lax.axis_size("col")
    group_id = lax.axis_index("dp")
    row_id = lax.axis_index("row")
    col_id = lax.axis_index("col")
    own_rows, own_feats = layer_input.shape
    group_rows = own_rows * col_count
    slab_rows = group_rows // row_count
    qkv_cols = qkv_weight.shape[1]
    attn_cols = dense_weight.shape[0]
    heads_here = qkv_cols // (3 * HD)
    score_scale = 1.0 / math.sqrt(HD)
    local_slab = (col_id * own_rows + jnp.arange(own_rows, dtype=jnp.int32)) // slab_rows
    slab_hits = local_slab[:, None] == jnp.arange(row_count, dtype=jnp.int32)[None, :]
    deal_here = lax.dynamic_index_in_dim(deal_table, group_id, 1, keepdims=False)
    source = jnp.sum(jnp.where(slab_hits, deal_here[None, :], 0), axis=1)
    pooled = lax.all_gather(layer_input, "dp", axis=0, tiled=True).reshape(
        dp_count, own_rows, own_feats
    )
    mine_rows = pick_rows(pooled, source).astype(jnp.bfloat16)
    input_all = lax.all_gather(mine_rows, "col", axis=0, tiled=True)
    input_wide = input_all.astype(jnp.float32)
    row_stats = lax.psum(
        (jnp.sum(input_wide, axis=1), jnp.sum(input_wide * input_wide, axis=1)), "row"
    )
    row_mean = row_stats[0] / D
    inv_std = lax.rsqrt(row_stats[1] / D - row_mean * row_mean + norm_epsilon)
    normed = (input_wide - row_mean[:, None]) * inv_std[:, None]
    own_start = col_id * own_rows
    normed_own = lax.dynamic_slice_in_dim(normed, own_start, own_rows, 0)
    inv_std_own = lax.dynamic_slice_in_dim(inv_std, own_start, own_rows, 0)
    ln1_all = (normed * ln1_gain + ln1_bias).astype(jnp.bfloat16)
    ln2_all = (normed * ln2_gain + ln2_bias).astype(jnp.bfloat16)
    part_one = ln1_all
    part_two = ln2_all
    first_sums = lax.psum_scatter(
        jnp.concatenate(
            [
                jnp.dot(part_one, qkv_weight, preferred_element_type=jnp.float32),
                jnp.dot(part_two, fc1_weight, preferred_element_type=jnp.float32),
            ],
            axis=1,
        ),
        "row",
        scatter_dimension=0,
        tiled=True,
    )
    qkv_out = first_sums[:, :qkv_cols] + qkv_bias
    hidden = first_sums[:, qkv_cols:] + fc1_bias
    slab_source = (
        lax.dynamic_index_in_dim(deal_here, row_id, 0, keepdims=False) * row_count + row_id
    )
    seq_lengths = lax.dynamic_index_in_dim(lengths, slab_source, 0, keepdims=False)
    sequence_ids, positions = segment_layout(seq_lengths, slab_rows)
    token_place = jnp.arange(slab_rows, dtype=jnp.int32)
    cos_table, sin_table = rotary_tables(positions)
    packed = qkv_out.reshape(slab_rows, heads_here, 3, HD)
    query_pre = packed[:, :, 0]
    key_pre = packed[:, :, 1]
    queries = rotate(query_pre, cos_table, sin_table).astype(jnp.bfloat16)
    keys_rot = rotate(key_pre, cos_table, sin_table).astype(jnp.bfloat16)
    values = packed[:, :, 2].astype(jnp.bfloat16)

    def block_scores(block_id):
        first_row = block_id * QBLK
        last_row = first_row + QBLK
        allowed = (sequence_ids[first_row:last_row, None] == sequence_ids[None, :last_row]) & (
            token_place[None, :last_row] <= token_place[first_row:last_row, None]
        )
        scores = (
            jnp.einsum("qhd,khd->hqk", queries, keys_rot, preferred_element_type=jnp.float32)
            * score_scale
        )
        return jnp.where(allowed[None], scores, masked_score)

    block_id = 0
    last_row = (block_id + 1) * QBLK
    scores = block_scores(block_id)
    row_top = jnp.max(scores, axis=-1, keepdims=True)
    exp_total = jnp.sum(jnp.exp(scores - row_top), axis=-1, keepdims=True)
    log_total = row_top + jnp.log(exp_total)
    probs_low = jnp.exp(scores - log_total).astype(jnp.bfloat16)
    mixtures = jnp.einsum("hqk,khd->qhd", probs_low, values, preferred_element_type=jnp.float32)
    log_totals = [log_total]
    attn_out = mixtures.reshape(slab_rows, attn_cols).astype(jnp.bfloat16)
    activated = jax.nn.gelu(hidden, approximate=False).astype(jnp.bfloat16)
    attn_all, act_all = (
        lax.all_gather(attn_out, "row", axis=0, tiled=True),
        lax.all_gather(activated, "row", axis=0, tiled=True),
    )
    part_one = attn_all
    part_two = act_all
    branch_sum = lax.psum_scatter(
        jnp.dot(part_one, dense_weight, preferred_element_type=jnp.float32)
        + jnp.dot(part_two, fc2_weight, preferred_element_type=jnp.float32),
        "col",
        scatter_dimension=0,
        tiled=True,
    )
    output = (mine_rows.astype(jnp.float32) + branch_sum + dense_bias + fc2_bias).astype(
        jnp.bfloat16
    )
    grad_all = lax.all_gather(cotangent, "col", axis=0, tiled=True)
    dense_grad = contract_rows(attn_all, grad_all)
    fc2_grad = contract_rows(act_all, grad_all)
    out_bias_grad = jnp.sum(grad_all, axis=0, dtype=jnp.float32)
    grad_block = grad_all
    grad_second = lax.psum_scatter(
        jnp.concatenate(
            [contract_cols(grad_block, dense_weight), contract_cols(grad_block, fc2_weight)], axis=1
        ),
        "row",
        scatter_dimension=0,
        tiled=True,
    )
    grad_mix = grad_second[:, :attn_cols].astype(jnp.bfloat16).reshape(slab_rows, heads_here, HD)
    gelu_back = jax.vjp(partial(jax.nn.gelu, approximate=False), hidden)[1]
    grad_hidden = gelu_back(grad_second[:, attn_cols:])[0]
    grad_key = jnp.zeros((slab_rows, heads_here, HD), jnp.float32)
    grad_value = jnp.zeros((slab_rows, heads_here, HD), jnp.float32)
    block_id = 0
    first_row = block_id * QBLK
    last_row = first_row + QBLK
    probs_full = jnp.exp(block_scores(block_id) - log_totals[block_id])
    probs_low = probs_full.astype(jnp.bfloat16)
    grad_block = grad_mix
    grad_value = grad_value.at[:last_row].add(
        jnp.einsum("hqk,qhd->khd", probs_low, grad_block, preferred_element_type=jnp.float32)
    )
    grad_probs = jnp.einsum("qhd,khd->hqk", grad_block, values, preferred_element_type=jnp.float32)
    centre = jnp.sum(probs_full * grad_probs, axis=-1, keepdims=True)
    grad_scores = (probs_full * (grad_probs - centre)).astype(jnp.bfloat16)
    grad_queries = (
        jnp.einsum("hqk,khd->qhd", grad_scores, keys_rot, preferred_element_type=jnp.float32)
        * score_scale
    )
    grad_key = grad_key.at[:last_row].add(
        jnp.einsum("hqk,qhd->khd", grad_scores, queries, preferred_element_type=jnp.float32)
        * score_scale
    )
    turn_back = jax.vjp(lambda values_in: rotate(values_in, cos_table, sin_table), query_pre)[1]
    grad_query_pre = turn_back(grad_queries)[0]
    grad_key_pre = turn_back(grad_key)[0]
    grad_qkv = jnp.stack([grad_query_pre, grad_key_pre, grad_value], axis=2).reshape(
        slab_rows, qkv_cols
    )
    grad_first = jnp.concatenate([grad_qkv, grad_hidden], axis=1).astype(jnp.bfloat16)
    grad_first_all = lax.all_gather(grad_first, "row", axis=0, tiled=True)
    grad_qkv_all = grad_first_all[:, :qkv_cols]
    grad_hidden_all = grad_first_all[:, qkv_cols:]
    qkv_weight_grad = contract_rows(ln1_all, grad_qkv_all)
    qkv_bias_grad = jnp.sum(grad_qkv_all, axis=0, dtype=jnp.float32)
    fc1_weight_grad = contract_rows(ln2_all, grad_hidden_all)
    fc1_bias_grad = jnp.sum(grad_hidden_all, axis=0, dtype=jnp.float32)
    grad_block = grad_first_all
    summed = lax.psum_scatter(
        jnp.concatenate(
            [
                contract_cols(grad_block[:, :qkv_cols], qkv_weight),
                contract_cols(grad_block[:, qkv_cols:], fc1_weight),
            ],
            axis=1,
        ),
        "col",
        scatter_dimension=0,
        tiled=True,
    )
    grad_ln_one = summed[:, :own_feats]
    grad_ln_two = summed[:, own_feats:]
    gain_terms = (
        jnp.sum(grad_ln_one * normed_own, axis=0),
        jnp.sum(grad_ln_one, axis=0),
        jnp.sum(grad_ln_two * normed_own, axis=0),
        jnp.sum(grad_ln_two, axis=0),
    )
    grad_normed = grad_ln_one * ln1_gain + grad_ln_two * ln2_gain
    row_sums = lax.psum(
        (jnp.sum(grad_normed, axis=1), jnp.sum(grad_normed * normed_own, axis=1)), "row"
    )
    grad_dealt = cotangent.astype(jnp.float32) + inv_std_own[:, None] * (
        grad_normed - row_sums[0][:, None] / D - normed_own * row_sums[1][:, None] / D
    )
    gain_sums = lax.psum(
        (gain_terms[0], gain_terms[1], gain_terms[2], gain_terms[3]), ("dp", "col")
    )
    weights_summed = lax.psum(
        (
            qkv_weight_grad,
            qkv_bias_grad,
            dense_grad,
            fc1_weight_grad,
            fc1_bias_grad,
            fc2_grad,
            out_bias_grad,
        ),
        "dp",
    )
    pool_back = lax.all_gather(grad_dealt, "dp", axis=0, tiled=True).reshape(
        dp_count, own_rows, own_feats
    )
    back_here = jnp.sum(
        jnp.where(deal_table == group_id, jnp.arange(dp_count, dtype=jnp.int32)[None, :], 0), axis=1
    )
    target = jnp.sum(jnp.where(slab_hits, back_here[None, :], 0), axis=1)
    input_grad = pick_rows(pool_back, target)
    return (
        output,
        input_grad,
        gain_sums[0],
        gain_sums[1],
        weights_summed[0],
        weights_summed[1],
        weights_summed[2],
        weights_summed[6],
        gain_sums[2],
        gain_sums[3],
        weights_summed[3],
        weights_summed[4],
        weights_summed[5],
        weights_summed[6],
    )


UNIT = 256
TILE = 512


def product(left, right, dims):
    return lax.dot_general(left, right, (dims, ((), ())), preferred_element_type=F32)


def fold_lanes(values):
    total = values[:, :128]
    for at in range(128, values.shape[1], 128):
        total = total + values[:, at : at + 128]
    return total


class Copies:
    def __init__(self, send_sems, recv_sems):
        self.send_sems, self.recv_sems, self.used = send_sems, recv_sems, 0

    def make(self, source, target, device):
        number = self.used
        self.used += 1

        def build():
            return pltpu.make_async_remote_copy(
                src_ref=source(),
                dst_ref=target(),
                send_sem=self.send_sems.at[number],
                recv_sem=self.recv_sems.at[number],
                device_id=device,
                device_id_type=pl.DeviceIdType.MESH,
            )

        return build


def attention_head(qkv, back, cos, low, high, allowed):
    scale = 1.0 / math.sqrt(HD)

    def turn(values):
        return values * cos + pltpu.roll(values, HD - 16, 1) * low + pltpu.roll(values, 16, 1) * high

    def turn_back(values):
        return (
            values * cos
            + pltpu.roll(values * high, HD - 16, 1)
            + pltpu.roll(values * low, 16, 1)
        )

    query = turn(qkv[:, :HD]).astype(BF16)
    key = turn(qkv[:, HD : 2 * HD]).astype(BF16)
    value = qkv[:, 2 * HD :].astype(BF16)
    scores = product(query, key, ((1,), (1,))) * scale
    scores = jnp.where(allowed, scores, masked_score)
    weight = jnp.exp(scores - jnp.max(scores, axis=1, keepdims=True))
    probs = weight * (1.0 / jnp.sum(weight, axis=1, keepdims=True))
    probs_low = probs.astype(BF16)
    attn = product(probs_low, value, ((1,), (0,))).astype(BF16)
    grad_probs = product(back, value, ((1,), (1,)))
    centre = jnp.sum(probs * grad_probs, axis=1, keepdims=True)
    grad_scores = (probs * (grad_probs - centre)).astype(BF16)
    grad_query = product(grad_scores, key, ((1,), (0,))) * scale
    grad_key = product(grad_scores, query, ((0,), (0,))) * scale
    grad_value = product(probs_low, back, ((0,), (0,)))
    return attn, [turn_back(grad_query), turn_back(grad_key), grad_value]


def layer_kernel(
    lengths,
    deal_table,
    x_own,
    cot_in,
    norm_own,
    qkv_bias,
    fc1_bias,
    out_bias,
    turns,
    qkv_w,
    dense_w,
    fc1_w,
    fc2_w,
    first_sum,
    second_sum,
    output,
    input_grad,
    small_sum,
    grad_norm,
    cot_own,
    stats,
    x_all,
    cot_all,
    ln1,
    ln2,
    w1,
    w2,
    acts,
    grads,
    first_part,
    second_part,
    out_part,
    out_core,
    out_chip,
    out_x,
    out_half,
    out_y,
    out_item,
    dx_part,
    dx_core,
    dx_chip,
    dx_x,
    dx_half,
    dx_y,
    cot_up,
    cot_down,
    cot_far,
    cot_send,
    cot_edge,
    out_up,
    out_down,
    out_far,
    out_send,
    out_edge,
    acc,
    norm_all,
    first_in,
    second_in,
    first_other,
    second_other,
    first_slot,
    second_slot,
    sum_acc,
    unit_sums,
    small_part,
    small_row,
    small_units,
    small_col,
    small_here,
    small_in,
    small_half,
    small_other,
    row_part,
    row_sums,
    send_sems,
    recv_sems,
    local_sems,
):
    z, r, c = lax.axis_index("dp"), lax.axis_index("row"), lax.axis_index("col")
    y, core = r // 2, r % 2
    mid = ((z + 1) // 2) % 2
    upper = z // 2
    z_in = mid * (3 - z) + (1 - mid) * (1 + upper)
    z_out = 3 * upper
    is_mid, is_edge = mid == 1, mid == 0
    peer = [r, 2 * y + (1 - core), 2 * (1 - y) + core, 2 * (1 - y) + (1 - core)]
    slabs, slab, feats = x_own.shape
    own_rows = slabs * slab
    rows = 2 * own_rows
    hidden_here = fc1_w.shape[1] // 4
    qkv_here = qkv_w.shape[1] // 4
    attn_here = dense_w.shape[0] // 4
    to_row = [{"row": peer[j]} for j in range(4)]
    to_col = {"col": 1 - c}
    to_in = {"dp": z_in}
    to_out = {"dp": z_out}
    copies = Copies(send_sems, recv_sems)
    sent = []

    barrier = pltpu.get_barrier_semaphore()

    def greet(device):
        pl.semaphore_signal(barrier, inc=1, device_id=device, device_id_type=pl.DeviceIdType.MESH)

    for j in (1, 2, 3):
        greet(to_row[j])
    greet(to_col)
    greet(to_in)

    @pl.when(is_mid)
    def _():
        greet(to_out)
        pl.semaphore_wait(barrier, 6)

    @pl.when(is_edge)
    def _():
        pl.semaphore_wait(barrier, 5)

    def start(copy):
        copy().start()
        sent.append(copy)

    def when(flag, action):
        pl.when(flag)(action)

    local_used = [0]

    def local(source, target):
        number = local_used[0]
        local_used[0] += 1

        def build():
            return pltpu.make_async_copy(source(), target(), local_sems.at[number])

        build().start()
        return build

    own_half = pl.ds(c * own_rows, own_rows)
    far_half = pl.ds((1 - c) * own_rows, own_rows)

    class Gather:
        def __init__(self, own, whole, by_row):
            self.own, self.whole = own, whole

            def place(j, half, q):
                return lambda: whole.at[peer[j], slabs * half + q]

            def own_slab(q):
                return lambda: own.at[q]

            ids = range(slabs)
            self.to_y = [copies.make(own_slab(q), place(0, c, q), to_row[2]) for q in ids]
            self.to_x = [copies.make(own_slab(q), place(0, c, q), to_col) for q in ids]
            self.to_core = [copies.make(own_slab(q), place(0, c, q), to_row[1]) for q in ids]
            self.y_core = [copies.make(place(2, c, q), place(2, c, q), to_row[1]) for q in ids]
            self.x_core = [
                copies.make(place(0, 1 - c, q), place(0, 1 - c, q), to_row[1]) for q in ids
            ]
            self.far_core = [
                copies.make(place(2, 1 - c, q), place(2, 1 - c, q), to_row[1]) for q in ids
            ]
            self.by_row = by_row
            self.far = [
                copies.make(place(0, 1 - c, q), place(0, 1 - c, q), to_row[2])
                if q in by_row
                else copies.make(place(2, c, q), place(2, c, q), to_col)
                for q in ids
            ]
            self.kept = [None] * slabs

        def begin(self, q):
            start(self.to_y[q])
            start(self.to_x[q])
            start(self.to_core[q])
            self.kept[q] = local(
                lambda: self.own.at[q], lambda: self.whole.at[r, slabs * c + q]
            )

        def after_y(self, q):
            self.to_y[q]().wait_recv()
            if q not in self.by_row:
                start(self.far[q])
            start(self.y_core[q])

        def after_x(self, q):
            self.to_x[q]().wait_recv()
            if q in self.by_row:
                start(self.far[q])
            start(self.x_core[q])

        def after_far(self, q):
            self.far[q]().wait_recv()
            start(self.far_core[q])

        def end(self, q):
            self.kept[q]().wait()
            for group in (self.to_core, self.y_core, self.x_core, self.far_core):
                group[q]().wait_recv()

    def choose(q, goes, plane, refs, target):
        def body(*blocks):
            value = blocks[0][...]
            for (source, _), block in zip(refs[1:], blocks[1:]):
                value = jnp.where(goes(q, source, plane), block[...], value)
            blocks[-1][...] = value

        tile = slab // 4
        block = pl.BlockSpec((tile, feats), lambda i: (i, 0))
        pltpu.emit_pipeline(
            body, grid=(4,), in_specs=[block] * len(refs), out_specs=[block]
        )(*[ref.at[q] for _, ref in refs], target.at[q])

    class Route:
        def __init__(self, item, goes, up, down, far, send, edge, target):
            self.item, self.goes, self.up, self.down = item, goes, up, down
            self.far, self.send, self.edge, self.target = far, send, edge, target

            def at(ref, q):
                return lambda: ref.at[q]

            ids = range(slabs)
            self.upward = [copies.make(at(item, q), at(up, q), {"dp": z + 1}) for q in ids]
            self.downward = [copies.make(at(item, q), at(down, q), {"dp": z - 1}) for q in ids]
            self.far_up = [copies.make(at(up, q), at(far, q), to_in) for q in ids]
            self.far_down = [copies.make(at(down, q), at(far, q), to_in) for q in ids]
            self.outward = [copies.make(at(send, q), at(edge, q), to_out) for q in ids]

        def begin(self, q):
            when(z < 2, lambda: self.upward[q]().start())
            when(z > 1, lambda: self.downward[q]().start())

        def relay(self, q):
            def from_below():
                self.upward[q]().wait_recv()
                self.far_up[q]().start()

            def from_above():
                self.downward[q]().wait_recv()
                self.far_down[q]().start()

            when(z == 1, from_below)
            when(z == 2, from_above)

        def hand_out(self, q):
            def middle():
                def below():
                    self.downward[q]().wait_recv()
                    self.far_down[q]().wait_recv()

                def above():
                    self.upward[q]().wait_recv()
                    self.far_up[q]().wait_recv()

                when(z == 1, below)
                when(z == 2, above)
                refs = [
                    (z, self.item),
                    (z - 1, self.up),
                    (z + 1, self.down),
                    (3 * (2 - z), self.far),
                ]
                choose(q, self.goes, z_out, refs, self.send)
                self.outward[q]().start()
                choose(q, self.goes, z, refs, self.target)

            when(is_mid, middle)

        def take(self, q):
            def edge():
                self.outward[q]().wait_recv()
                block = pl.BlockSpec((slab // 4, feats), lambda i: (i, 0))

                def body(edge_ref, item_ref, target_ref):
                    mine = self.goes(q, z, z)
                    target_ref[...] = jnp.where(mine, item_ref[...], edge_ref[...])

                pltpu.emit_pipeline(
                    body, grid=(4,), in_specs=[block] * 2, out_specs=[block]
                )(self.edge.at[q], self.item.at[q], self.target.at[q])

            when(is_edge, edge)

        def finish(self):
            for q in range(slabs):
                when(z < 2, lambda: self.upward[q]().wait_send())
                when(z > 1, lambda: self.downward[q]().wait_send())
                when(z == 1, lambda: self.far_up[q]().wait_send())
                when(z == 2, lambda: self.far_down[q]().wait_send())
                when(is_mid, lambda: self.outward[q]().wait_send())

    def undealt(q, source, plane):
        return deal_table[slabs * c + q, source] == plane

    def dealt(q, source, plane):
        return deal_table[slabs * c + q, plane] == source

    x_gather = Gather(x_own, x_all, ())
    cot_gather = Gather(cot_own, cot_all, (1,))
    cot_route = Route(
        cot_in, undealt, cot_up, cot_down, cot_far, cot_send, cot_edge, cot_own
    )
    norm_copies = [
        copies.make(lambda: norm_own, lambda: norm_all.at[r], to_row[j]) for j in (1, 2, 3)
    ]

    odd = z % 2
    across_row = 2 * (1 - y) + core + odd * (1 - 2 * core)
    to_across = {"row": across_row}
    to_pair = {"dp": z + 1 - 2 * odd}

    class Fetch:
        def __init__(
            self, paired, first, first_at, first_width, at, second, second_at, second_width, low
        ):
            size = UNIT if first is fc1_w else qkv_here

            def first_source(taker):
                lanes = pl.multiple_of(taker * first_width + first_at, 256)
                return lambda: first.at[:, pl.ds(lanes, size)]

            def second_source(taker):
                begin = pl.multiple_of(taker * second_width + second_at, 256)
                return lambda: second.at[pl.ds(begin, UNIT)]

            def first_target(giver):
                return lambda: w1.at[giver, :, pl.ds(at, size)]

            def second_target(giver):
                return lambda: w2.at[giver, pl.ds(low, UNIT)]

            pairs = ((first_source, first_target), (second_source, second_target))
            self.beside = [copies.make(f(peer[1]), t(r), to_row[1]) for f, t in pairs]
            self.paired = paired
            if paired:
                self.over = [copies.make(f(across_row), t(r), to_across) for f, t in pairs]
                self.shared = [
                    copies.make(t(across_row), t(across_row), to_pair) for _, t in pairs
                ]
            else:
                self.over = [
                    copies.make(f(peer[j]), t(r), to_row[j]) for f, t in pairs for j in (2, 3)
                ]
            self.kept = [(f(r), t(r)) for f, t in pairs]

        def begin(self):
            for copy in self.over + self.beside:
                start(copy)
            self.kept = [local(*pair) for pair in self.kept]

        def share(self):
            if not self.paired:
                return
            for copy, onward in zip(self.over, self.shared):
                copy().wait_recv()
                start(onward)

        def end(self):
            for copy in self.beside + (self.shared if self.paired else self.over):
                copy().wait_recv()
            for copy in self.kept:
                copy().wait()

    attn_fetch = Fetch(False, qkv_w, 0, qkv_here, 0, dense_w, 0, attn_here, 0)
    mlp_fetch = [
        Fetch(at < 2 * UNIT, fc1_w, at, hidden_here, qkv_here + at, fc2_w, at, hidden_here, attn_here + at)
        for at in range(0, hidden_here, UNIT)
    ]

    kinds = [0, 0, 0]
    keep = upper

    class Unit:
        def __init__(self, kind, at, width=UNIT):
            place, offset = kinds[kind] // UNIT, kinds[kind] % UNIT
            kinds[kind] += width
            if kind == 1:
                part, self.total = first_part, first_sum

                def held(ref, index):
                    return ref.at[index, :, :, pl.ds(offset, width)]

                self.arrived, self.other = held(first_in, place), held(first_other, place)
                self.slot = partial(held, first_slot)
                half = feats // 2
                self.whole = lambda: part.at[:, :, pl.ds(at, width)]

                def region(which, index):
                    return self.total.at[index, pl.ds(which * half, half), pl.ds(at, width)]

            else:
                part, self.total = second_part, second_sum
                self.arrived = second_in.at[place, :, pl.ds(offset, width)]
                self.other = second_other.at[place, :, pl.ds(offset // 2, width // 2)]
                self.slot = lambda index: second_slot.at[index, :, pl.ds(offset, width)]
                half = width // 2
                self.whole = lambda: part.at[:, pl.ds(at, width)]

                def region(which, index):
                    return self.total.at[index, pl.ds(at + which * half, half)]

            self.half, self.region = half, region
            every = slice(None)
            self.inward = copies.make(self.whole, lambda: self.arrived, to_in)
            self.across = copies.make(
                lambda: self.arrived.at[:, pl.ds((1 - keep) * half, half)],
                lambda: self.other,
                to_in,
            )
            self.spread = [
                copies.make(
                    partial(lambda j: self.other.at[peer[j]], j),
                    lambda: region(keep, r),
                    to_row[j],
                )
                for j in (1, 2, 3)
            ]
            self.over = copies.make(
                lambda: region(keep, every), lambda: region(keep, every), to_in
            )
            self.outward = [
                copies.make(lambda: region(keep, every), lambda: region(keep, every), to_out),
                copies.make(
                    lambda: region(1 - keep, every), lambda: region(1 - keep, every), to_out
                ),
            ]
            self.load, self.store = local_used[0], local_used[0] + 1
            local_used[0] += 2

        def loading(self, turn):
            return pltpu.make_async_copy(
                self.whole(), self.slot(turn % 2), local_sems.at[self.load]
            )

        def storing(self):
            return pltpu.make_async_copy(
                self.other.at[r], self.region(keep, r), local_sems.at[self.store]
            )

        def add(self, target, term, offset):
            step = 64

            def body(i, carry):
                here = pl.ds(pl.multiple_of(i * step, step), step)
                there = pl.ds(pl.multiple_of(offset + i * step, step), step)
                target[:, here] = (target[:, here].astype(F32) + term[:, there].astype(F32)).astype(BF16)
                return carry

            lax.fori_loop(0, target.shape[1] // step, body, 0)

        def sum_chip_pair(self, turn):
            self.loading(turn).wait()
            self.inward().wait_recv()
            self.add(self.arrived, self.slot(turn % 2), 0)
            self.across().start()

        def sum_line(self):
            self.across().wait_recv()
            self.add(self.other, self.arrived, keep * self.half)
            for copy in self.spread:
                copy().start()
            self.storing().start()

        def pass_kept(self):
            for copy in self.spread:
                copy().wait_recv()
            self.storing().wait()
            self.over().start()
            self.outward[0]().start()

        def pass_other(self):
            self.over().wait_recv()
            self.outward[1]().start()

        def finish(self, unsent):
            def edge():
                for copy in self.outward:
                    copy().wait_recv()
                if unsent:
                    self.inward().wait_send()

            def middle():
                for copy in [self.across, self.over] + self.spread + self.outward:
                    copy().wait_send()

            when(is_edge, edge)
            when(is_mid, middle)

    def chunk_units(at):
        width = UNIT // 2 if at in (0, hidden_here - UNIT) else UNIT
        parts = range(at, at + UNIT, width)
        return [Unit(2, attn_here + part, width) for part in parts] + [
            Unit(1, qkv_here + part, width) for part in parts
        ]

    mlp_units = [chunk_units(at) for at in range(0, hidden_here, UNIT)]
    attn_units = [Unit(2, 0)] + [Unit(1, at) for at in range(0, qkv_here, UNIT)]

    def norm_body(x_ref, one_ref, two_ref, stat_ref):
        wide = jnp.concatenate([x_ref[j, 0] for j in range(4)], axis=1).astype(F32)
        norms = jnp.concatenate([norm_all[j] for j in range(4)], axis=1)
        mean = jnp.sum(wide, axis=1, keepdims=True) / D
        square = jnp.sum(wide * wide, axis=1, keepdims=True) / D
        inv_std = lax.rsqrt(square - mean * mean + norm_epsilon)
        normed = (wide - mean) * inv_std
        one_ref[...] = (normed * norms[0:1] + norms[1:2]).astype(BF16)
        two_ref[...] = (normed * norms[2:3] + norms[3:4]).astype(BF16)
        lane = lax.broadcasted_iota(jnp.int32, stat_ref.shape, 1)
        stat_ref[...] = jnp.where(lane < 64, mean, inv_std)

    def norm_stage():
        tile = 256
        flat = pl.BlockSpec((tile, D), lambda i: (i, 0))
        pltpu.emit_pipeline(
            norm_body,
            grid=(rows // tile,),
            in_specs=[
                pl.BlockSpec(
                    (4, 1, tile, feats), lambda i: (0, i * tile // slab, i % (slab // tile), 0)
                )
            ],
            out_specs=[flat, flat, pl.BlockSpec((tile, 128), lambda i: (i, 0))],
        )(x_all, ln1, ln2, stats)

    def mlp_stage(k):
        at = k * UNIT
        bias = fc1_bias[r, :, at : at + UNIT]

        def body(ln_ref, cot_ref, first_ref, second_ref, act_ref, grad_ref):
            step = pl.program_id(0)

            @pl.when(step == 0)
            def _():
                acc[:, : 2 * UNIT, :] = jnp.zeros((4, 2 * UNIT, feats), F32)
                sum_acc[:, :UNIT] = jnp.zeros((8, UNIT), F32)

            hidden = bias
            grad_act = None
            for j in range(4):
                lanes = slice(j * feats, (j + 1) * feats)
                hidden = hidden + product(ln_ref[:, lanes], first_ref[j], ((1,), (0,)))
                term = product(cot_ref[j, 0], second_ref[j], ((1,), (1,)))
                grad_act = term if j == 0 else grad_act + term
            curve = 0.5 * (1.0 + lax.erf(hidden * math.sqrt(0.5)))
            bell = jnp.exp(-0.5 * hidden * hidden) * (1.0 / math.sqrt(2.0 * math.pi))
            act = (hidden * curve).astype(BF16)
            grad_hidden = (grad_act * (curve + hidden * bell)).astype(BF16)
            act_ref[...] = act
            grad_ref[...] = grad_hidden
            sum_acc[0:1, :UNIT] += jnp.sum(grad_hidden.astype(F32), axis=0, keepdims=True)
            for j in range(4):
                lanes = slice(j * feats, (j + 1) * feats)
                acc[j, :UNIT] += product(act, cot_ref[j, 0], ((0,), (0,)))
                acc[j, UNIT : 2 * UNIT] += product(grad_hidden, ln_ref[:, lanes], ((0,), (0,)))

        pltpu.emit_pipeline(
            body,
            grid=(rows // TILE,),
            in_specs=[
                pl.BlockSpec((TILE, D), lambda i: (i, 0)),
                pl.BlockSpec((4, 1, slab, feats), lambda i: (0, i, 0, 0)),
                pl.BlockSpec((4, feats, UNIT), lambda i: (0, 0, (qkv_here + at) // UNIT)),
                pl.BlockSpec((4, UNIT, feats), lambda i: (0, (attn_here + at) // UNIT, 0)),
            ],
            out_specs=[
                pl.BlockSpec((TILE, UNIT), lambda i: (i, (attn_here + at) // UNIT)),
                pl.BlockSpec((TILE, UNIT), lambda i: (i, (qkv_here + at) // UNIT)),
            ],
        )(ln2, cot_all, w1, w2, acts, grads)
        grad_stage(UNIT, qkv_here + at, attn_here + at, 1, k == 0)
        unit_sums[0:1, qkv_here + at : qkv_here + at + UNIT] = sum_acc[0:1, :UNIT]

    def grad_stage(width, first_at, second_at, which, fresh):
        def body(first_ref, part_one, part_two):
            j = pl.program_id(0)
            grad = acc[j, UNIT : UNIT + width].T
            weight = first_ref[0].astype(F32)
            part_one[0] = grad.astype(BF16)
            part_two[0] = acc[j, :UNIT].astype(BF16)
            terms = [fold_lanes(grad * weight), fold_lanes(weight * sum_acc[0:1, :width])]
            ones = jnp.ones((8, 128), F32)
            for k in (0, 1):
                sums = lax.dot_general(
                    ones,
                    terms[k],
                    (((1,), (1,)), ((), ())),
                    precision=lax.Precision.HIGHEST,
                    preferred_element_type=F32,
                )[0:1]
                at = 2 * which + k
                if not fresh:
                    sums = sums + small_part[j, at : at + 1]
                small_part[j, at : at + 1] = sums

        lanes = slice(first_at, first_at + width)
        block = pl.BlockSpec((1, feats, width), lambda j: (j, 0, 0))
        pltpu.emit_pipeline(
            body,
            grid=(4,),
            in_specs=[block],
            out_specs=[block, pl.BlockSpec((1, UNIT, feats), lambda j: (j, second_at // UNIT, 0))],
        )(w1.at[:, :, lanes], first_part.at[:, :, lanes], second_part)

    def attention_slab(s):
        once = pl.Buffered(1)
        heads = qkv_here // (3 * HD)
        bias = qkv_bias[r]

        def body(ln_ref, cot_ref, first_ref, second_ref, act_ref, grad_ref):
            qkv = bias
            back = None
            for j in range(4):
                lanes = slice(j * feats, (j + 1) * feats)
                qkv = qkv + product(ln_ref[:, lanes], first_ref[j], ((1,), (0,)))
                term = product(cot_ref[j, 0], second_ref[j], ((1,), (1,)))
                back = term if j == 0 else back + term
            back = back.astype(BF16)
            at = lax.broadcasted_iota(jnp.int32, (TILE, TILE), 0)
            of = lax.broadcasted_iota(jnp.int32, (TILE, TILE), 1)
            token = lax.broadcasted_iota(jnp.int32, (TILE, HD), 0)
            lane = lax.broadcasted_iota(jnp.int32, (TILE, HD), 1)
            begin = jnp.zeros((TILE, HD), jnp.int32)
            edge = 0
            for k in range(lengths.shape[1] - 1):
                edge = edge + lengths[4 * z + s, k]
                begin = jnp.where(token >= edge, edge, begin)
            allowed = (of <= at) & (of >= begin[:, :1])
            angle = (token - begin).astype(F32) * turns[0:1]
            cos, sin = jnp.cos(angle), jnp.sin(angle)
            low = jnp.where(lane < ROT // 2, -sin, 0.0)
            high = jnp.where(lane < ROT // 2, 0.0, sin)
            for h in range(heads):
                attn, grads_here = attention_head(
                    qkv[:, h * 3 * HD : (h + 1) * 3 * HD],
                    back[:, h * HD : (h + 1) * HD],
                    cos,
                    low,
                    high,
                    allowed,
                )
                act_ref[:, h * HD : (h + 1) * HD] = attn
                for i in range(3):
                    at_lane = (h * 3 + i) * HD
                    grad_ref[:, at_lane : at_lane + HD] = grads_here[i].astype(BF16)
            attn, grad = act_ref[...], grad_ref[...]
            sums = jnp.sum(grad.astype(F32), axis=0, keepdims=True)
            sum_acc[0:1, :qkv_here] = sums if s == 0 else sum_acc[0:1, :qkv_here] + sums
            for j in range(4):
                lanes = slice(j * feats, (j + 1) * feats)
                second_term = product(attn, cot_ref[j, 0], ((0,), (0,)))
                first_term = product(grad, ln_ref[:, lanes], ((0,), (0,)))
                acc[j, :UNIT] = second_term if s == 0 else acc[j, :UNIT] + second_term
                acc[j, UNIT:] = first_term if s == 0 else acc[j, UNIT:] + first_term

        pltpu.emit_pipeline(
            body,
            grid=(1,),
            in_specs=[
                pl.BlockSpec((TILE, D), lambda i: (s, 0), pipeline_mode=once),
                pl.BlockSpec((4, 1, slab, feats), lambda i: (0, s, 0, 0), pipeline_mode=once),
                pl.BlockSpec((4, feats, qkv_here), lambda i: (0, 0, 0), pipeline_mode=once),
                pl.BlockSpec((4, UNIT, feats), lambda i: (0, 0, 0), pipeline_mode=once),
            ],
            out_specs=[
                pl.BlockSpec((TILE, UNIT), lambda i: (s, 0), pipeline_mode=once),
                pl.BlockSpec((TILE, qkv_here), lambda i: (s, 0), pipeline_mode=once),
            ],
        )(
            ln1,
            cot_all,
            w1.at[:, :, :qkv_here],
            w2,
            acts,
            grads.at[:, :qkv_here],
        )
        if s == 3:
            grad_stage(qkv_here, 0, 0, 0, True)
            unit_sums[0:1, :qkv_here] = sum_acc[0:1, :qkv_here]

    def out_stage(n):
        def body(act_ref, second_ref, part_ref):
            part_ref[0] = product(act_ref[...], second_ref[0], ((1,), (0,))).astype(BF16)

        pltpu.emit_pipeline(
            body,
            grid=(rows // TILE,),
            in_specs=[
                pl.BlockSpec((TILE, acts.shape[1]), lambda i: (i, 0)),
                pl.BlockSpec((1, w2.shape[1], feats), lambda i: (n, 0, 0)),
            ],
            out_specs=[pl.BlockSpec((1, TILE, feats), lambda i: (n, i, 0))],
        )(acts, w2, out_part)

    def dx_stage(n):
        def body(grad_ref, first_ref, part_ref):
            norms = norm_all[n]
            one = product(grad_ref[:, :qkv_here], first_ref[0, :, :qkv_here], ((1,), (1,)))
            two = product(grad_ref[:, qkv_here:], first_ref[0, :, qkv_here:], ((1,), (1,)))
            part_ref[0] = (one * norms[0:1] + two * norms[2:3]).astype(BF16)

        pltpu.emit_pipeline(
            body,
            grid=(rows // TILE,),
            in_specs=[
                pl.BlockSpec((TILE, grads.shape[1]), lambda i: (i, 0)),
                pl.BlockSpec((1, feats, w1.shape[2]), lambda i: (n, 0, 0)),
            ],
            out_specs=[pl.BlockSpec((1, TILE, feats), lambda i: (n, i, 0))],
        )(grads, w1, dx_part)

    class Scatter:
        def __init__(self, part, from_core, chip, from_x, half, from_y):
            self.part, self.from_core, self.chip = part, from_core, chip
            self.from_x, self.half, self.from_y = from_x, half, from_y
            self.to_core = [
                copies.make(
                    partial(lambda j: part.at[peer[j]], j),
                    partial(lambda j: from_core.at[peer[j] // 2], j),
                    to_row[1],
                )
                for j in (1, 3)
            ]
            self.to_x = copies.make(
                lambda: chip.at[:, far_half], lambda: from_x, to_col
            )
            self.to_y = copies.make(lambda: half.at[1 - y], lambda: from_y, to_row[2])

        def begin(self):
            for copy in self.to_core:
                start(copy)

        def second(self):
            for copy in self.to_core:
                copy().wait_recv()

            def body(left, right, target):
                target[...] = (left[...].astype(F32) + right[...].astype(F32)).astype(BF16)

            block = pl.BlockSpec((1, TILE, feats), lambda s, i: (s, i, 0))
            pltpu.emit_pipeline(
                body,
                grid=(2, rows // TILE),
                in_specs=[
                    pl.BlockSpec((1, TILE, feats), lambda s, i: (2 * s + core, i, 0)),
                    block,
                ],
                out_specs=[block],
            )(self.part, self.from_core, self.chip)
            start(self.to_x)

        def third(self):
            self.to_x().wait_recv()

            def body(left, right, target):
                target[...] = (left[...].astype(F32) + right[...].astype(F32)).astype(BF16)

            block = pl.BlockSpec((1, TILE, feats), lambda s, i: (s, i, 0))
            tiles = own_rows // TILE
            pltpu.emit_pipeline(
                body,
                grid=(2, tiles),
                in_specs=[
                    pl.BlockSpec((1, TILE, feats), lambda s, i: (s, c * tiles + i, 0)),
                    block,
                ],
                out_specs=[block],
            )(self.chip, self.from_x, self.half)
            start(self.to_y)

        def last(self, body, extra, target):
            self.to_y().wait_recv()
            flat = pl.BlockSpec((1, slab, feats), lambda i: (i, 0, 0))
            pltpu.emit_pipeline(
                body,
                grid=(own_rows // TILE,),
                in_specs=[
                    pl.BlockSpec((1, TILE, feats), lambda i: (y, i, 0)),
                    pl.BlockSpec((TILE, feats), lambda i: (i, 0)),
                    flat,
                ],
                out_specs=[flat],
            )(self.half, self.from_y, extra, target)

    out_scatter = Scatter(out_part, out_core, out_chip, out_x, out_half, out_y)
    dx_scatter = Scatter(dx_part, dx_core, dx_chip, dx_x, dx_half, dx_y)
    out_route = Route(
        out_item, dealt, out_up, out_down, out_far, out_send, out_edge, output
    )

    def finish_output():
        def body(half_ref, y_ref, x_ref, item_ref):
            item_ref[0] = (
                half_ref[0].astype(F32)
                + y_ref[...].astype(F32)
                + x_ref[0].astype(F32)
                + out_bias[0:1]
            ).astype(BF16)

        out_scatter.last(body, x_own, out_item)

    row_copies = [
        copies.make(lambda: row_part, lambda: row_sums.at[r], to_row[j]) for j in (1, 2, 3)
    ]

    def sum_grad():
        dx_scatter.to_y().wait_recv()

        def body(half_ref, y_ref, x_ref, stat_ref, target_ref):
            grad = half_ref[0].astype(F32) + y_ref[...].astype(F32)
            target_ref[...] = grad
            normed = (x_ref[0].astype(F32) - stat_ref[:, :1]) * stat_ref[:, 127:]
            one = jnp.sum(grad, axis=1, keepdims=True)
            two = jnp.sum(grad * normed, axis=1, keepdims=True)
            lane = lax.broadcasted_iota(jnp.int32, (TILE, 128), 1)
            both = jnp.where(lane == 0, one, jnp.where(lane == 1, two, 0.0))
            row_part[pl.program_id(0)] = both.T[:8]

        pltpu.emit_pipeline(
            body,
            grid=(own_rows // TILE,),
            in_specs=[
                pl.BlockSpec((1, TILE, feats), lambda i: (y, i, 0)),
                pl.BlockSpec((TILE, feats), lambda i: (i, 0)),
                pl.BlockSpec((1, slab, feats), lambda i: (i, 0, 0)),
                pl.BlockSpec((TILE, 128), lambda i: (slabs * c + i, 0)),
            ],
            out_specs=[pl.BlockSpec((TILE, feats), lambda i: (i, 0))],
        )(dx_half, dx_y, x_own, stats, grad_norm)
        for copy in row_copies:
            start(copy)
        row_sums[r] = row_part[...]

    def finish_grad():
        for copy in row_copies:
            copy().wait_recv()

        def body(grad_ref, cot_ref, x_ref, stat_ref, target_ref):
            step = pl.program_id(0)
            sums = row_sums[0, step] + row_sums[1, step] + row_sums[2, step] + row_sums[3, step]
            sums = jnp.concatenate([sums, jnp.zeros((120, TILE), F32)], axis=0).T * (1.0 / D)
            normed = (x_ref[0].astype(F32) - stat_ref[:, :1]) * stat_ref[:, 127:]
            target_ref[0] = cot_ref[0].astype(F32) + stat_ref[:, 127:] * (
                grad_ref[...] - sums[:, 0:1] - normed * sums[:, 1:2]
            )

        flat = pl.BlockSpec((1, slab, feats), lambda i: (i, 0, 0))
        pltpu.emit_pipeline(
            body,
            grid=(own_rows // TILE,),
            in_specs=[
                pl.BlockSpec((TILE, feats), lambda i: (i, 0)),
                flat,
                flat,
                pl.BlockSpec((TILE, 128), lambda i: (slabs * c + i, 0)),
            ],
            out_specs=[flat],
        )(grad_norm, cot_own, x_own, stats, input_grad)

    sums_wide = small_units.shape[2]
    small_copies = [
        copies.make(
            partial(lambda j: small_part.at[peer[j]], j), lambda: small_row.at[r], to_row[j]
        )
        for j in (1, 2, 3)
    ]
    unit_copies = [
        copies.make(lambda: unit_sums, lambda: small_units.at[r], to_row[j]) for j in (1, 2, 3)
    ]
    col_copy = copies.make(
        lambda: small_here.at[:, pl.ds(sums_wide, feats)], lambda: small_col, to_col
    )
    small_inward = copies.make(lambda: small_here, lambda: small_in, to_in)
    small_across = copies.make(lambda: small_half, lambda: small_other, to_in)
    small_outward = copies.make(lambda: small_in, lambda: small_in, to_out)

    def small_begin():
        small_part[:, 4:] = jnp.zeros((4, 4, feats), F32)
        for copy in small_copies + unit_copies:
            start(copy)
        small_row[r] = small_part[r]
        small_units[r] = unit_sums[...]

    def small_second():
        for copy in small_copies + unit_copies:
            copy().wait_recv()
        small_here[...] = jnp.zeros(small_here.shape, F32)
        for j in range(4):
            small_here[j : j + 1, :sums_wide] = small_units[j, 0:1]
        small_here[:, sums_wide:] = small_row[0] + small_row[1] + small_row[2] + small_row[3]

        def body(cot_ref):
            total = jnp.sum(cot_ref[0].astype(F32), axis=0, keepdims=True)
            small_here[4:5, sums_wide:] += total

        pltpu.emit_pipeline(
            body,
            grid=(slabs,),
            in_specs=[pl.BlockSpec((1, slab, feats), lambda i: (i, 0, 0))],
        )(cot_own)
        start(col_copy)

    def small_third():
        col_copy().wait_recv()
        col_copy().wait_send()
        small_here[:, sums_wide:] += small_col[...]
        when(is_edge, lambda: small_inward().start())

    def small_halve():
        def middle():
            small_inward().wait_recv()
            small_half[...] = small_here[...] + small_in[...]
            small_across().start()

        when(is_mid, middle)

    def small_close():
        def middle():
            small_across().wait_recv()
            small_in[...] = small_half[...] + small_other[...]
            small_outward().start()

        when(is_mid, middle)

    def small_finish():
        def edge():
            small_outward().wait_recv()
            small_inward().wait_send()

        def middle():
            small_across().wait_send()
            small_outward().wait_send()

        when(is_edge, edge)
        when(is_mid, middle)
        total = small_in[...]
        small_sum[:, :sums_wide] = total[:, :sums_wide]
        norms = norm_own[...]
        sums = total[:, sums_wide:]
        gains = [
            (sums[k : k + 1] - norms[k + 1 : k + 2] * sums[k + 1 : k + 2]) / norms[k : k + 1]
            for k in (0, 2)
        ]
        small_sum[:, sums_wide:] = jnp.concatenate(
            [gains[0], sums[1:2], gains[1], sums[3:4], sums[4:]], axis=0
        )

    line = []
    begun, loaded, served = [0], [0], [0]
    flight = 2

    def lead():
        while begun[0] < min(len(line), served[0] + 2):
            at = begun[0]

            def edge():
                if at >= flight:
                    line[at - flight].inward().wait_send()
                line[at].inward().start()

            when(is_edge, edge)
            begun[0] += 1
        while loaded[0] < min(len(line), served[0] + 2):
            at = loaded[0]
            when(is_mid, lambda: line[at].loading(at).start())
            loaded[0] += 1

    def queue(units):
        line.extend(units)
        lead()

    def serve(count, closing=False):
        for _ in range(count):
            at = served[0]
            if at >= len(line) and not closing:
                return
            lead()

            def middle():
                if 0 <= at - 3 < len(line):
                    line[at - 3].pass_other()
                if 0 <= at - 2 < len(line):
                    line[at - 2].pass_kept()
                if 0 <= at - 1 < len(line):
                    line[at - 1].sum_line()
                if at < len(line):
                    line[at].sum_chip_pair(at)

            when(is_mid, middle)
            served[0] += 1
            lead()

    slab_ids = range(slabs)
    for q in slab_ids:
        x_gather.begin(q)
    cot_route.begin(0)
    norm_all[r] = norm_own[...]
    for copy in norm_copies:
        start(copy)
    cot_route.relay(0)
    cot_route.begin(1)
    for q in slab_ids:
        x_gather.after_y(q)
    mlp_fetch[0].begin()
    cot_route.relay(1)
    cot_route.hand_out(0)
    for q in slab_ids:
        x_gather.after_x(q)
    cot_route.take(0)
    cot_gather.begin(0)
    cot_route.hand_out(1)
    mlp_fetch[0].share()
    for q in slab_ids:
        x_gather.after_far(q)
    cot_route.take(1)
    cot_gather.begin(1)
    mlp_fetch[1].begin()
    cot_gather.after_y(0)
    cot_gather.after_x(0)
    cot_gather.after_y(1)
    cot_gather.after_x(1)
    for q in slab_ids:
        x_gather.end(q)
    for copy in norm_copies:
        copy().wait_recv()
    mlp_fetch[1].share()
    norm_stage()
    for q in slab_ids:
        cot_gather.after_far(q)
    mlp_fetch[2].begin()
    for q in slab_ids:
        cot_gather.end(q)
    mlp_fetch[0].end()
    mlp_stage(0)
    queue(mlp_units[0])
    mlp_fetch[2].share()
    attn_fetch.begin()
    mlp_fetch[1].end()
    mlp_stage(1)
    queue(mlp_units[1])
    serve(1)
    mlp_fetch[2].end()
    mlp_stage(2)
    mlp_fetch[3].begin()
    queue(mlp_units[2])
    serve(2)
    attn_fetch.end()
    attention_slab(0)
    serve(1)
    attention_slab(1)
    serve(1)
    attention_slab(2)
    serve(1)
    attention_slab(3)
    queue(attn_units)
    serve(1)
    mlp_fetch[3].end()
    mlp_stage(3)
    queue(mlp_units[3])
    serve(1)
    out_stage(0)
    out_stage(1)
    serve(1)
    out_stage(2)
    out_stage(3)
    out_scatter.begin()
    serve(1)
    dx_stage(0)
    out_scatter.second()
    dx_stage(1)
    serve(1)
    dx_stage(2)
    dx_stage(3)
    dx_scatter.begin()
    serve(1)
    small_begin()
    out_scatter.third()
    small_second()
    serve(1)
    finish_output()
    out_route.begin(0)
    dx_scatter.second()
    small_third()
    serve(1)
    out_route.relay(0)
    out_route.begin(1)
    small_halve()
    serve(1)
    out_route.relay(1)
    out_route.hand_out(0)
    serve(1)
    small_close()
    dx_scatter.third()
    serve(1)
    out_route.hand_out(1)
    serve(1)
    sum_grad()
    serve(1, True)
    out_route.take(0)
    finish_grad()
    serve(1, True)
    out_route.take(1)
    while served[0] < len(line) + 3:
        serve(1, True)
    for at, unit in enumerate(line):
        unit.finish(at >= len(line) - flight)
    small_finish()
    cot_route.finish()
    out_route.finish()
    for copy in sent:
        if copy is not col_copy:
            copy().wait_send()


def widen_body(first_ref, dense_ref, fc2_ref, qkv_out, fc1_out, dense_out, fc2_out):
    qkv_here = qkv_out.shape[1]
    qkv_out[...] = first_ref[0, :, :qkv_here].astype(F32)
    fc1_out[...] = first_ref[0, :, qkv_here:].astype(F32)
    dense_out[...] = dense_ref[0].astype(F32)
    fc2_out[...] = fc2_ref[0].astype(F32)


def widen(first_sum, second_sum, qkv_here, attn_here):
    feats, first_cols = first_sum.shape[1:]
    hidden_here = first_cols - qkv_here
    tiles = hidden_here // attn_here
    tile = feats // tiles
    return pl.pallas_call(
        widen_body,
        grid=(4, tiles),
        in_specs=[
            pl.BlockSpec((1, tile, first_cols), lambda s, i: (s, i, 0)),
            pl.BlockSpec((1, attn_here // tiles, feats), lambda s, i: (s, i, 0)),
            pl.BlockSpec((1, attn_here, feats), lambda s, i: (s, 1 + i, 0)),
        ],
        out_specs=[
            pl.BlockSpec((tile, qkv_here), lambda s, i: (i, s)),
            pl.BlockSpec((tile, hidden_here), lambda s, i: (i, s)),
            pl.BlockSpec((attn_here // tiles, feats), lambda s, i: (s * tiles + i, 0)),
            pl.BlockSpec((attn_here, feats), lambda s, i: (s * tiles + i, 0)),
        ],
        out_shape=[
            jax.ShapeDtypeStruct((feats, 4 * qkv_here), F32),
            jax.ShapeDtypeStruct((feats, 4 * hidden_here), F32),
            jax.ShapeDtypeStruct((4 * attn_here, feats), F32),
            jax.ShapeDtypeStruct((4 * hidden_here, feats), F32),
        ],
        compiler_params=pltpu.CompilerParams(vmem_limit_bytes=32 * 1024 * 1024),
    )(first_sum, second_sum, second_sum)


def dealt_layer(
    layer_input,
    lengths,
    deal_table,
    ln1_gain,
    ln1_bias,
    qkv_weight,
    qkv_bias,
    dense_weight,
    dense_bias,
    ln2_gain,
    ln2_bias,
    fc1_weight,
    fc1_bias,
    fc2_weight,
    fc2_bias,
    cotangent,
):
    own_rows, feats = layer_input.shape
    rows = 2 * own_rows
    slab = own_rows // 2
    qkv_cols = qkv_weight.shape[1]
    qkv_here = qkv_cols // 4
    attn_here = dense_weight.shape[0] // 4
    hidden_cols = fc1_weight.shape[1]
    hidden_here = hidden_cols // 4
    first_cols = qkv_here + hidden_here
    second_rows = attn_here + hidden_here

    norms = jnp.stack([ln1_gain, ln1_bias, ln2_gain, ln2_bias] * 2)
    out_bias = (dense_bias + fc2_bias).reshape(1, feats)
    turns = 1.0 / 10000.0 ** (np.arange(0, ROT, 2) / ROT)
    turns = np.concatenate([turns, turns, np.zeros(HD - ROT)])
    turns = np.broadcast_to(turns.astype(np.float32), (8, HD))

    low = lambda *shape: jax.ShapeDtypeStruct(shape, BF16)
    wide = lambda *shape: jax.ShapeDtypeStruct(shape, F32)
    first = low(4, feats, first_cols)
    second = low(4, second_rows, feats)
    item = low(2, slab, feats)
    small_shape = (8, first_cols + feats)
    outputs = [first, second, item, wide(2, slab, feats)]
    scatter = [
        low(4, rows, feats),
        low(2, rows, feats),
        low(2, rows, feats),
        low(2, own_rows, feats),
        low(2, own_rows, feats),
        low(own_rows, feats),
    ]
    buffers = (
        [wide(own_rows, feats), item, wide(rows, 128)]
        + [low(4, 4, slab, feats)] * 2
        + [low(rows, D)] * 2
        + [first, second, low(rows, second_rows), low(rows, first_cols)]
        + [first, second]
        + scatter
        + [item]
        + scatter
        + [item] * 10
    )
    any_space = pl.BlockSpec(memory_space=pl.ANY)
    vmem = pl.BlockSpec(memory_space=pltpu.VMEM)
    smem = pl.BlockSpec(memory_space=pltpu.SMEM)
    copies = 250
    first_units, second_units = first_cols // UNIT, second_rows // UNIT
    results = pl.pallas_call(
        layer_kernel,
        in_specs=[smem] * 2 + [any_space] * 2 + [vmem] * 5 + [any_space] * 4,
        out_specs=[any_space] * 4 + [vmem] + [any_space] * len(buffers),
        out_shape=outputs + [wide(*small_shape)] + buffers,
        scratch_shapes=[
            pltpu.VMEM((4, UNIT + qkv_here, feats), F32),
            pltpu.VMEM((4, 8, feats), F32),
            pltpu.VMEM((first_units, 4, feats, UNIT), BF16),
            pltpu.VMEM((second_units, 4, UNIT, feats), BF16),
            pltpu.VMEM((first_units, 4, feats // 2, UNIT), BF16),
            pltpu.VMEM((second_units, 4, UNIT // 2, feats), BF16),
            pltpu.VMEM((2, 4, feats, UNIT), BF16),
            pltpu.VMEM((2, 4, UNIT, feats), BF16),
            pltpu.VMEM((8, qkv_here), F32),
            pltpu.VMEM((8, first_cols), F32),
            pltpu.VMEM((4, 8, feats), F32),
            pltpu.VMEM((4, 8, feats), F32),
            pltpu.VMEM((4, 8, first_cols), F32),
            pltpu.VMEM((8, feats), F32),
            pltpu.VMEM(small_shape, F32),
            pltpu.VMEM(small_shape, F32),
            pltpu.VMEM(small_shape, F32),
            pltpu.VMEM(small_shape, F32),
            pltpu.VMEM((2, 8, slab), F32),
            pltpu.VMEM((4, 2, 8, slab), F32),
            pltpu.SemaphoreType.DMA((copies,)),
            pltpu.SemaphoreType.DMA((copies,)),
            pltpu.SemaphoreType.DMA((96,)),
        ],
        compiler_params=pltpu.CompilerParams(
            collective_id=0, has_side_effects=True, vmem_limit_bytes=60 * 1024 * 1024
        ),
        cost_estimate=pl.CostEstimate(
            flops=6 * rows * D * (first_cols + second_rows),
            bytes_accessed=200 * 1024 * 1024,
            transcendentals=rows * hidden_here,
        ),
    )(
        lengths,
        deal_table,
        layer_input.reshape(2, slab, feats),
        cotangent.reshape(2, slab, feats),
        norms,
        qkv_bias.reshape(4, 1, qkv_here),
        fc1_bias.reshape(4, 1, hidden_here),
        out_bias,
        turns,
        qkv_weight,
        dense_weight,
        fc1_weight,
        fc2_weight,
    )
    first_sum, second_sum, output, input_grad, small = results[:5]
    qkv_grad, fc1_grad, dense_grad, fc2_grad = widen(first_sum, second_sum, qkv_here, attn_here)
    norm_sums = small[:5, first_cols:]
    return (
        output.reshape(own_rows, feats),
        input_grad.reshape(own_rows, feats),
        norm_sums[0],
        norm_sums[1],
        qkv_grad,
        small[:4, :qkv_here].reshape(qkv_cols),
        dense_grad,
        norm_sums[4],
        norm_sums[2],
        norm_sums[3],
        fc1_grad,
        small[:4, qkv_here:first_cols].reshape(hidden_cols),
        fc2_grad,
        norm_sums[4],
    )


def solution(mesh):
    grid = tuple(mesh.shape[axis] for axis in ("dp", "row", "col"))
    placed = (
        P(("dp", "col"), "row"),
        P(),
        P(),
        P("row"),
        P("row"),
        P("row", "col"),
        P("col"),
        P("col", "row"),
        P("row"),
        P("row"),
        P("row"),
        P("row", "col"),
        P("col"),
        P("col", "row"),
        P("row"),
        P(("dp", "col"), "row"),
    )
    return jax.shard_map(
        dealt_layer if grid == (4, 4, 2) else local,
        mesh=mesh,
        in_specs=placed,
        out_specs=(
            P(("dp", "col"), "row"),
            P(("dp", "col"), "row"),
            P("row"),
            P("row"),
            P("row", "col"),
            P("col"),
            P("col", "row"),
            P("row"),
            P("row"),
            P("row"),
            P("row", "col"),
            P("col"),
            P("col", "row"),
            P("row"),
        ),
        check_vma=False,
    )
```

```python
from functools import partial
import math

import jax
import jax.numpy as jnp
import numpy as np
from jax import lax
from jax.experimental import pallas as pl
from jax.experimental.pallas import tpu as pltpu
from jax.sharding import PartitionSpec as P

D = 2048
HD = 128
ROT = 32
QBLK = 512
CHUNK = 256
BF16 = jnp.bfloat16
F32 = jnp.float32


norm_epsilon = 1e-05
masked_score = -1000000000.0


def rotary_tables(positions):
    frequency = 1.0 / 10000.0 ** (jnp.arange(0, ROT, 2, dtype=jnp.float32) / ROT)
    angles = positions.astype(jnp.float32)[:, None] * frequency[None, :]
    angles = jnp.concatenate([angles, angles], axis=1)
    return (jnp.cos(angles), jnp.sin(angles))


def rotate(values, cos_table, sin_table):
    half_rot = ROT // 2
    rotated = values[..., :ROT]
    turned = jnp.concatenate([-rotated[..., half_rot:], rotated[..., :half_rot]], axis=-1)
    rotated = rotated * cos_table[:, None, :] + turned * sin_table[:, None, :]
    return jnp.concatenate([rotated, values[..., ROT:]], axis=-1)


def segment_layout(seq_lengths, length):
    seq_ends = jnp.cumsum(seq_lengths)
    token_place = jnp.arange(length, dtype=jnp.int32)
    sequence_ids = jnp.sum((token_place[:, None] >= seq_ends[None, :]).astype(jnp.int32), axis=1)
    starts = seq_ends - seq_lengths
    seq_hits = sequence_ids[:, None] == jnp.arange(seq_lengths.shape[0], dtype=jnp.int32)[None, :]
    seq_begin = jnp.sum(jnp.where(seq_hits, starts[None, :], 0), axis=1)
    return (sequence_ids, token_place - seq_begin)


def contract_rows(left_side, right_side):
    return lax.dot_general(
        left_side, right_side, (((0,), (0,)), ((), ())), preferred_element_type=jnp.float32
    )


def contract_cols(left_side, right_side):
    return lax.dot_general(
        left_side, right_side, (((1,), (1,)), ((), ())), preferred_element_type=jnp.float32
    )


def pick_rows(pooled, chosen):
    row_hits = chosen[None, :] == jnp.arange(pooled.shape[0], dtype=jnp.int32)[:, None]
    return jnp.sum(jnp.where(row_hits[:, :, None], pooled.astype(jnp.float32), 0.0), axis=0)


def local(
    layer_input,
    lengths,
    deal_table,
    ln1_gain,
    ln1_bias,
    qkv_weight,
    qkv_bias,
    dense_weight,
    dense_bias,
    ln2_gain,
    ln2_bias,
    fc1_weight,
    fc1_bias,
    fc2_weight,
    fc2_bias,
    cotangent,
):
    dp_count = lax.axis_size("dp")
    row_count = lax.axis_size("row")
    col_count = lax.axis_size("col")
    group_id = lax.axis_index("dp")
    row_id = lax.axis_index("row")
    col_id = lax.axis_index("col")
    own_rows, own_feats = layer_input.shape
    group_rows = own_rows * col_count
    slab_rows = group_rows // row_count
    qkv_cols = qkv_weight.shape[1]
    attn_cols = dense_weight.shape[0]
    heads_here = qkv_cols // (3 * HD)
    score_scale = 1.0 / math.sqrt(HD)
    local_slab = (col_id * own_rows + jnp.arange(own_rows, dtype=jnp.int32)) // slab_rows
    slab_hits = local_slab[:, None] == jnp.arange(row_count, dtype=jnp.int32)[None, :]
    deal_here = lax.dynamic_index_in_dim(deal_table, group_id, 1, keepdims=False)
    source = jnp.sum(jnp.where(slab_hits, deal_here[None, :], 0), axis=1)
    pooled = lax.all_gather(layer_input, "dp", axis=0, tiled=True).reshape(
        dp_count, own_rows, own_feats
    )
    mine_rows = pick_rows(pooled, source).astype(jnp.bfloat16)
    input_all = lax.all_gather(mine_rows, "col", axis=0, tiled=True)
    input_wide = input_all.astype(jnp.float32)
    row_stats = lax.psum(
        (jnp.sum(input_wide, axis=1), jnp.sum(input_wide * input_wide, axis=1)), "row"
    )
    row_mean = row_stats[0] / D
    inv_std = lax.rsqrt(row_stats[1] / D - row_mean * row_mean + norm_epsilon)
    normed = (input_wide - row_mean[:, None]) * inv_std[:, None]
    own_start = col_id * own_rows
    normed_own = lax.dynamic_slice_in_dim(normed, own_start, own_rows, 0)
    inv_std_own = lax.dynamic_slice_in_dim(inv_std, own_start, own_rows, 0)
    ln1_all = (normed * ln1_gain + ln1_bias).astype(jnp.bfloat16)
    ln2_all = (normed * ln2_gain + ln2_bias).astype(jnp.bfloat16)
    part_one = ln1_all
    part_two = ln2_all
    first_sums = lax.psum_scatter(
        jnp.concatenate(
            [
                jnp.dot(part_one, qkv_weight, preferred_element_type=jnp.float32),
                jnp.dot(part_two, fc1_weight, preferred_element_type=jnp.float32),
            ],
            axis=1,
        ),
        "row",
        scatter_dimension=0,
        tiled=True,
    )
    qkv_out = first_sums[:, :qkv_cols] + qkv_bias
    hidden = first_sums[:, qkv_cols:] + fc1_bias
    slab_source = (
        lax.dynamic_index_in_dim(deal_here, row_id, 0, keepdims=False) * row_count + row_id
    )
    seq_lengths = lax.dynamic_index_in_dim(lengths, slab_source, 0, keepdims=False)
    sequence_ids, positions = segment_layout(seq_lengths, slab_rows)
    token_place = jnp.arange(slab_rows, dtype=jnp.int32)
    cos_table, sin_table = rotary_tables(positions)
    packed = qkv_out.reshape(slab_rows, heads_here, 3, HD)
    query_pre = packed[:, :, 0]
    key_pre = packed[:, :, 1]
    queries = rotate(query_pre, cos_table, sin_table).astype(jnp.bfloat16)
    keys_rot = rotate(key_pre, cos_table, sin_table).astype(jnp.bfloat16)
    values = packed[:, :, 2].astype(jnp.bfloat16)

    def block_scores(block_id):
        first_row = block_id * QBLK
        last_row = first_row + QBLK
        allowed = (sequence_ids[first_row:last_row, None] == sequence_ids[None, :last_row]) & (
            token_place[None, :last_row] <= token_place[first_row:last_row, None]
        )
        scores = (
            jnp.einsum("qhd,khd->hqk", queries, keys_rot, preferred_element_type=jnp.float32)
            * score_scale
        )
        return jnp.where(allowed[None], scores, masked_score)

    block_id = 0
    last_row = (block_id + 1) * QBLK
    scores = block_scores(block_id)
    row_top = jnp.max(scores, axis=-1, keepdims=True)
    exp_total = jnp.sum(jnp.exp(scores - row_top), axis=-1, keepdims=True)
    log_total = row_top + jnp.log(exp_total)
    probs_low = jnp.exp(scores - log_total).astype(jnp.bfloat16)
    mixtures = jnp.einsum("hqk,khd->qhd", probs_low, values, preferred_element_type=jnp.float32)
    log_totals = [log_total]
    attn_out = mixtures.reshape(slab_rows, attn_cols).astype(jnp.bfloat16)
    activated = jax.nn.gelu(hidden, approximate=False).astype(jnp.bfloat16)
    attn_all, act_all = (
        lax.all_gather(attn_out, "row", axis=0, tiled=True),
        lax.all_gather(activated, "row", axis=0, tiled=True),
    )
    part_one = attn_all
    part_two = act_all
    branch_sum = lax.psum_scatter(
        jnp.dot(part_one, dense_weight, preferred_element_type=jnp.float32)
        + jnp.dot(part_two, fc2_weight, preferred_element_type=jnp.float32),
        "col",
        scatter_dimension=0,
        tiled=True,
    )
    output = (mine_rows.astype(jnp.float32) + branch_sum + dense_bias + fc2_bias).astype(
        jnp.bfloat16
    )
    grad_all = lax.all_gather(cotangent, "col", axis=0, tiled=True)
    dense_grad = contract_rows(attn_all, grad_all)
    fc2_grad = contract_rows(act_all, grad_all)
    out_bias_grad = jnp.sum(grad_all, axis=0, dtype=jnp.float32)
    grad_block = grad_all
    grad_second = lax.psum_scatter(
        jnp.concatenate(
            [contract_cols(grad_block, dense_weight), contract_cols(grad_block, fc2_weight)], axis=1
        ),
        "row",
        scatter_dimension=0,
        tiled=True,
    )
    grad_mix = grad_second[:, :attn_cols].astype(jnp.bfloat16).reshape(slab_rows, heads_here, HD)
    gelu_back = jax.vjp(partial(jax.nn.gelu, approximate=False), hidden)[1]
    grad_hidden = gelu_back(grad_second[:, attn_cols:])[0]
    grad_key = jnp.zeros((slab_rows, heads_here, HD), jnp.float32)
    grad_value = jnp.zeros((slab_rows, heads_here, HD), jnp.float32)
    block_id = 0
    first_row = block_id * QBLK
    last_row = first_row + QBLK
    probs_full = jnp.exp(block_scores(block_id) - log_totals[block_id])
    probs_low = probs_full.astype(jnp.bfloat16)
    grad_block = grad_mix
    grad_value = grad_value.at[:last_row].add(
        jnp.einsum("hqk,qhd->khd", probs_low, grad_block, preferred_element_type=jnp.float32)
    )
    grad_probs = jnp.einsum("qhd,khd->hqk", grad_block, values, preferred_element_type=jnp.float32)
    centre = jnp.sum(probs_full * grad_probs, axis=-1, keepdims=True)
    grad_scores = (probs_full * (grad_probs - centre)).astype(jnp.bfloat16)
    grad_queries = (
        jnp.einsum("hqk,khd->qhd", grad_scores, keys_rot, preferred_element_type=jnp.float32)
        * score_scale
    )
    grad_key = grad_key.at[:last_row].add(
        jnp.einsum("hqk,qhd->khd", grad_scores, queries, preferred_element_type=jnp.float32)
        * score_scale
    )
    turn_back = jax.vjp(lambda values_in: rotate(values_in, cos_table, sin_table), query_pre)[1]
    grad_query_pre = turn_back(grad_queries)[0]
    grad_key_pre = turn_back(grad_key)[0]
    grad_qkv = jnp.stack([grad_query_pre, grad_key_pre, grad_value], axis=2).reshape(
        slab_rows, qkv_cols
    )
    grad_first = jnp.concatenate([grad_qkv, grad_hidden], axis=1).astype(jnp.bfloat16)
    grad_first_all = lax.all_gather(grad_first, "row", axis=0, tiled=True)
    grad_qkv_all = grad_first_all[:, :qkv_cols]
    grad_hidden_all = grad_first_all[:, qkv_cols:]
    qkv_weight_grad = contract_rows(ln1_all, grad_qkv_all)
    qkv_bias_grad = jnp.sum(grad_qkv_all, axis=0, dtype=jnp.float32)
    fc1_weight_grad = contract_rows(ln2_all, grad_hidden_all)
    fc1_bias_grad = jnp.sum(grad_hidden_all, axis=0, dtype=jnp.float32)
    grad_block = grad_first_all
    summed = lax.psum_scatter(
        jnp.concatenate(
            [
                contract_cols(grad_block[:, :qkv_cols], qkv_weight),
                contract_cols(grad_block[:, qkv_cols:], fc1_weight),
            ],
            axis=1,
        ),
        "col",
        scatter_dimension=0,
        tiled=True,
    )
    grad_ln_one = summed[:, :own_feats]
    grad_ln_two = summed[:, own_feats:]
    gain_terms = (
        jnp.sum(grad_ln_one * normed_own, axis=0),
        jnp.sum(grad_ln_one, axis=0),
        jnp.sum(grad_ln_two * normed_own, axis=0),
        jnp.sum(grad_ln_two, axis=0),
    )
    grad_normed = grad_ln_one * ln1_gain + grad_ln_two * ln2_gain
    row_sums = lax.psum(
        (jnp.sum(grad_normed, axis=1), jnp.sum(grad_normed * normed_own, axis=1)), "row"
    )
    grad_dealt = cotangent.astype(jnp.float32) + inv_std_own[:, None] * (
        grad_normed - row_sums[0][:, None] / D - normed_own * row_sums[1][:, None] / D
    )
    gain_sums = lax.psum(
        (gain_terms[0], gain_terms[1], gain_terms[2], gain_terms[3]), ("dp", "col")
    )
    weights_summed = lax.psum(
        (
            qkv_weight_grad,
            qkv_bias_grad,
            dense_grad,
            fc1_weight_grad,
            fc1_bias_grad,
            fc2_grad,
            out_bias_grad,
        ),
        "dp",
    )
    pool_back = lax.all_gather(grad_dealt, "dp", axis=0, tiled=True).reshape(
        dp_count, own_rows, own_feats
    )
    back_here = jnp.sum(
        jnp.where(deal_table == group_id, jnp.arange(dp_count, dtype=jnp.int32)[None, :], 0), axis=1
    )
    target = jnp.sum(jnp.where(slab_hits, back_here[None, :], 0), axis=1)
    input_grad = pick_rows(pool_back, target)
    return (
        output,
        input_grad,
        gain_sums[0],
        gain_sums[1],
        weights_summed[0],
        weights_summed[1],
        weights_summed[2],
        weights_summed[6],
        gain_sums[2],
        gain_sums[3],
        weights_summed[3],
        weights_summed[4],
        weights_summed[5],
        weights_summed[6],
    )


UNIT = 256
TILE = 512


def product(left, right, dims):
    return lax.dot_general(left, right, (dims, ((), ())), preferred_element_type=F32)


def fold_lanes(values):
    total = values[:, :128]
    for at in range(128, values.shape[1], 128):
        total = total + values[:, at : at + 128]
    return total


class Copies:
    def __init__(self, send_sems, recv_sems):
        self.send_sems, self.recv_sems, self.used = send_sems, recv_sems, 0

    def make(self, source, target, device):
        number = self.used
        self.used += 1

        def build():
            return pltpu.make_async_remote_copy(
                src_ref=source(),
                dst_ref=target(),
                send_sem=self.send_sems.at[number],
                recv_sem=self.recv_sems.at[number],
                device_id=device,
                device_id_type=pl.DeviceIdType.MESH,
            )

        return build


def attention_head(qkv, back, cos, low, high, allowed):
    scale = 1.0 / math.sqrt(HD)

    def turn(values):
        return values * cos + pltpu.roll(values, HD - 16, 1) * low + pltpu.roll(values, 16, 1) * high

    def turn_back(values):
        return (
            values * cos
            + pltpu.roll(values * high, HD - 16, 1)
            + pltpu.roll(values * low, 16, 1)
        )

    query = turn(qkv[:, :HD]).astype(BF16)
    key = turn(qkv[:, HD : 2 * HD]).astype(BF16)
    value = qkv[:, 2 * HD :].astype(BF16)
    scores = product(query, key, ((1,), (1,))) * scale
    scores = jnp.where(allowed, scores, masked_score)
    weight = jnp.exp(scores - jnp.max(scores, axis=1, keepdims=True))
    probs = weight * (1.0 / jnp.sum(weight, axis=1, keepdims=True))
    probs_low = probs.astype(BF16)
    attn = product(probs_low, value, ((1,), (0,))).astype(BF16)
    grad_probs = product(back, value, ((1,), (1,)))
    centre = jnp.sum(probs * grad_probs, axis=1, keepdims=True)
    grad_scores = (probs * (grad_probs - centre)).astype(BF16)
    grad_query = product(grad_scores, key, ((1,), (0,))) * scale
    grad_key = product(grad_scores, query, ((0,), (0,))) * scale
    grad_value = product(probs_low, back, ((0,), (0,)))
    return attn, [turn_back(grad_query), turn_back(grad_key), grad_value]


def layer_kernel(
    lengths,
    deal_table,
    x_own,
    cot_in,
    norm_own,
    qkv_bias,
    fc1_bias,
    out_bias,
    turns,
    qkv_w,
    dense_w,
    fc1_w,
    fc2_w,
    first_sum,
    second_sum,
    output,
    input_grad,
    small_sum,
    grad_norm,
    cot_own,
    stats,
    x_all,
    cot_all,
    ln1,
    ln2,
    w1,
    w2,
    acts,
    grads,
    first_part,
    second_part,
    out_part,
    out_core,
    out_chip,
    out_x,
    out_half,
    out_y,
    out_item,
    dx_part,
    dx_core,
    dx_chip,
    dx_x,
    dx_half,
    dx_y,
    cot_up,
    cot_down,
    cot_far,
    cot_send,
    cot_edge,
    out_up,
    out_down,
    out_far,
    out_send,
    out_edge,
    acc,
    norm_all,
    first_in,
    second_in,
    first_other,
    second_other,
    first_slot,
    second_slot,
    sum_acc,
    unit_sums,
    small_part,
    small_row,
    small_units,
    small_col,
    small_here,
    small_in,
    small_half,
    small_other,
    row_part,
    row_sums,
    send_sems,
    recv_sems,
    local_sems,
):
    z, r, c = lax.axis_index("dp"), lax.axis_index("row"), lax.axis_index("col")
    y, core = r // 2, r % 2
    mid = ((z + 1) // 2) % 2
    upper = z // 2
    z_in = mid * (3 - z) + (1 - mid) * (1 + upper)
    z_out = 3 * upper
    is_mid, is_edge = mid == 1, mid == 0
    peer = [r, 2 * y + (1 - core), 2 * (1 - y) + core, 2 * (1 - y) + (1 - core)]
    slabs, slab, feats = x_own.shape
    own_rows = slabs * slab
    rows = 2 * own_rows
    hidden_here = fc1_w.shape[1] // 4
    qkv_here = qkv_w.shape[1] // 4
    attn_here = dense_w.shape[0] // 4
    to_row = [{"row": peer[j]} for j in range(4)]
    to_col = {"col": 1 - c}
    to_in = {"dp": z_in}
    to_out = {"dp": z_out}
    copies = Copies(send_sems, recv_sems)
    sent = []

    barrier = pltpu.get_barrier_semaphore()

    def greet(device):
        pl.semaphore_signal(barrier, inc=1, device_id=device, device_id_type=pl.DeviceIdType.MESH)

    for j in (1, 2, 3):
        greet(to_row[j])
    greet(to_col)
    greet(to_in)

    @pl.when(is_mid)
    def _():
        greet(to_out)
        pl.semaphore_wait(barrier, 6)

    @pl.when(is_edge)
    def _():
        pl.semaphore_wait(barrier, 5)

    def start(copy):
        copy().start()
        sent.append(copy)

    def when(flag, action):
        pl.when(flag)(action)

    local_used = [0]

    def local(source, target):
        number = local_used[0]
        local_used[0] += 1

        def build():
            return pltpu.make_async_copy(source(), target(), local_sems.at[number])

        build().start()
        return build

    own_half = pl.ds(c * own_rows, own_rows)
    far_half = pl.ds((1 - c) * own_rows, own_rows)

    class Gather:
        def __init__(self, own, whole, by_row):
            self.own, self.whole = own, whole

            def place(j, half, q):
                return lambda: whole.at[peer[j], slabs * half + q]

            def own_slab(q):
                return lambda: own.at[q]

            ids = range(slabs)
            self.to_y = [copies.make(own_slab(q), place(0, c, q), to_row[2]) for q in ids]
            self.to_x = [copies.make(own_slab(q), place(0, c, q), to_col) for q in ids]
            self.to_core = [copies.make(own_slab(q), place(0, c, q), to_row[1]) for q in ids]
            self.y_core = [copies.make(place(2, c, q), place(2, c, q), to_row[1]) for q in ids]
            self.x_core = [
                copies.make(place(0, 1 - c, q), place(0, 1 - c, q), to_row[1]) for q in ids
            ]
            self.far_core = [
                copies.make(place(2, 1 - c, q), place(2, 1 - c, q), to_row[1]) for q in ids
            ]
            self.by_row = by_row
            self.far = [
                copies.make(place(0, 1 - c, q), place(0, 1 - c, q), to_row[2])
                if q in by_row
                else copies.make(place(2, c, q), place(2, c, q), to_col)
                for q in ids
            ]
            self.kept = [None] * slabs

        def begin(self, q):
            start(self.to_y[q])
            start(self.to_x[q])
            start(self.to_core[q])
            self.kept[q] = local(
                lambda: self.own.at[q], lambda: self.whole.at[r, slabs * c + q]
            )

        def after_y(self, q):
            self.to_y[q]().wait_recv()
            if q not in self.by_row:
                start(self.far[q])
            start(self.y_core[q])

        def after_x(self, q):
            self.to_x[q]().wait_recv()
            if q in self.by_row:
                start(self.far[q])
            start(self.x_core[q])

        def after_far(self, q):
            self.far[q]().wait_recv()
            start(self.far_core[q])

        def end(self, q):
            self.kept[q]().wait()
            for group in (self.to_core, self.y_core, self.x_core, self.far_core):
                group[q]().wait_recv()

    def choose(q, goes, plane, refs, target):
        def body(*blocks):
            value = blocks[0][...]
            for (source, _), block in zip(refs[1:], blocks[1:]):
                value = jnp.where(goes(q, source, plane), block[...], value)
            blocks[-1][...] = value

        tile = slab // 4
        block = pl.BlockSpec((tile, feats), lambda i: (i, 0))
        pltpu.emit_pipeline(
            body, grid=(4,), in_specs=[block] * len(refs), out_specs=[block]
        )(*[ref.at[q] for _, ref in refs], target.at[q])

    class Route:
        def __init__(self, item, goes, up, down, far, send, edge, target):
            self.item, self.goes, self.up, self.down = item, goes, up, down
            self.far, self.send, self.edge, self.target = far, send, edge, target

            def at(ref, q):
                return lambda: ref.at[q]

            ids = range(slabs)
            self.upward = [copies.make(at(item, q), at(up, q), {"dp": z + 1}) for q in ids]
            self.downward = [copies.make(at(item, q), at(down, q), {"dp": z - 1}) for q in ids]
            self.far_up = [copies.make(at(up, q), at(far, q), to_in) for q in ids]
            self.far_down = [copies.make(at(down, q), at(far, q), to_in) for q in ids]
            self.outward = [copies.make(at(send, q), at(edge, q), to_out) for q in ids]

        def begin(self, q):
            when(z < 2, lambda: self.upward[q]().start())
            when(z > 1, lambda: self.downward[q]().start())

        def relay(self, q):
            def from_below():
                self.upward[q]().wait_recv()
                self.far_up[q]().start()

            def from_above():
                self.downward[q]().wait_recv()
                self.far_down[q]().start()

            when(z == 1, from_below)
            when(z == 2, from_above)

        def hand_out(self, q):
            def middle():
                def below():
                    self.downward[q]().wait_recv()
                    self.far_down[q]().wait_recv()

                def above():
                    self.upward[q]().wait_recv()
                    self.far_up[q]().wait_recv()

                when(z == 1, below)
                when(z == 2, above)
                refs = [
                    (z, self.item),
                    (z - 1, self.up),
                    (z + 1, self.down),
                    (3 * (2 - z), self.far),
                ]
                choose(q, self.goes, z_out, refs, self.send)
                self.outward[q]().start()
                choose(q, self.goes, z, refs, self.target)

            when(is_mid, middle)

        def take(self, q):
            def edge():
                self.outward[q]().wait_recv()
                block = pl.BlockSpec((slab // 4, feats), lambda i: (i, 0))

                def body(edge_ref, item_ref, target_ref):
                    mine = self.goes(q, z, z)
                    target_ref[...] = jnp.where(mine, item_ref[...], edge_ref[...])

                pltpu.emit_pipeline(
                    body, grid=(4,), in_specs=[block] * 2, out_specs=[block]
                )(self.edge.at[q], self.item.at[q], self.target.at[q])

            when(is_edge, edge)

        def finish(self):
            for q in range(slabs):
                when(z < 2, lambda: self.upward[q]().wait_send())
                when(z > 1, lambda: self.downward[q]().wait_send())
                when(z == 1, lambda: self.far_up[q]().wait_send())
                when(z == 2, lambda: self.far_down[q]().wait_send())
                when(is_mid, lambda: self.outward[q]().wait_send())

    def undealt(q, source, plane):
        return deal_table[slabs * c + q, source] == plane

    def dealt(q, source, plane):
        return deal_table[slabs * c + q, plane] == source

    x_gather = Gather(x_own, x_all, ())
    cot_gather = Gather(cot_own, cot_all, (1,))
    cot_route = Route(
        cot_in, undealt, cot_up, cot_down, cot_far, cot_send, cot_edge, cot_own
    )
    norm_copies = [
        copies.make(lambda: norm_own, lambda: norm_all.at[r], to_row[j]) for j in (1, 2, 3)
    ]

    odd = z % 2
    across_row = 2 * (1 - y) + core + odd * (1 - 2 * core)
    to_across = {"row": across_row}
    to_pair = {"dp": z + 1 - 2 * odd}

    class Fetch:
        def __init__(
            self, paired, first, first_at, first_width, at, second, second_at, second_width, low
        ):
            size = UNIT if first is fc1_w else qkv_here

            def first_source(taker):
                lanes = pl.multiple_of(taker * first_width + first_at, 256)
                return lambda: first.at[:, pl.ds(lanes, size)]

            def second_source(taker):
                begin = pl.multiple_of(taker * second_width + second_at, 256)
                return lambda: second.at[pl.ds(begin, UNIT)]

            def first_target(giver):
                return lambda: w1.at[giver, :, pl.ds(at, size)]

            def second_target(giver):
                return lambda: w2.at[giver, pl.ds(low, UNIT)]

            pairs = ((first_source, first_target), (second_source, second_target))
            self.beside = [copies.make(f(peer[1]), t(r), to_row[1]) for f, t in pairs]
            self.paired = paired
            if paired:
                self.over = [copies.make(f(across_row), t(r), to_across) for f, t in pairs]
                self.shared = [
                    copies.make(t(across_row), t(across_row), to_pair) for _, t in pairs
                ]
            else:
                self.over = [
                    copies.make(f(peer[j]), t(r), to_row[j]) for f, t in pairs for j in (2, 3)
                ]
            self.kept = [(f(r), t(r)) for f, t in pairs]

        def begin(self):
            for copy in self.over + self.beside:
                start(copy)
            self.kept = [local(*pair) for pair in self.kept]

        def share(self):
            if not self.paired:
                return
            for copy, onward in zip(self.over, self.shared):
                copy().wait_recv()
                start(onward)

        def end(self):
            for copy in self.beside + (self.shared if self.paired else self.over):
                copy().wait_recv()
            for copy in self.kept:
                copy().wait()

    attn_fetch = Fetch(False, qkv_w, 0, qkv_here, 0, dense_w, 0, attn_here, 0)
    mlp_fetch = [
        Fetch(at < 2 * UNIT, fc1_w, at, hidden_here, qkv_here + at, fc2_w, at, hidden_here, attn_here + at)
        for at in range(0, hidden_here, UNIT)
    ]

    kinds = [0, 0, 0]
    keep = upper

    class Unit:
        def __init__(self, kind, at, width=UNIT):
            place, offset = kinds[kind] // UNIT, kinds[kind] % UNIT
            kinds[kind] += width
            if kind == 1:
                part, self.total = first_part, first_sum

                def held(ref, index):
                    return ref.at[index, :, :, pl.ds(offset, width)]

                self.arrived, self.other = held(first_in, place), held(first_other, place)
                self.slot = partial(held, first_slot)
                half = feats // 2
                self.whole = lambda: part.at[:, :, pl.ds(at, width)]

                def region(which, index):
                    return self.total.at[index, pl.ds(which * half, half), pl.ds(at, width)]

            else:
                part, self.total = second_part, second_sum
                self.arrived = second_in.at[place, :, pl.ds(offset, width)]
                self.other = second_other.at[place, :, pl.ds(offset // 2, width // 2)]
                self.slot = lambda index: second_slot.at[index, :, pl.ds(offset, width)]
                half = width // 2
                self.whole = lambda: part.at[:, pl.ds(at, width)]

                def region(which, index):
                    return self.total.at[index, pl.ds(at + which * half, half)]

            self.half, self.region = half, region
            every = slice(None)
            self.inward = copies.make(self.whole, lambda: self.arrived, to_in)
            self.across = copies.make(
                lambda: self.arrived.at[:, pl.ds((1 - keep) * half, half)],
                lambda: self.other,
                to_in,
            )
            self.spread = [
                copies.make(
                    partial(lambda j: self.other.at[peer[j]], j),
                    lambda: region(keep, r),
                    to_row[j],
                )
                for j in (1, 2, 3)
            ]
            self.over = copies.make(
                lambda: region(keep, every), lambda: region(keep, every), to_in
            )
            self.outward = [
                copies.make(lambda: region(keep, every), lambda: region(keep, every), to_out),
                copies.make(
                    lambda: region(1 - keep, every), lambda: region(1 - keep, every), to_out
                ),
            ]
            self.load, self.store = local_used[0], local_used[0] + 1
            local_used[0] += 2

        def loading(self, turn):
            return pltpu.make_async_copy(
                self.whole(), self.slot(turn % 2), local_sems.at[self.load]
            )

        def storing(self):
            return pltpu.make_async_copy(
                self.other.at[r], self.region(keep, r), local_sems.at[self.store]
            )

        def add(self, target, term, offset):
            step = 64

            def body(i, carry):
                here = pl.ds(pl.multiple_of(i * step, step), step)
                there = pl.ds(pl.multiple_of(offset + i * step, step), step)
                target[:, here] = (target[:, here].astype(F32) + term[:, there].astype(F32)).astype(BF16)
                return carry

            lax.fori_loop(0, target.shape[1] // step, body, 0)

        def sum_chip_pair(self, turn):
            self.loading(turn).wait()
            self.inward().wait_recv()
            self.add(self.arrived, self.slot(turn % 2), 0)
            self.across().start()

        def sum_line(self):
            self.across().wait_recv()
            self.add(self.other, self.arrived, keep * self.half)
            for copy in self.spread:
                copy().start()
            self.storing().start()

        def pass_kept(self):
            for copy in self.spread:
                copy().wait_recv()
            self.storing().wait()
            self.over().start()
            self.outward[0]().start()

        def pass_other(self):
            self.over().wait_recv()
            self.outward[1]().start()

        def finish(self, unsent):
            def edge():
                for copy in self.outward:
                    copy().wait_recv()
                if unsent:
                    self.inward().wait_send()

            def middle():
                for copy in [self.across, self.over] + self.spread + self.outward:
                    copy().wait_send()

            when(is_edge, edge)
            when(is_mid, middle)

    def chunk_units(at):
        width = UNIT // 2 if at in (0, hidden_here - UNIT) else UNIT
        parts = range(at, at + UNIT, width)
        return [Unit(2, attn_here + part, width) for part in parts] + [
            Unit(1, qkv_here + part, width) for part in parts
        ]

    mlp_units = [chunk_units(at) for at in range(0, hidden_here, UNIT)]
    attn_units = [Unit(2, 0)] + [Unit(1, at) for at in range(0, qkv_here, UNIT)]

    def norm_body(x_ref, one_ref, two_ref, stat_ref):
        wide = jnp.concatenate([x_ref[j, 0] for j in range(4)], axis=1).astype(F32)
        norms = jnp.concatenate([norm_all[j] for j in range(4)], axis=1)
        mean = jnp.sum(wide, axis=1, keepdims=True) / D
        square = jnp.sum(wide * wide, axis=1, keepdims=True) / D
        inv_std = lax.rsqrt(square - mean * mean + norm_epsilon)
        normed = (wide - mean) * inv_std
        one_ref[...] = (normed * norms[0:1] + norms[1:2]).astype(BF16)
        two_ref[...] = (normed * norms[2:3] + norms[3:4]).astype(BF16)
        lane = lax.broadcasted_iota(jnp.int32, stat_ref.shape, 1)
        stat_ref[...] = jnp.where(lane < 64, mean, inv_std)

    def norm_stage():
        tile = 256
        flat = pl.BlockSpec((tile, D), lambda i: (i, 0))
        pltpu.emit_pipeline(
            norm_body,
            grid=(rows // tile,),
            in_specs=[
                pl.BlockSpec(
                    (4, 1, tile, feats), lambda i: (0, i * tile // slab, i % (slab // tile), 0)
                )
            ],
            out_specs=[flat, flat, pl.BlockSpec((tile, 128), lambda i: (i, 0))],
        )(x_all, ln1, ln2, stats)

    def mlp_stage(k):
        at = k * UNIT
        bias = fc1_bias[r, :, at : at + UNIT]

        def body(ln_ref, cot_ref, first_ref, second_ref, act_ref, grad_ref):
            step = pl.program_id(0)

            @pl.when(step == 0)
            def _():
                acc[:, : 2 * UNIT, :] = jnp.zeros((4, 2 * UNIT, feats), F32)
                sum_acc[:, :UNIT] = jnp.zeros((8, UNIT), F32)

            hidden = bias
            grad_act = None
            for j in range(4):
                lanes = slice(j * feats, (j + 1) * feats)
                hidden = hidden + product(ln_ref[:, lanes], first_ref[j], ((1,), (0,)))
                term = product(cot_ref[j, 0], second_ref[j], ((1,), (1,)))
                grad_act = term if j == 0 else grad_act + term
            curve = 0.5 * (1.0 + lax.erf(hidden * math.sqrt(0.5)))
            bell = jnp.exp(-0.5 * hidden * hidden) * (1.0 / math.sqrt(2.0 * math.pi))
            act = (hidden * curve).astype(BF16)
            grad_hidden = (grad_act * (curve + hidden * bell)).astype(BF16)
            act_ref[...] = act
            grad_ref[...] = grad_hidden
            sum_acc[0:1, :UNIT] += jnp.sum(grad_hidden.astype(F32), axis=0, keepdims=True)
            for j in range(4):
                lanes = slice(j * feats, (j + 1) * feats)
                acc[j, :UNIT] += product(act, cot_ref[j, 0], ((0,), (0,)))
                acc[j, UNIT : 2 * UNIT] += product(grad_hidden, ln_ref[:, lanes], ((0,), (0,)))

        pltpu.emit_pipeline(
            body,
            grid=(rows // TILE,),
            in_specs=[
                pl.BlockSpec((TILE, D), lambda i: (i, 0)),
                pl.BlockSpec((4, 1, slab, feats), lambda i: (0, i, 0, 0)),
                pl.BlockSpec((4, feats, UNIT), lambda i: (0, 0, (qkv_here + at) // UNIT)),
                pl.BlockSpec((4, UNIT, feats), lambda i: (0, (attn_here + at) // UNIT, 0)),
            ],
            out_specs=[
                pl.BlockSpec((TILE, UNIT), lambda i: (i, (attn_here + at) // UNIT)),
                pl.BlockSpec((TILE, UNIT), lambda i: (i, (qkv_here + at) // UNIT)),
            ],
        )(ln2, cot_all, w1, w2, acts, grads)
        grad_stage(UNIT, qkv_here + at, attn_here + at, 1, k == 0)
        unit_sums[0:1, qkv_here + at : qkv_here + at + UNIT] = sum_acc[0:1, :UNIT]

    def grad_stage(width, first_at, second_at, which, fresh):
        def body(first_ref, part_one, part_two):
            j = pl.program_id(0)
            grad = acc[j, UNIT : UNIT + width].T
            weight = first_ref[0].astype(F32)
            part_one[0] = grad.astype(BF16)
            part_two[0] = acc[j, :UNIT].astype(BF16)
            terms = [fold_lanes(grad * weight), fold_lanes(weight * sum_acc[0:1, :width])]
            ones = jnp.ones((8, 128), F32)
            for k in (0, 1):
                sums = lax.dot_general(
                    ones,
                    terms[k],
                    (((1,), (1,)), ((), ())),
                    precision=lax.Precision.HIGHEST,
                    preferred_element_type=F32,
                )[0:1]
                at = 2 * which + k
                if not fresh:
                    sums = sums + small_part[j, at : at + 1]
                small_part[j, at : at + 1] = sums

        lanes = slice(first_at, first_at + width)
        block = pl.BlockSpec((1, feats, width), lambda j: (j, 0, 0))
        pltpu.emit_pipeline(
            body,
            grid=(4,),
            in_specs=[block],
            out_specs=[block, pl.BlockSpec((1, UNIT, feats), lambda j: (j, second_at // UNIT, 0))],
        )(w1.at[:, :, lanes], first_part.at[:, :, lanes], second_part)

    def attention_slab(s):
        once = pl.Buffered(1)
        heads = qkv_here // (3 * HD)
        bias = qkv_bias[r]

        def body(ln_ref, cot_ref, first_ref, second_ref, act_ref, grad_ref):
            qkv = bias
            back = None
            for j in range(4):
                lanes = slice(j * feats, (j + 1) * feats)
                qkv = qkv + product(ln_ref[:, lanes], first_ref[j], ((1,), (0,)))
                term = product(cot_ref[j, 0], second_ref[j], ((1,), (1,)))
                back = term if j == 0 else back + term
            back = back.astype(BF16)
            at = lax.broadcasted_iota(jnp.int32, (TILE, TILE), 0)
            of = lax.broadcasted_iota(jnp.int32, (TILE, TILE), 1)
            token = lax.broadcasted_iota(jnp.int32, (TILE, HD), 0)
            lane = lax.broadcasted_iota(jnp.int32, (TILE, HD), 1)
            begin = jnp.zeros((TILE, HD), jnp.int32)
            edge = 0
            for k in range(lengths.shape[1] - 1):
                edge = edge + lengths[4 * z + s, k]
                begin = jnp.where(token >= edge, edge, begin)
            allowed = (of <= at) & (of >= begin[:, :1])
            angle = (token - begin).astype(F32) * turns[0:1]
            cos, sin = jnp.cos(angle), jnp.sin(angle)
            low = jnp.where(lane < ROT // 2, -sin, 0.0)
            high = jnp.where(lane < ROT // 2, 0.0, sin)
            for h in range(heads):
                attn, grads_here = attention_head(
                    qkv[:, h * 3 * HD : (h + 1) * 3 * HD],
                    back[:, h * HD : (h + 1) * HD],
                    cos,
                    low,
                    high,
                    allowed,
                )
                act_ref[:, h * HD : (h + 1) * HD] = attn
                for i in range(3):
                    at_lane = (h * 3 + i) * HD
                    grad_ref[:, at_lane : at_lane + HD] = grads_here[i].astype(BF16)
            attn, grad = act_ref[...], grad_ref[...]
            sums = jnp.sum(grad.astype(F32), axis=0, keepdims=True)
            sum_acc[0:1, :qkv_here] = sums if s == 0 else sum_acc[0:1, :qkv_here] + sums
            for j in range(4):
                lanes = slice(j * feats, (j + 1) * feats)
                second_term = product(attn, cot_ref[j, 0], ((0,), (0,)))
                first_term = product(grad, ln_ref[:, lanes], ((0,), (0,)))
                acc[j, :UNIT] = second_term if s == 0 else acc[j, :UNIT] + second_term
                acc[j, UNIT:] = first_term if s == 0 else acc[j, UNIT:] + first_term

        pltpu.emit_pipeline(
            body,
            grid=(1,),
            in_specs=[
                pl.BlockSpec((TILE, D), lambda i: (s, 0), pipeline_mode=once),
                pl.BlockSpec((4, 1, slab, feats), lambda i: (0, s, 0, 0), pipeline_mode=once),
                pl.BlockSpec((4, feats, qkv_here), lambda i: (0, 0, 0), pipeline_mode=once),
                pl.BlockSpec((4, UNIT, feats), lambda i: (0, 0, 0), pipeline_mode=once),
            ],
            out_specs=[
                pl.BlockSpec((TILE, UNIT), lambda i: (s, 0), pipeline_mode=once),
                pl.BlockSpec((TILE, qkv_here), lambda i: (s, 0), pipeline_mode=once),
            ],
        )(
            ln1,
            cot_all,
            w1.at[:, :, :qkv_here],
            w2,
            acts,
            grads.at[:, :qkv_here],
        )
        if s == 3:
            grad_stage(qkv_here, 0, 0, 0, True)
            unit_sums[0:1, :qkv_here] = sum_acc[0:1, :qkv_here]

    def out_stage(n):
        def body(act_ref, second_ref, part_ref):
            part_ref[0] = product(act_ref[...], second_ref[0], ((1,), (0,))).astype(BF16)

        pltpu.emit_pipeline(
            body,
            grid=(rows // TILE,),
            in_specs=[
                pl.BlockSpec((TILE, acts.shape[1]), lambda i: (i, 0)),
                pl.BlockSpec((1, w2.shape[1], feats), lambda i: (n, 0, 0)),
            ],
            out_specs=[pl.BlockSpec((1, TILE, feats), lambda i: (n, i, 0))],
        )(acts, w2, out_part)

    def dx_stage(n):
        def body(grad_ref, first_ref, part_ref):
            norms = norm_all[n]
            one = product(grad_ref[:, :qkv_here], first_ref[0, :, :qkv_here], ((1,), (1,)))
            two = product(grad_ref[:, qkv_here:], first_ref[0, :, qkv_here:], ((1,), (1,)))
            part_ref[0] = (one * norms[0:1] + two * norms[2:3]).astype(BF16)

        pltpu.emit_pipeline(
            body,
            grid=(rows // TILE,),
            in_specs=[
                pl.BlockSpec((TILE, grads.shape[1]), lambda i: (i, 0)),
                pl.BlockSpec((1, feats, w1.shape[2]), lambda i: (n, 0, 0)),
            ],
            out_specs=[pl.BlockSpec((1, TILE, feats), lambda i: (n, i, 0))],
        )(grads, w1, dx_part)

    class Scatter:
        def __init__(self, part, from_core, chip, from_x, half, from_y):
            self.part, self.from_core, self.chip = part, from_core, chip
            self.from_x, self.half, self.from_y = from_x, half, from_y
            self.to_core = [
                copies.make(
                    partial(lambda j: part.at[peer[j]], j),
                    partial(lambda j: from_core.at[peer[j] // 2], j),
                    to_row[1],
                )
                for j in (1, 3)
            ]
            self.to_x = copies.make(
                lambda: chip.at[:, far_half], lambda: from_x, to_col
            )
            self.to_y = copies.make(lambda: half.at[1 - y], lambda: from_y, to_row[2])

        def begin(self):
            for copy in self.to_core:
                start(copy)

        def second(self):
            for copy in self.to_core:
                copy().wait_recv()

            def body(left, right, target):
                target[...] = (left[...].astype(F32) + right[...].astype(F32)).astype(BF16)

            block = pl.BlockSpec((1, TILE, feats), lambda s, i: (s, i, 0))
            pltpu.emit_pipeline(
                body,
                grid=(2, rows // TILE),
                in_specs=[
                    pl.BlockSpec((1, TILE, feats), lambda s, i: (2 * s + core, i, 0)),
                    block,
                ],
                out_specs=[block],
            )(self.part, self.from_core, self.chip)
            start(self.to_x)

        def third(self):
            self.to_x().wait_recv()

            def body(left, right, target):
                target[...] = (left[...].astype(F32) + right[...].astype(F32)).astype(BF16)

            block = pl.BlockSpec((1, TILE, feats), lambda s, i: (s, i, 0))
            tiles = own_rows // TILE
            pltpu.emit_pipeline(
                body,
                grid=(2, tiles),
                in_specs=[
                    pl.BlockSpec((1, TILE, feats), lambda s, i: (s, c * tiles + i, 0)),
                    block,
                ],
                out_specs=[block],
            )(self.chip, self.from_x, self.half)
            start(self.to_y)

        def last(self, body, extra, target):
            self.to_y().wait_recv()
            flat = pl.BlockSpec((1, slab, feats), lambda i: (i, 0, 0))
            pltpu.emit_pipeline(
                body,
                grid=(own_rows // TILE,),
                in_specs=[
                    pl.BlockSpec((1, TILE, feats), lambda i: (y, i, 0)),
                    pl.BlockSpec((TILE, feats), lambda i: (i, 0)),
                    flat,
                ],
                out_specs=[flat],
            )(self.half, self.from_y, extra, target)

    out_scatter = Scatter(out_part, out_core, out_chip, out_x, out_half, out_y)
    dx_scatter = Scatter(dx_part, dx_core, dx_chip, dx_x, dx_half, dx_y)
    out_route = Route(
        out_item, dealt, out_up, out_down, out_far, out_send, out_edge, output
    )

    def finish_output():
        def body(half_ref, y_ref, x_ref, item_ref):
            item_ref[0] = (
                half_ref[0].astype(F32)
                + y_ref[...].astype(F32)
                + x_ref[0].astype(F32)
                + out_bias[0:1]
            ).astype(BF16)

        out_scatter.last(body, x_own, out_item)

    row_copies = [
        copies.make(lambda: row_part, lambda: row_sums.at[r], to_row[j]) for j in (1, 2, 3)
    ]

    def sum_grad():
        dx_scatter.to_y().wait_recv()

        def body(half_ref, y_ref, x_ref, stat_ref, target_ref):
            grad = half_ref[0].astype(F32) + y_ref[...].astype(F32)
            target_ref[...] = grad
            normed = (x_ref[0].astype(F32) - stat_ref[:, :1]) * stat_ref[:, 127:]
            one = jnp.sum(grad, axis=1, keepdims=True)
            two = jnp.sum(grad * normed, axis=1, keepdims=True)
            lane = lax.broadcasted_iota(jnp.int32, (TILE, 128), 1)
            both = jnp.where(lane == 0, one, jnp.where(lane == 1, two, 0.0))
            row_part[pl.program_id(0)] = both.T[:8]

        pltpu.emit_pipeline(
            body,
            grid=(own_rows // TILE,),
            in_specs=[
                pl.BlockSpec((1, TILE, feats), lambda i: (y, i, 0)),
                pl.BlockSpec((TILE, feats), lambda i: (i, 0)),
                pl.BlockSpec((1, slab, feats), lambda i: (i, 0, 0)),
                pl.BlockSpec((TILE, 128), lambda i: (slabs * c + i, 0)),
            ],
            out_specs=[pl.BlockSpec((TILE, feats), lambda i: (i, 0))],
        )(dx_half, dx_y, x_own, stats, grad_norm)
        for copy in row_copies:
            start(copy)
        row_sums[r] = row_part[...]

    def finish_grad():
        for copy in row_copies:
            copy().wait_recv()

        def body(grad_ref, cot_ref, x_ref, stat_ref, target_ref):
            step = pl.program_id(0)
            sums = row_sums[0, step] + row_sums[1, step] + row_sums[2, step] + row_sums[3, step]
            sums = jnp.concatenate([sums, jnp.zeros((120, TILE), F32)], axis=0).T * (1.0 / D)
            normed = (x_ref[0].astype(F32) - stat_ref[:, :1]) * stat_ref[:, 127:]
            target_ref[0] = cot_ref[0].astype(F32) + stat_ref[:, 127:] * (
                grad_ref[...] - sums[:, 0:1] - normed * sums[:, 1:2]
            )

        flat = pl.BlockSpec((1, slab, feats), lambda i: (i, 0, 0))
        pltpu.emit_pipeline(
            body,
            grid=(own_rows // TILE,),
            in_specs=[
                pl.BlockSpec((TILE, feats), lambda i: (i, 0)),
                flat,
                flat,
                pl.BlockSpec((TILE, 128), lambda i: (slabs * c + i, 0)),
            ],
            out_specs=[flat],
        )(grad_norm, cot_own, x_own, stats, input_grad)

    sums_wide = small_units.shape[2]
    small_copies = [
        copies.make(
            partial(lambda j: small_part.at[peer[j]], j), lambda: small_row.at[r], to_row[j]
        )
        for j in (1, 2, 3)
    ]
    unit_copies = [
        copies.make(lambda: unit_sums, lambda: small_units.at[r], to_row[j]) for j in (1, 2, 3)
    ]
    col_copy = copies.make(
        lambda: small_here.at[:, pl.ds(sums_wide, feats)], lambda: small_col, to_col
    )
    small_inward = copies.make(lambda: small_here, lambda: small_in, to_in)
    small_across = copies.make(lambda: small_half, lambda: small_other, to_in)
    small_outward = copies.make(lambda: small_in, lambda: small_in, to_out)

    def small_begin():
        small_part[:, 4:] = jnp.zeros((4, 4, feats), F32)
        for copy in small_copies + unit_copies:
            start(copy)
        small_row[r] = small_part[r]
        small_units[r] = unit_sums[...]

    def small_second():
        for copy in small_copies + unit_copies:
            copy().wait_recv()
        small_here[...] = jnp.zeros(small_here.shape, F32)
        for j in range(4):
            small_here[j : j + 1, :sums_wide] = small_units[j, 0:1]
        small_here[:, sums_wide:] = small_row[0] + small_row[1] + small_row[2] + small_row[3]

        def body(cot_ref):
            total = jnp.sum(cot_ref[0].astype(F32), axis=0, keepdims=True)
            small_here[4:5, sums_wide:] += total

        pltpu.emit_pipeline(
            body,
            grid=(slabs,),
            in_specs=[pl.BlockSpec((1, slab, feats), lambda i: (i, 0, 0))],
        )(cot_own)
        start(col_copy)

    def small_third():
        col_copy().wait_recv()
        col_copy().wait_send()
        small_here[:, sums_wide:] += small_col[...]
        when(is_edge, lambda: small_inward().start())

    def small_halve():
        def middle():
            small_inward().wait_recv()
            small_half[...] = small_here[...] + small_in[...]
            small_across().start()

        when(is_mid, middle)

    def small_close():
        def middle():
            small_across().wait_recv()
            small_in[...] = small_half[...] + small_other[...]
            small_outward().start()

        when(is_mid, middle)

    def small_finish():
        def edge():
            small_outward().wait_recv()
            small_inward().wait_send()

        def middle():
            small_across().wait_send()
            small_outward().wait_send()

        when(is_edge, edge)
        when(is_mid, middle)
        total = small_in[...]
        small_sum[:, :sums_wide] = total[:, :sums_wide]
        norms = norm_own[...]
        sums = total[:, sums_wide:]
        gains = [
            (sums[k : k + 1] - norms[k + 1 : k + 2] * sums[k + 1 : k + 2]) / norms[k : k + 1]
            for k in (0, 2)
        ]
        small_sum[:, sums_wide:] = jnp.concatenate(
            [gains[0], sums[1:2], gains[1], sums[3:4], sums[4:]], axis=0
        )

    line = []
    begun, loaded, served = [0], [0], [0]
    flight = 2

    def lead():
        while begun[0] < min(len(line), served[0] + 2):
            at = begun[0]

            def edge():
                if at >= flight:
                    line[at - flight].inward().wait_send()
                line[at].inward().start()

            when(is_edge, edge)
            begun[0] += 1
        while loaded[0] < min(len(line), served[0] + 2):
            at = loaded[0]
            when(is_mid, lambda: line[at].loading(at).start())
            loaded[0] += 1

    def queue(units):
        line.extend(units)
        lead()

    def serve(count, closing=False):
        for _ in range(count):
            at = served[0]
            if at >= len(line) and not closing:
                return
            lead()

            def middle():
                if 0 <= at - 3 < len(line):
                    line[at - 3].pass_other()
                if 0 <= at - 2 < len(line):
                    line[at - 2].pass_kept()
                if 0 <= at - 1 < len(line):
                    line[at - 1].sum_line()
                if at < len(line):
                    line[at].sum_chip_pair(at)

            when(is_mid, middle)
            served[0] += 1
            lead()

    slab_ids = range(slabs)
    for q in slab_ids:
        x_gather.begin(q)
    cot_route.begin(0)
    norm_all[r] = norm_own[...]
    for copy in norm_copies:
        start(copy)
    cot_route.relay(0)
    cot_route.begin(1)
    for q in slab_ids:
        x_gather.after_y(q)
    mlp_fetch[0].begin()
    cot_route.relay(1)
    cot_route.hand_out(0)
    for q in slab_ids:
        x_gather.after_x(q)
    cot_route.take(0)
    cot_gather.begin(0)
    cot_route.hand_out(1)
    mlp_fetch[0].share()
    for q in slab_ids:
        x_gather.after_far(q)
    cot_route.take(1)
    cot_gather.begin(1)
    mlp_fetch[1].begin()
    cot_gather.after_y(0)
    cot_gather.after_x(0)
    cot_gather.after_y(1)
    cot_gather.after_x(1)
    for q in slab_ids:
        x_gather.end(q)
    for copy in norm_copies:
        copy().wait_recv()
    mlp_fetch[1].share()
    norm_stage()
    for q in slab_ids:
        cot_gather.after_far(q)
    mlp_fetch[2].begin()
    for q in slab_ids:
        cot_gather.end(q)
    mlp_fetch[0].end()
    mlp_stage(0)
    queue(mlp_units[0])
    mlp_fetch[2].share()
    attn_fetch.begin()
    mlp_fetch[1].end()
    mlp_stage(1)
    queue(mlp_units[1])
    serve(1)
    mlp_fetch[2].end()
    mlp_stage(2)
    mlp_fetch[3].begin()
    queue(mlp_units[2])
    serve(2)
    attn_fetch.end()
    attention_slab(0)
    serve(1)
    attention_slab(1)
    serve(1)
    attention_slab(2)
    serve(1)
    attention_slab(3)
    queue(attn_units)
    serve(1)
    mlp_fetch[3].end()
    mlp_stage(3)
    queue(mlp_units[3])
    serve(1)
    out_stage(0)
    out_stage(1)
    serve(1)
    out_stage(2)
    out_stage(3)
    out_scatter.begin()
    serve(1)
    dx_stage(0)
    out_scatter.second()
    dx_stage(1)
    serve(1)
    dx_stage(2)
    dx_stage(3)
    dx_scatter.begin()
    serve(1)
    small_begin()
    serve(1)
    out_scatter.third()
    small_second()
    serve(1)
    finish_output()
    out_route.begin(0)
    dx_scatter.second()
    small_third()
    serve(1)
    out_route.relay(0)
    out_route.begin(1)
    small_halve()
    serve(1)
    out_route.relay(1)
    out_route.hand_out(0)
    serve(1)
    small_close()
    dx_scatter.third()
    serve(1)
    out_route.hand_out(1)
    serve(1)
    sum_grad()
    serve(1, True)
    out_route.take(0)
    finish_grad()
    serve(1, True)
    out_route.take(1)
    while served[0] < len(line) + 3:
        serve(1, True)
    for at, unit in enumerate(line):
        unit.finish(at >= len(line) - flight)
    small_finish()
    cot_route.finish()
    out_route.finish()
    for copy in sent:
        if copy is not col_copy:
            copy().wait_send()


def widen_body(first_ref, dense_ref, fc2_ref, qkv_out, fc1_out, dense_out, fc2_out):
    qkv_here = qkv_out.shape[1]
    qkv_out[...] = first_ref[0, :, :qkv_here].astype(F32)
    fc1_out[...] = first_ref[0, :, qkv_here:].astype(F32)
    dense_out[...] = dense_ref[0].astype(F32)
    fc2_out[...] = fc2_ref[0].astype(F32)


def widen(first_sum, second_sum, qkv_here, attn_here):
    feats, first_cols = first_sum.shape[1:]
    hidden_here = first_cols - qkv_here
    tiles = hidden_here // attn_here
    tile = feats // tiles
    return pl.pallas_call(
        widen_body,
        grid=(4, tiles),
        in_specs=[
            pl.BlockSpec((1, tile, first_cols), lambda s, i: (s, i, 0)),
            pl.BlockSpec((1, attn_here // tiles, feats), lambda s, i: (s, i, 0)),
            pl.BlockSpec((1, attn_here, feats), lambda s, i: (s, 1 + i, 0)),
        ],
        out_specs=[
            pl.BlockSpec((tile, qkv_here), lambda s, i: (i, s)),
            pl.BlockSpec((tile, hidden_here), lambda s, i: (i, s)),
            pl.BlockSpec((attn_here // tiles, feats), lambda s, i: (s * tiles + i, 0)),
            pl.BlockSpec((attn_here, feats), lambda s, i: (s * tiles + i, 0)),
        ],
        out_shape=[
            jax.ShapeDtypeStruct((feats, 4 * qkv_here), F32),
            jax.ShapeDtypeStruct((feats, 4 * hidden_here), F32),
            jax.ShapeDtypeStruct((4 * attn_here, feats), F32),
            jax.ShapeDtypeStruct((4 * hidden_here, feats), F32),
        ],
        compiler_params=pltpu.CompilerParams(vmem_limit_bytes=32 * 1024 * 1024),
    )(first_sum, second_sum, second_sum)


def dealt_layer(
    layer_input,
    lengths,
    deal_table,
    ln1_gain,
    ln1_bias,
    qkv_weight,
    qkv_bias,
    dense_weight,
    dense_bias,
    ln2_gain,
    ln2_bias,
    fc1_weight,
    fc1_bias,
    fc2_weight,
    fc2_bias,
    cotangent,
):
    own_rows, feats = layer_input.shape
    rows = 2 * own_rows
    slab = own_rows // 2
    qkv_cols = qkv_weight.shape[1]
    qkv_here = qkv_cols // 4
    attn_here = dense_weight.shape[0] // 4
    hidden_cols = fc1_weight.shape[1]
    hidden_here = hidden_cols // 4
    first_cols = qkv_here + hidden_here
    second_rows = attn_here + hidden_here

    norms = jnp.stack([ln1_gain, ln1_bias, ln2_gain, ln2_bias] * 2)
    out_bias = (dense_bias + fc2_bias).reshape(1, feats)
    turns = 1.0 / 10000.0 ** (np.arange(0, ROT, 2) / ROT)
    turns = np.concatenate([turns, turns, np.zeros(HD - ROT)])
    turns = np.broadcast_to(turns.astype(np.float32), (8, HD))

    low = lambda *shape: jax.ShapeDtypeStruct(shape, BF16)
    wide = lambda *shape: jax.ShapeDtypeStruct(shape, F32)
    first = low(4, feats, first_cols)
    second = low(4, second_rows, feats)
    item = low(2, slab, feats)
    small_shape = (8, first_cols + feats)
    outputs = [first, second, item, wide(2, slab, feats)]
    scatter = [
        low(4, rows, feats),
        low(2, rows, feats),
        low(2, rows, feats),
        low(2, own_rows, feats),
        low(2, own_rows, feats),
        low(own_rows, feats),
    ]
    buffers = (
        [wide(own_rows, feats), item, wide(rows, 128)]
        + [low(4, 4, slab, feats)] * 2
        + [low(rows, D)] * 2
        + [first, second, low(rows, second_rows), low(rows, first_cols)]
        + [first, second]
        + scatter
        + [item]
        + scatter
        + [item] * 10
    )
    any_space = pl.BlockSpec(memory_space=pl.ANY)
    vmem = pl.BlockSpec(memory_space=pltpu.VMEM)
    smem = pl.BlockSpec(memory_space=pltpu.SMEM)
    copies = 250
    first_units, second_units = first_cols // UNIT, second_rows // UNIT
    results = pl.pallas_call(
        layer_kernel,
        in_specs=[smem] * 2 + [any_space] * 2 + [vmem] * 5 + [any_space] * 4,
        out_specs=[any_space] * 4 + [vmem] + [any_space] * len(buffers),
        out_shape=outputs + [wide(*small_shape)] + buffers,
        scratch_shapes=[
            pltpu.VMEM((4, UNIT + qkv_here, feats), F32),
            pltpu.VMEM((4, 8, feats), F32),
            pltpu.VMEM((first_units, 4, feats, UNIT), BF16),
            pltpu.VMEM((second_units, 4, UNIT, feats), BF16),
            pltpu.VMEM((first_units, 4, feats // 2, UNIT), BF16),
            pltpu.VMEM((second_units, 4, UNIT // 2, feats), BF16),
            pltpu.VMEM((2, 4, feats, UNIT), BF16),
            pltpu.VMEM((2, 4, UNIT, feats), BF16),
            pltpu.VMEM((8, qkv_here), F32),
            pltpu.VMEM((8, first_cols), F32),
            pltpu.VMEM((4, 8, feats), F32),
            pltpu.VMEM((4, 8, feats), F32),
            pltpu.VMEM((4, 8, first_cols), F32),
            pltpu.VMEM((8, feats), F32),
            pltpu.VMEM(small_shape, F32),
            pltpu.VMEM(small_shape, F32),
            pltpu.VMEM(small_shape, F32),
            pltpu.VMEM(small_shape, F32),
            pltpu.VMEM((2, 8, slab), F32),
            pltpu.VMEM((4, 2, 8, slab), F32),
            pltpu.SemaphoreType.DMA((copies,)),
            pltpu.SemaphoreType.DMA((copies,)),
            pltpu.SemaphoreType.DMA((96,)),
        ],
        compiler_params=pltpu.CompilerParams(
            collective_id=0, has_side_effects=True, vmem_limit_bytes=60 * 1024 * 1024
        ),
        cost_estimate=pl.CostEstimate(
            flops=6 * rows * D * (first_cols + second_rows),
            bytes_accessed=200 * 1024 * 1024,
            transcendentals=rows * hidden_here,
        ),
    )(
        lengths,
        deal_table,
        layer_input.reshape(2, slab, feats),
        cotangent.reshape(2, slab, feats),
        norms,
        qkv_bias.reshape(4, 1, qkv_here),
        fc1_bias.reshape(4, 1, hidden_here),
        out_bias,
        turns,
        qkv_weight,
        dense_weight,
        fc1_weight,
        fc2_weight,
    )
    first_sum, second_sum, output, input_grad, small = results[:5]
    qkv_grad, fc1_grad, dense_grad, fc2_grad = widen(first_sum, second_sum, qkv_here, attn_here)
    norm_sums = small[:5, first_cols:]
    return (
        output.reshape(own_rows, feats),
        input_grad.reshape(own_rows, feats),
        norm_sums[0],
        norm_sums[1],
        qkv_grad,
        small[:4, :qkv_here].reshape(qkv_cols),
        dense_grad,
        norm_sums[4],
        norm_sums[2],
        norm_sums[3],
        fc1_grad,
        small[:4, qkv_here:first_cols].reshape(hidden_cols),
        fc2_grad,
        norm_sums[4],
    )


def solution(mesh):
    grid = tuple(mesh.shape[axis] for axis in ("dp", "row", "col"))
    placed = (
        P(("dp", "col"), "row"),
        P(),
        P(),
        P("row"),
        P("row"),
        P("row", "col"),
        P("col"),
        P("col", "row"),
        P("row"),
        P("row"),
        P("row"),
        P("row", "col"),
        P("col"),
        P("col", "row"),
        P("row"),
        P(("dp", "col"), "row"),
    )
    return jax.shard_map(
        dealt_layer if grid == (4, 4, 2) else local,
        mesh=mesh,
        in_specs=placed,
        out_specs=(
            P(("dp", "col"), "row"),
            P(("dp", "col"), "row"),
            P("row"),
            P("row"),
            P("row", "col"),
            P("col"),
            P("col", "row"),
            P("row"),
            P("row"),
            P("row"),
            P("row", "col"),
            P("col"),
            P("col", "row"),
            P("row"),
        ),
        check_vma=False,
    )
```
